32 devices in a mesh: rve: 2 (over x), sub: 16 (over z, y, core).
Axes of the slice: x: 2, y: 2, z: 4, core: 2. Of those that a mesh axis runs over, the one named last changes fastest.
Arguments:
- condensed: float32 [49152, 1536], P(('rve', 'sub')), parts along dimension 0, may hold values from -0.15625 to 0.15625
- eigen_loads: float32 [49152, 128], P(('rve', 'sub')), parts along dimension 0, may hold values from -6 to 6
- coarse_inverse: float32 [1536, 768], P(('rve', 'sub')), parts along dimension 0, may hold values from -0.21875 to 0.21875
- face_rows: int32 [16, 2, 128], P('sub'), may hold values from 0 to 1535, as said below
- primal_rows: int32 [16, 96], P('sub'), may hold values from 0 to 1535, as said below
- primal_slot: int32 [16, 96], P('sub'), may hold values from 0 to 95, each once within a row
Outputs:
- displaced: float32 [49152, 128], P(('rve', 'sub')), parts along dimension 0
- multipliers: float32 [4096, 128], P(('rve', 'sub')), parts along dimension 0
The draws below stay inside these ranges and needn't reach their ends.
There are 2 independent parts, one for each index of `rve`. The reference program is written for one: setup_inputs(seed, part) draws one part's arguments, and reference() takes and returns one part's arrays. A program takes and returns all parts, laid end to end along the dimension named above; an argument that names none is the same for every part. Nothing has to cross between parts.
Inputs may be any that keep to these rules, and one draw needn't show every extreme that they name: `face_rows`: in each subdomain the 128 left-face rows, the 128 right-face rows and the 96 primal rows in primal_rows are all distinct. `primal_rows`: distinct from that subdomain's face rows.
All inputs are finite; a program needn't handle non-finite values.
Results may differ from the reference program's by a relative error of at most 0.0001.
Values sent between devices are 32-bit elements; how exact they have to be, the bound alone decides.
No kernel may reach another device: no remote copies, remote signals or barrier semaphores. Data moves between devices by JAX's collectives and lax.ppermute only.
A program may use at most 64 MiB of HBM per device.

```python
import jax
import jax.numpy as jnp
from jax import lax

B = 1536
PR = 96
IF = 128
COLS = 128
ITERS = 3
PC = 48
SUBS = 16
NC = 768


def layout_rows(key):
    keys = jax.random.split(jax.random.fold_in(key, 11), SUBS)
    return jax.vmap(lambda item: jax.random.permutation(item, B))(keys)


def draw_face_rows(key, part):
    perms = layout_rows(key)
    return perms[:, :2 * IF].reshape(SUBS, 2, IF).astype(jnp.int32)


def draw_primal_rows(key, part):
    perms = layout_rows(key)
    return perms[:, 2 * IF:2 * IF + PR].astype(jnp.int32)


def level_of(own_key, extent, cuts, smallest, largest):
    factor_of = 1.0
    for position, parts in cuts:
        draws = jax.random.uniform(jax.random.fold_in(jax.random.fold_in(own_key, 6), position), (parts,), jnp.float32, smallest / len(cuts), largest / len(cuts))
        factor_of = factor_of * jnp.repeat(jnp.exp(draws), extent[position] // parts).reshape((-1,) + (1,) * (len(extent) - 1 - position))
    return factor_of


def normal_values(own_key, dims, spread, bound, cuts=(), held_as=jnp.bfloat16):
    level = level_of(own_key, dims, cuts, -0.22, 0.18) if cuts else 1.0
    array = jax.random.normal(own_key, dims, jnp.float32) * spread * level
    return jnp.minimum(jnp.maximum(array, -bound), bound).astype(held_as)


def setup_inputs(seed: int = 0, part: int = 0) -> dict:
    key_list = jax.random.split(jax.random.key(seed), 7)
    part_splits = jax.random.split(jax.random.fold_in(key_list[6], part), 7)
    return {
        "condensed": normal_values(part_splits[0], (SUBS * B, B), B ** -0.5, 0.15625, ((0, 16),), jnp.float32),
        "eigen_loads": normal_values(part_splits[1], (SUBS * B, COLS), 1.0, 6.0, ((0, 16),), jnp.float32),
        "coarse_inverse": normal_values(part_splits[2], (NC, NC), NC ** -0.5, 0.21875, ((0, 16),), jnp.float32),
        "face_rows": draw_face_rows(jax.random.fold_in(key_list[6], 71), part),
        "primal_rows": draw_primal_rows(jax.random.fold_in(key_list[6], 71), part),
        "primal_slot": jax.vmap(lambda own: jax.random.permutation(own, PR))(jax.random.split(key_list[5], SUBS)).reshape((SUBS, PR)).astype(jnp.int32),
    }


DAMPING = 0.5


def add_faces(loads, right_rows, left_rows, right_term, left_term):
    return loads.at[right_rows].add(-right_term).at[left_rows].add(left_term)


def place_slots(values, slots):
    return jnp.zeros((PR, values.shape[1]), jnp.float32).at[slots].set(values)


def reference(condensed, eigen_loads, coarse_inverse, face_rows, primal_rows, primal_slot):
    blocks = condensed.reshape(SUBS, B, B)
    loads_all = eigen_loads.reshape(SUBS, B, COLS)
    left_rows = face_rows[:, 0, :]
    right_rows = face_rows[:, 1, :]
    prolong = jnp.take_along_axis(blocks, primal_rows[:, None, :], 2)
    multipliers = jnp.zeros((SUBS, IF, COLS), jnp.float32)
    displaced = loads_all
    for step in range(ITERS):
        previous = jnp.roll(multipliers, 1, axis=0)
        loads = jax.vmap(add_faces)(loads_all, right_rows, left_rows, multipliers, previous)
        displaced = jnp.einsum("sij,sjc->sic", blocks, loads, precision=lax.Precision.HIGHEST)
        picked = jnp.take_along_axis(displaced, primal_rows[:, :, None], 1)
        slotted = jax.vmap(place_slots)(picked, primal_slot)
        assembled = slotted[:, :PC] + jnp.roll(slotted[:, PC:], 1, axis=0)
        coarse_sol = jnp.dot(coarse_inverse, assembled.reshape(NC, COLS), precision=lax.Precision.HIGHEST, preferred_element_type=jnp.float32).reshape(SUBS, PC, COLS)
        paired = jnp.concatenate([coarse_sol, jnp.roll(coarse_sol, -1, axis=0)], axis=1)
        gathered = jnp.take_along_axis(paired, primal_slot[:, :, None], 1)
        displaced = displaced - jnp.einsum("sij,sjc->sic", prolong, gathered, precision=lax.Precision.HIGHEST)
        right_vals = jnp.take_along_axis(displaced, right_rows[:, :, None], 1)
        left_vals = jnp.take_along_axis(displaced, left_rows[:, :, None], 1)
        multipliers = multipliers + DAMPING * (right_vals - jnp.roll(left_vals, -1, axis=0))
    return displaced.reshape(SUBS * B, COLS), multipliers.reshape(SUBS * IF, COLS)
```

```python
import functools

import jax
import jax.numpy as jnp
from jax import lax
from jax.experimental import pallas as pl
from jax.experimental.pallas import tpu as pltpu
from jax.sharding import PartitionSpec as P

ITERS = 3
DAMPING = 0.5
GROUP = 4
LANES = 128
BF16 = jnp.bfloat16
F32 = jnp.float32


def call(kernel, out_shapes, args, in_specs=None, grid=None, out_specs=None, scratch=(), flops=0, size=0):
    vmem = pl.BlockSpec(memory_space=pltpu.VMEM)
    if in_specs is None:
        in_specs = [pl.BlockSpec(memory_space=pltpu.SMEM)] + [vmem] * (len(args) - 1)
    if out_specs is None:
        out_specs = [vmem] * len(out_shapes)
    options = {} if grid is None else {"grid": grid}
    return pl.pallas_call(
        kernel,
        out_shape=[jax.ShapeDtypeStruct(s, F32) for s in out_shapes],
        in_specs=in_specs,
        out_specs=out_specs,
        scratch_shapes=list(scratch),
        compiler_params=pltpu.CompilerParams(vmem_limit_bytes=48 * 1024 * 1024),
        cost_estimate=pl.CostEstimate(flops=flops, bytes_accessed=size, transcendentals=0),
        **options,
    )(*args)


def halves(x):
    high = x.astype(BF16)
    return high, (x - high.astype(F32)).astype(BF16)


def dot(a, b):
    return jnp.dot(a, b, preferred_element_type=F32)


def product(a, b):
    ah, al = halves(a)
    bh, bl = halves(b)
    n = b.shape[1]
    both = dot(ah, jnp.concatenate([bh, bl], axis=1))
    return both[:, :n] + both[:, n:] + dot(al, bh)


def lane_block(rows):
    return lax.broadcasted_iota(jnp.int32, (rows, LANES), 1) // (LANES // GROUP)


def turned(x, blocks):
    width = LANES // GROUP
    if isinstance(blocks, int):
        shift = (blocks % GROUP) * width
        return x if shift == 0 else pltpu.roll(x, shift, 1)
    return pltpu.roll(x, lax.rem(blocks + 2 * GROUP, GROUP) * width, 1)


def cut(x, member, out_refs):
    rows = x.shape[0] // GROUP
    block = lane_block(rows)
    parts = [x[q * rows:(q + 1) * rows] for q in range(GROUP)]
    for k, out in enumerate(out_refs):
        to = member ^ k
        packed = jnp.zeros((rows, LANES), F32)
        for q in range(GROUP):
            packed = jnp.where(block == q, turned(parts[q], q - to), packed)
        out[...] = packed


def joined(pieces, member):
    rows = pieces[0].shape[0]
    block = lane_block(rows)
    out = []
    for q in range(GROUP):
        part = jnp.zeros((rows, LANES), F32)
        for k, piece in enumerate(pieces):
            came = member ^ k
            part = jnp.where(block == came, turned(piece, came - q), part)
        out.append(part)
    return jnp.concatenate(out, axis=0)


def packed(x, chunk):
    first = lane_block(chunk) == 0
    out = None
    for q in range(x.shape[0] // chunk):
        part = turned(jnp.where(first, x[q * chunk:(q + 1) * chunk], 0.0), q)
        out = part if out is None else out + part
    return out


def unpacked(x, count):
    return jnp.concatenate([turned(x, -q) for q in range(count)], axis=0)


def chunk_of(owned):
    return -(-owned // (GROUP * 8)) * 8


def payload(v, width, owned, out):
    chunk = chunk_of(owned)
    first = lane_block(owned) == 0
    coarse = v[2 * width:]
    below = turned(coarse[owned:], 1)
    out[0:owned] = coarse[:owned] + jnp.where(first, 0.0, below)
    out[owned:owned + chunk] = packed(below, chunk)
    small = width // GROUP
    at = owned + chunk
    out[at:at + small] = packed(v[:width], small)
    out[at + small:at + 2 * small] = packed(turned(v[width:2 * width], 1), small)


def selector(rows_ref, et_ref):
    sets, width = rows_ref.shape
    for group in range(sets):
        row = rows_ref[group:group + 1, :].astype(F32)
        column = jnp.broadcast_to(row, (width, width)).T
        for c in range(et_ref.shape[1] // width):
            lane = lax.broadcasted_iota(jnp.int32, (width, width), 1) + c * width
            hit = column == lane.astype(F32)
            et_ref[group * width:(group + 1) * width, c * width:(c + 1) * width] = jnp.where(hit, 1.0, 0.0).astype(BF16)


def first_kernel(kept, pos, rows_ref, k_ref, f_ref, u_ref, *rest):
    pieces, (et, loads) = rest[:GROUP], rest[GROUP:]
    step = pl.program_id(0)
    rows, columns = k_ref.shape[0], f_ref.shape[1]

    @pl.when(step == 0)
    def _():
        selector(rows_ref, et)
        high, low = halves(f_ref[...])
        loads[:, :columns] = high
        loads[:, columns:] = low

    high, low = halves(k_ref[...])
    both = dot(high, loads[...])
    u = both[:, :columns] + both[:, columns:] + dot(low, loads[:, :columns])
    u_ref[pl.ds(pl.multiple_of(step * rows, rows), rows), :] = u

    @pl.when(step == pl.num_programs(0) - 1)
    def _():
        high, low = halves(u_ref[...])
        v = dot(et[...], jnp.concatenate([high, low], axis=1))
        v = v[:, :columns] + v[:, columns:]
        cut(v[:kept], pos[0], pieces)


def columns_kernel(rows_ref, k_ref, ks_ref, a_ref, et):
    step = pl.program_id(0)
    rows = k_ref.shape[0]

    @pl.when(step == 0)
    def _():
        selector(rows_ref, et)

    high, low = halves(k_ref[...])
    dims = (((1,), (1,)), ((), ()))
    picked = lax.dot_general(high, et[...], dims, preferred_element_type=F32)
    picked = picked + lax.dot_general(low, et[...], dims, preferred_element_type=F32)
    ks_ref[pl.ds(pl.multiple_of(step * rows, rows), rows), :] = picked

    @pl.when(step == pl.num_programs(0) - 1)
    def _():
        high, low = halves(ks_ref[...])
        a_ref[...] = (dot(et[...], high) + dot(et[...], low))[:a_ref.shape[0]]


def coarse_kernel(pos, c0, c1, c2, c3, plane, up, down):
    owned = c0.shape[0]
    for k, piece in enumerate((c0, c1, c2, c3)):
        member = pos[0] ^ k
        plane[pl.ds(pl.multiple_of(member * owned, 8), owned), :] = piece[...]
    up[...] = plane[(GROUP - 1) * owned:, :]
    down[...] = plane[:2 * owned, :]


def edges_kernel(width, pos, a0, a1, a2, a3, up, down):
    for k, piece in enumerate((a0, a1, a2, a3)):
        member = pos[0] ^ k

        @pl.when(member == GROUP - 1)
        def _():
            up[...] = piece[width:2 * width, 2 * width:]

        @pl.when(member == 0)
        def _():
            down[...] = piece[:width, 2 * width:]


def start_kernel(width, owned, pos, p0, p1, p2, p3, v_ref, pay_ref):
    v = joined([p0[...], p1[...], p2[...], p3[...]], pos[0])
    v_ref[...] = v
    payload(v, width, owned, pay_ref)


def turn_kernel(width, owned, kind, pos, pays, above, plane, below, a0, a1, a2, a3, edge_up, edge_down, v0, *rest):
    if kind == "first":
        now = v0
    else:
        now, left_ref, right_ref = rest[:3]
        rest = rest[3:]
    outs, (stack,) = rest[:-1], rest[-1:]
    member, group = pos[0], pos[1]
    groups = pays.shape[0]
    chunk = chunk_of(owned)
    small = width // GROUP
    at = owned + chunk
    blocks = (a0, a1, a2, a3)
    first = lane_block(owned) == 0

    for h in range(groups):
        extra = unpacked(pays[(h - 1) % groups, owned:at, :], -(-owned // chunk))[:owned]
        whole = pays[h, :owned, :] + jnp.where(first, extra, 0.0)
        for i in range(GROUP):
            high, low = halves(turned(whole, -i))
            place = slice((h * GROUP + i) * owned, (h * GROUP + i + 1) * owned)
            stack[place, :LANES] = high
            stack[place, LANES:] = low

    def solved(c_ref):
        high, low = halves(c_ref[...])
        both = dot(high, stack[...])
        return both[:, :LANES] + both[:, LANES:] + dot(low, stack[:, :LANES])

    w = jnp.concatenate([solved(above), solved(plane), solved(below)], axis=0)
    pair = lane_block(2 * owned)
    q = jnp.zeros((2 * owned, LANES), F32)
    for i in range(GROUP):
        q = jnp.where(pair == i, turned(w[(i + 1) * owned:(i + 3) * owned], i), q)
    filler = jnp.zeros((width - 2 * owned, LANES), F32)

    def applied(cols, rows, x):
        block = lane_block(x.shape[0])
        total = None
        for k in range(GROUP):
            mine = jnp.where(block == (member ^ k), x, 0.0)
            part = product(blocks[k][rows, cols], mine)
            total = part if total is None else total + part
        return total

    padded = jnp.concatenate([q, filler], axis=0)
    faces = now[:2 * width, :] - applied(slice(2 * width, 3 * width), slice(0, 2 * width), padded)
    left, right = faces[:width], faces[width:]
    before = jnp.concatenate([w[:2 * owned], filler], axis=0)
    after = jnp.concatenate([w[(GROUP + 1) * owned:], filler], axis=0)
    previous = lax.rem(group + groups - 1, groups)
    following = lax.rem(group + 1, groups)
    right_before = unpacked(pays[previous, at + small:at + 2 * small, :], GROUP) - product(edge_up[...], before)
    left_after = unpacked(pays[following, at:at + small, :], GROUP) - product(edge_down[...], after)
    block = lane_block(width)
    beyond = jnp.where(block == GROUP - 1, turned(left_after, GROUP - 1), turned(left, -1))
    behind = jnp.where(block == 0, right_before, turned(right, 1))
    lam_right = DAMPING * (right - beyond)
    lam_left = DAMPING * (behind - left)
    if kind != "first":
        lam_right = lam_right + right_ref[...]
        lam_left = lam_left + left_ref[...]
    if kind == "last":
        cut(jnp.concatenate([q, lam_right], axis=0), member, outs)
        return
    v_ref, left_out, right_out, pay_ref = outs[:4]
    left_out[...] = lam_left
    right_out[...] = lam_right
    v = v0[...] + applied(slice(0, 2 * width), slice(None), jnp.concatenate([lam_left, -lam_right], axis=0))
    v_ref[...] = v
    payload(v, width, owned, pay_ref)
    if kind == "middle":
        cut(jnp.concatenate([lam_left, lam_right], axis=0), member, outs[4:])


def spread_kernel(width, pos, p0, p1, p2, p3, u_ref, ks_ref, out_ref):
    lam = joined([p0[...], p1[...], p2[...], p3[...]], pos[0])
    rows = lax.broadcasted_iota(jnp.int32, lam.shape, 0)
    out_ref[...] = u_ref[...] + product(ks_ref[:, :2 * width], jnp.where(rows < width, lam, -lam))


def final_kernel(width, owned, pos, p0, p1, p2, p3, u_ref, ks_ref, out_ref, lam_ref):
    x = joined([p0[...], p1[...], p2[...], p3[...]], pos[0])
    lam_ref[...] = x[2 * owned:]
    filler = jnp.zeros((width - 2 * owned, LANES), F32)
    q = jnp.concatenate([x[:2 * owned], filler], axis=0)
    out_ref[...] = u_ref[...] - product(ks_ref[:, 2 * width:], q)


def local(condensed, eigen_loads, coarse_inverse, face_rows, primal_rows, primal_slot):
    order, columns = eigen_loads.shape
    owned, coarse = coarse_inverse.shape
    width = face_rows.shape[2]
    kept = 2 * width + 2 * owned
    count = lax.axis_size("sub")
    groups = count // GROUP
    me = lax.axis_index("sub")
    pos = jnp.stack([me % GROUP, me // GROUP]).astype(jnp.int32)

    def mate(x, k):
        return lax.ppermute(x, "sub", [(s, s ^ k) for s in range(count)])

    def planes(x, by):
        return lax.ppermute(x, "sub", [(s, (s + by * GROUP) % count) for s in range(count)])

    def along(x):
        lines = [[h * GROUP + m for h in range(groups)] for m in range(GROUP)]
        return lax.all_gather(x, "sub", axis_index_groups=lines)

    def traded(pieces):
        return [pieces[0]] + [mate(pieces[k], k) for k in range(1, GROUP)]

    def plane_all(x):
        second = mate(x, 2)
        return [x, mate(x, 1), second, mate(second, 1)]

    slots = lax.broadcasted_iota(jnp.int32, (2 * owned, width), 1)
    by_slot = jnp.max(jnp.where(primal_slot[0][:, None] == slots, primal_rows[0][:, None], -1), axis=0)
    rows = jnp.concatenate([face_rows[0], by_slot[None]], axis=0)

    c_blocks = plane_all(coarse_inverse)

    block = 256 if order % 256 == 0 else order
    k_spec = pl.BlockSpec((block, order), lambda i: (i, 0))
    smem = pl.BlockSpec(memory_space=pltpu.SMEM)

    def whole(*shape):
        return pl.BlockSpec(shape, lambda i: (0,) * len(shape))

    small = kept // GROUP
    u0, *pieces = call(
        functools.partial(first_kernel, kept),
        [(order, columns)] + [(small, LANES)] * GROUP,
        (pos, rows, condensed, eigen_loads),
        in_specs=[smem, whole(3, width), k_spec, whole(order, columns)],
        grid=(order // block,),
        out_specs=[whole(order, columns)] + [whole(small, LANES)] * GROUP,
        scratch=[pltpu.VMEM((3 * width, order), BF16), pltpu.VMEM((order, 2 * columns), BF16)],
        flops=6 * order * order * columns,
        size=4 * order * order,
    )
    pieces = traded(pieces)
    ks, a_own = call(
        columns_kernel,
        [(order, 3 * width), (kept, 3 * width)],
        (rows, condensed),
        in_specs=[whole(3, width), k_spec],
        grid=(order // block,),
        out_specs=[whole(order, 3 * width), whole(kept, 3 * width)],
        scratch=[pltpu.VMEM((3 * width, order), BF16)],
        flops=4 * order * order * 3 * width,
        size=4 * order * order,
    )
    plane, c_up, c_down = call(
        coarse_kernel,
        [(GROUP * owned, coarse), (owned, coarse), (2 * owned, coarse)],
        (pos, *c_blocks),
    )
    above, below = planes(c_up, 1), planes(c_down, -1)
    chunk = chunk_of(owned)
    pay_rows = owned + chunk + 2 * (width // GROUP)
    v0, pay = call(
        functools.partial(start_kernel, width, owned),
        [(kept, LANES), (pay_rows, LANES)],
        (pos, *pieces),
    )
    a_blocks = plane_all(a_own)
    a_up, a_down = call(functools.partial(edges_kernel, width), [(width, width)] * 2, (pos, *a_blocks))
    edge_up, edge_down = planes(a_up, 1), planes(a_down, -1)

    fixed = (above, plane, below, *a_blocks, edge_up, edge_down, v0)
    stack = [pltpu.VMEM((coarse, 2 * LANES), BF16)]
    state = ()
    for step in range(ITERS):
        kind = "first" if step == 0 else "last" if step == ITERS - 1 else "middle"
        shapes = [(kept, LANES), (width, LANES), (width, LANES), (pay_rows, LANES)]
        if kind == "middle":
            shapes = shapes + [(2 * width // GROUP, LANES)] * GROUP
        if kind == "last":
            shapes = [((2 * owned + width) // GROUP, LANES)] * GROUP
        outs = call(
            functools.partial(turn_kernel, width, owned, kind),
            shapes,
            (pos, along(pay), *fixed, *state),
            scratch=stack,
        )
        if kind != "last":
            state, pay = outs[:3], outs[3]
        if kind == "middle":
            lam_pieces = traded(outs[4:])
            (spread,) = call(
                functools.partial(spread_kernel, width),
                [(order, columns)],
                (pos, *lam_pieces, u0, ks),
                flops=6 * order * 2 * width * columns,
                size=4 * order * 5 * width,
            )
    displaced, multipliers = call(
        functools.partial(final_kernel, width, owned),
        [(order, columns), (width, columns)],
        (pos, *traded(outs), spread, ks),
    )
    return displaced, multipliers


def solution(mesh):
    placed = (
        P(("rve", "sub"), None),
        P(("rve", "sub"), None),
        P(("rve", "sub"), None),
        P("sub", None, None),
        P("sub", None),
        P("sub", None),
    )
    return jax.shard_map(
        local,
        mesh=mesh,
        in_specs=placed,
        out_specs=(P(("rve", "sub"), None), P(("rve", "sub"), None)),
        check_vma=False,
    )
```

```python
import functools

import jax
import jax.numpy as jnp
from jax import lax
from jax.experimental import pallas as pl
from jax.experimental.pallas import tpu as pltpu
from jax.sharding import PartitionSpec as P

ITERS = 3
DAMPING = 0.5
GROUP = 4
LANES = 128
BF16 = jnp.bfloat16
F32 = jnp.float32


def call(kernel, outs, args, smem=1, hbm=(), scratch=(), vmem=24):
    in_specs = [
        pl.BlockSpec(memory_space=pltpu.SMEM if i < smem else pltpu.HBM if i in hbm else pltpu.VMEM)
        for i in range(len(args))
    ]
    shapes = [o if isinstance(o[0], tuple) else (o, F32) for o in outs]
    return pl.pallas_call(
        kernel,
        out_shape=[jax.ShapeDtypeStruct(s, d) for s, d in shapes],
        in_specs=in_specs,
        out_specs=[pl.BlockSpec(memory_space=pltpu.VMEM)] * len(shapes),
        scratch_shapes=list(scratch),
        compiler_params=pltpu.CompilerParams(vmem_limit_bytes=vmem * 1024 * 1024),
    )(*args)


def halves(x):
    high = x.astype(BF16)
    return high, (x - high.astype(F32)).astype(BF16)


def dot(a, b):
    return jnp.dot(a, b, preferred_element_type=F32)


def product(a, b):
    ah, al = halves(a)
    bh, bl = halves(b)
    n = b.shape[1]
    both = dot(ah, jnp.concatenate([bh, bl], axis=1))
    return both[:, :n] + both[:, n:] + dot(al, bh)


def lane_block(rows):
    return lax.broadcasted_iota(jnp.int32, (rows, LANES), 1) // (LANES // GROUP)


def turned(x, blocks):
    width = LANES // GROUP
    if isinstance(blocks, int):
        shift = (blocks % GROUP) * width
        return x if shift == 0 else pltpu.roll(x, shift, 1)
    return pltpu.roll(x, lax.rem(blocks + 2 * GROUP, GROUP) * width, 1)


def cut(x, member, out_refs):
    rows = x.shape[0] // GROUP
    block = lane_block(rows)
    parts = [x[q * rows:(q + 1) * rows] for q in range(GROUP)]
    for k, out in enumerate(out_refs):
        to = member ^ k
        packed = jnp.zeros((rows, LANES), F32)
        for q in range(GROUP):
            packed = jnp.where(block == q, turned(parts[q], q - to), packed)
        out[...] = packed


def joined(pieces, member):
    rows = pieces[0].shape[0]
    block = lane_block(rows)
    out = []
    for q in range(GROUP):
        part = jnp.zeros((rows, LANES), F32)
        for k, piece in enumerate(pieces):
            came = member ^ k
            part = jnp.where(block == came, turned(piece, came - q), part)
        out.append(part)
    return jnp.concatenate(out, axis=0)


def packed(x, chunk):
    first = lane_block(chunk) == 0
    out = None
    for q in range(x.shape[0] // chunk):
        part = turned(jnp.where(first, x[q * chunk:(q + 1) * chunk], 0.0), q)
        out = part if out is None else out + part
    return out


def unpacked(x, count):
    return jnp.concatenate([turned(x, -q) for q in range(count)], axis=0)


def chunk_of(owned):
    return -(-owned // (GROUP * 8)) * 8


def stacked(x):
    return jnp.concatenate(halves(x), axis=0)


def beside(x):
    return jnp.concatenate(halves(x), axis=1)


def combined(p, n):
    m = p.shape[0] // 2
    return p[:m, :n] + p[:m, n:] + p[m:, :n]


def payload(c, out):
    owned = c.shape[0] // 2
    below = turned(c[owned:], 1)
    out[:owned] = c[:owned] + jnp.where(lane_block(owned) == 0, 0.0, below)
    out[owned:] = packed(below, chunk_of(owned))


def fetch(source, count, rows, target, places, sem):
    def one(j, carry):
        pltpu.make_async_copy(source.at[pl.ds(rows(j), 1)], target.at[pl.ds(places(j), 1)], sem).start()
        return carry

    lax.fori_loop(0, count, one, 0, unroll=8)


def rows_kernel(pos, face, prim, slot, k_ref, f_ref, facev, primv, slotv, *rest):
    pieces, (ks, near, edge, right_side, sem) = rest[:GROUP], rest[GROUP:]
    width, count, order, columns = face.shape[1], prim.shape[1], ks.shape[1], f_ref.shape[1]
    side = 2 * width
    fetch(k_ref, prim.shape[1], lambda j: prim[0, j], ks, lambda j: side + slot[0, j], sem)
    fetch(k_ref, side, lambda j: face[j // width, j % width], ks, lambda j: j, sem)
    def indicator(row):
        place = lax.broadcasted_iota(jnp.int32, (order, row.shape[1]), 0).astype(F32)
        return jnp.where(place == row, 1.0, 0.0).astype(BF16)

    slots = jnp.broadcast_to(slotv[...].astype(F32), (count, count)).T
    prims = jnp.broadcast_to(primv[...].astype(F32), (count, count)).T
    wanted = lax.broadcasted_iota(jnp.int32, (count, count), 1).astype(F32)
    by_slot = jnp.sum(jnp.where(slots == wanted, prims, 0.0), axis=0, keepdims=True)
    right_side[:, :width] = indicator(facev[0:1].astype(F32))
    right_side[:, width:side] = indicator(facev[1:2].astype(F32))
    right_side[:, side:side + count] = indicator(by_slot)
    right_side[:, side + count:side + width] = jnp.zeros((order, width - count), BF16)
    right_side[:, side + width:] = beside(f_ref[...])
    pltpu.make_async_copy(k_ref.at[pl.ds(0, ks.shape[0])], ks, sem).wait()
    cut(combined(dot(stacked(ks[...]), right_side[:, side + width:]), columns), pos[0], pieces)

    def picked(rows, columns):
        high, low = halves(ks[rows])
        return dot(high, right_side[:, columns]) + dot(low, right_side[:, columns])

    cross = picked(slice(0, side), slice(side, side + width))
    near[:side] = cross
    edge[...] = jnp.where(pos[0] == GROUP - 1, cross[width:], cross[:width])
    own = picked(slice(side, side + count), slice(0, side))
    near[side:side + count] = own[:, :width]
    near[side + count:] = own[:, width:]


def far_kernel(pos, ks, right_side, far):
    side = far.shape[1]
    high, low = halves(ks[:side])
    far[...] = dot(high, right_side[:, :side]) + dot(low, right_side[:, :side])


def sweep_kernel(first, pos, right_side, k_ref, u_ref, ks_ref):
    rows, columns = u_ref.shape
    at = right_side.shape[1] - 2 * columns
    high, low = halves(k_ref[first:first + rows])
    both = dot(high, right_side[...])
    part = dot(low, right_side[:, :at + columns])
    u_ref[...] = both[:, at:at + columns] + both[:, at + columns:] + part[:, at:]
    ks_ref[...] = both[:, :at] + part[:, :at]


GOT = (-1, None, 5, 4)
GOT_NEXT = (5, 4, -1, None)


def solver_kernel(pos, mine, next_mine, got, next_got, theirs, out):
    owned = mine.shape[0]
    half = out.shape[0] // 2
    other = [theirs[i * owned:(i + 1) * owned] for i in range(4)]
    for m in range(GROUP):

        @pl.when(pos[0] == m)
        def _():
            p = m ^ 1
            held = [(m, mine[...]), (m ^ 2, next_mine[...]), (GOT[m], got[...]), (GOT_NEXT[m], next_got[...])]
            held += list(zip((p, p ^ 2, GOT[p], GOT_NEXT[p]), other))
            for block, values in held:
                if block is not None:
                    at = (block + 1) * owned
                    high, low = halves(values)
                    out[at:at + owned] = high
                    out[half + at:half + at + owned] = low


def blocks_kernel(width, pos, n0, n2, came, came_next, theirs, cross, own, edge_up, edge_down):
    side, size = 2 * width, n0.shape[0]
    count = (size - side) // 2
    other = [theirs[:size], theirs[size:2 * size], theirs[2 * size:2 * size + width], theirs[2 * size + width:]]
    for k, values in enumerate((n0[...], other[0], n2[...], other[1])):
        cross[:, k * width:(k + 1) * width] = stacked(values[:side])
        own[:, k * side:k * side + width] = stacked(values[side:side + count])
        own[:, k * side + width:(k + 1) * side] = stacked(values[side + count:])
    for m in range(GROUP):

        @pl.when(pos[0] == m)
        def _():
            held = {GOT[m]: came, GOT_NEXT[m]: came_next}
            for block, values in zip((GOT[m ^ 1], GOT_NEXT[m ^ 1]), other[2:]):
                held.setdefault(block, values)
            edge_up[...] = stacked(held[-1][...])
            edge_down[...] = stacked(held[4][...])


def spans_kernel(pos, n0, n1, n2, n3, out):
    side = n0.shape[1]
    for k, ref in enumerate((n0, n1, n2, n3)):
        out[:, k * side:(k + 1) * side] = stacked(ref[...])


def halos(v, up, down):
    width = v.shape[0] // 2
    down[...] = packed(v[:width], width // GROUP)
    up[...] = packed(turned(v[width:], 1), width // GROUP)


def start_kernel(pos, p0, p1, p2, p3, c_ref, v_ref, pay_ref, pay_up, pay_down):
    v = joined([p0[...], p1[...], p2[...], p3[...]], pos[0])
    side = v_ref.shape[0]
    v_ref[...] = v[:side]
    c_ref[...] = v[side:]
    payload(v[side:], pay_ref)
    size = pay_ref.shape[0]
    pay_up[:size] = pay_ref[...]
    pay_down[:size] = pay_ref[...]
    halos(v[:side], pay_up.at[size:], pay_down.at[size:])


def shared(x, member):
    block = lane_block(x.shape[0])
    high, low = halves(x)
    high, low = high.astype(F32), low.astype(F32)
    out = []
    for k in range(GROUP):
        mine = block == (member ^ k)
        pair = [jnp.where(mine, half, 0.0).astype(BF16) for half in (high, low)]
        out.append(jnp.concatenate(pair, axis=1))
    return jnp.concatenate(out, axis=0)


def again_kernel(pos, far, v0, left, right, v_ref, up, down):
    lam = jnp.concatenate([left[...], -right[...]], axis=0)
    v = v0[...] + combined(dot(far[...], shared(lam, pos[0])), LANES)
    v_ref[...] = v
    halos(v, up, down)


def turn_kernel(kind, groups, pos, *refs):
    pays, refs = refs[:groups], refs[groups:]
    solver, cross, own, edge_up, edge_down, c0, faces_ref = refs[:7]
    refs = refs[7:]
    size = pays[0].shape[0]
    if kind == "first":
        halo_up, halo_down = pays[1].at[size:], pays[groups - 1].at[size:]
    else:
        (halo_up, halo_down), refs = refs[:2], refs[2:]
    if kind != "first":
        left_ref, right_ref = refs[:2]
        refs = refs[2:]
    outs, stack = refs[:-1], refs[-1]
    member, group = pos[0], pos[1]
    owned, width = c0.shape[0] // 2, faces_ref.shape[0] // 2
    first = lane_block(owned) == 0

    for k in range(groups):
        h = lax.rem(group - k + groups, groups)
        extra = unpacked(pays[(k + 1) % groups][owned:size, :], -(-owned // chunk_of(owned)))[:owned]
        whole = pays[k][:owned, :] + jnp.where(first, extra, 0.0)
        for i in range(GROUP):
            place = pl.multiple_of((h * GROUP + i) * owned, 16)
            stack[pl.ds(place, owned), :] = beside(turned(whole, -i))

    w = combined(dot(solver[...], stack[...]), LANES)
    pair = lane_block(2 * owned)
    q = jnp.zeros((2 * owned, LANES), F32)
    for i in range(GROUP):
        q = jnp.where(pair == i, turned(w[(i + 1) * owned:(i + 3) * owned], i), q)
    filler = jnp.zeros((width - 2 * owned, LANES), F32)

    def padded(x):
        return jnp.concatenate([x, filler], axis=0)

    faces = faces_ref[...] - combined(dot(cross[...], shared(padded(q), member)), LANES)
    left, right = faces[:width], faces[width:]
    before, after = beside(padded(w[:2 * owned])), beside(padded(w[(GROUP + 1) * owned:]))
    right_before = unpacked(halo_up[...], GROUP) - combined(dot(edge_up[...], before), LANES)
    left_after = unpacked(halo_down[...], GROUP) - combined(dot(edge_down[...], after), LANES)
    block = lane_block(width)
    beyond = jnp.where(block == GROUP - 1, turned(left_after, GROUP - 1), turned(left, -1))
    behind = jnp.where(block == 0, right_before, turned(right, 1))
    lam_right = DAMPING * (right - beyond)
    lam_left = DAMPING * (behind - left)
    if kind != "first":
        lam_right = lam_right + right_ref[...]
        lam_left = lam_left + left_ref[...]
    if kind == "last":
        cut(jnp.concatenate([q, lam_right], axis=0), member, outs)
        return
    left_out, right_out, pay_ref = outs[:3]
    left_out[...] = lam_left
    right_out[...] = lam_right
    lam = jnp.concatenate([lam_left, -lam_right], axis=0)
    payload(c0[...] + combined(dot(own[...], shared(lam, member)), LANES), pay_ref)
    if kind == "middle":
        cut(jnp.concatenate([lam_left, lam_right], axis=0), member, outs[3:])


def spread_kernel(parts, pos, p0, p1, p2, p3, *refs):
    lam = joined([p0[...], p1[...], p2[...], p3[...]], pos[0])
    side = lam.shape[0]
    rows = lax.broadcasted_iota(jnp.int32, lam.shape, 0)
    lam = beside(jnp.where(rows < side // 2, lam, -lam))
    us, kss, out = refs[:parts], refs[parts:2 * parts], refs[2 * parts]
    at = 0
    for u, ks in zip(us, kss):
        out[at:at + u.shape[0]] = u[...] + combined(dot(stacked(ks[:, :side]), lam), LANES)
        at += u.shape[0]


def final_kernel(parts, owned, pos, p0, p1, p2, p3, u_ref, *refs):
    x = joined([p0[...], p1[...], p2[...], p3[...]], pos[0])
    kss, (out, lam_ref) = refs[:parts], refs[parts:]
    lam_ref[...] = x[2 * owned:]
    width = lam_ref.shape[0]
    q = beside(jnp.concatenate([x[:2 * owned], jnp.zeros((width - 2 * owned, LANES), F32)], axis=0))
    at = 0
    for ks in kss:
        rows = slice(at, at + ks.shape[0])
        out[rows] = u_ref[rows] - combined(dot(stacked(ks[:, 2 * width:]), q), LANES)
        at += ks.shape[0]


def local(condensed, eigen_loads, coarse_inverse, face_rows, primal_rows, primal_slot):
    order, columns = eigen_loads.shape
    owned, coarse = coarse_inverse.shape
    width = face_rows.shape[2]
    side, count = 2 * width, 2 * owned
    kept = side + count
    total = lax.axis_size("sub")
    groups = total // GROUP
    me = lax.axis_index("sub")
    pos = jnp.stack([me % GROUP, me // GROUP]).astype(jnp.int32)
    faces = face_rows[0]

    def mate(x, k):
        return lax.ppermute(x, "sub", [(s, s ^ k) for s in range(total)])

    def planes(x, by):
        return lax.ppermute(x, "sub", [(s, (s + by * GROUP) % total) for s in range(total)])

    def traded(pieces):
        return [pieces[0]] + [mate(pieces[k], k) for k in range(1, GROUP)]

    def after(x, other):
        return lax.optimization_barrier((x, other))[0]

    def crossing(pairs):
        return [(g * GROUP + a, (g * GROUP + b) % total) for g in range(groups) for a, b in pairs]

    ends = crossing([(GROUP - 1, GROUP), (0, -1), (1, -2)])
    ends_next = crossing([(GROUP - 1, GROUP + 2), (0, -3), (1, -4)])
    got = lax.ppermute(coarse_inverse, "sub", ends)
    got_next = lax.ppermute(coarse_inverse, "sub", ends_next)
    c_next = mate(coarse_inverse, 2)

    *pieces, ks, near, edge, right_side = call(
        rows_kernel,
        [(kept // GROUP, LANES)] * GROUP
        + [(kept, order), (side + 2 * count, width), (width, width), ((order, side + width + 2 * columns), BF16)],
        (pos, faces, primal_rows, primal_slot, condensed, eigen_loads, faces, primal_rows, primal_slot),
        smem=4,
        hbm=(4,),
        scratch=[pltpu.SemaphoreType.DMA],
        vmem=52,
    )
    parts = 4 if order % 64 == 0 else 1
    block = order // parts

    def swept(part, right_side):
        return call(
            functools.partial(sweep_kernel, part * block),
            [(block, columns), (block, side + width)],
            (pos, right_side, condensed),
        )

    *pieces, got, got_next, c_next = lax.optimization_barrier((*pieces, got, got_next, c_next))
    pieces = traded(pieces)
    near_next = mate(near, 2)
    came = lax.ppermute(edge, "sub", ends)
    sweeps = [swept(0, right_side)]
    pieces[0] = after(pieces[0], sweeps[0])
    small = (width // GROUP, LANES)
    pay_rows = owned + chunk_of(owned)
    c0, v0, pay, pay_up, pay_down = call(
        start_kernel,
        [(count, LANES), (side, LANES), (pay_rows, LANES)] + [(pay_rows + width // GROUP, LANES)] * 2,
        (pos, *pieces),
    )
    came_next = mate(after(came, pay), 2)
    for part in range(1, parts):
        sweeps.append(swept(part, after(right_side, (pay, sweeps[-1]))))
    arrived = [planes(pay_up, 1)] + [planes(pay, k) for k in range(2, groups - 1)] + [planes(pay_down, -1)]
    near_late, near_next, came_late, came_next, got, got_next, c_next, arrived, _ = lax.optimization_barrier(
        (near, near_next, came, came_next, got, got_next, c_next, arrived, sweeps[-2])
    )
    theirs_c = mate(jnp.concatenate([coarse_inverse, c_next, got, got_next], axis=0), 1)
    theirs = mate(jnp.concatenate([near_late, near_next, came_late, came_next], axis=0), 1)
    us, kss = [x[0] for x in sweeps], [x[1] for x in sweeps]
    (solver,) = call(
        solver_kernel,
        [((2 * (GROUP + 3) * owned, coarse), BF16)],
        (pos, coarse_inverse, c_next, got, got_next, theirs_c),
    )
    cross, own, edge_up, edge_down = call(
        functools.partial(blocks_kernel, width),
        [((2 * side, GROUP * width), BF16), ((2 * count, GROUP * side), BF16)] + [((side, width), BF16)] * 2,
        (pos, near, near_next, came, came_next, theirs),
    )
    (far,) = call(far_kernel, [(side, side)], (pos, after(ks, sweeps[1]), right_side))
    far_next = mate(after(far, near_next), 2)

    now, state, sides = v0, (), []
    for step in range(ITERS):
        kind = "first" if step == 0 else "last" if step == ITERS - 1 else "middle"
        if kind == "first":
            pays = [after(pay, sweeps), *arrived]
        else:
            pays = [pay] + [planes(pay, k) for k in range(1, groups)]
            sides = [planes(up, 1), planes(down, -1)]
        if step == ITERS - 1:
            lam_pieces = traded(lax.optimization_barrier((*lam_pieces, *sides))[:GROUP])
        shapes = [(width, LANES), (width, LANES), (pay_rows, LANES)]
        if kind == "middle":
            shapes = shapes + [(side // GROUP, LANES)] * GROUP
        if kind == "last":
            shapes = [((count + width) // GROUP, LANES)] * GROUP
        outs = call(
            functools.partial(turn_kernel, kind, groups),
            shapes,
            (pos, *pays, solver, cross, own, edge_up, edge_down, c0, now, *sides, *state),
            scratch=[pltpu.VMEM((coarse, 2 * LANES), BF16)],
        )
        if kind == "first":
            (far_all,) = call(
                spans_kernel,
                [((2 * side, GROUP * side), BF16)],
                (pos, far, mate(far, 1), far_next, mate(far_next, 1)),
            )
        if kind != "last":
            state, pay = outs[:2], outs[2]
            now, up, down = call(again_kernel, [(side, LANES), small, small], (pos, far_all, v0, *state))
        if kind == "middle":
            lam_pieces = outs[3:]
    (spread,) = call(
        functools.partial(spread_kernel, parts),
        [(order, columns)],
        (pos, *lam_pieces, *us, *kss),
    )
    displaced, multipliers = call(
        functools.partial(final_kernel, parts, owned),
        [(order, columns), (width, columns)],
        (pos, *traded(outs), spread, *kss),
    )
    return displaced, multipliers


def solution(mesh):
    placed = (
        P(("rve", "sub"), None),
        P(("rve", "sub"), None),
        P(("rve", "sub"), None),
        P("sub", None, None),
        P("sub", None),
        P("sub", None),
    )
    return jax.shard_map(
        local,
        mesh=mesh,
        in_specs=placed,
        out_specs=(P(("rve", "sub"), None), P(("rve", "sub"), None)),
        check_vma=False,
    )
```

```python
import functools

import jax
import jax.numpy as jnp
from jax import lax
from jax.experimental import pallas as pl
from jax.experimental.pallas import tpu as pltpu
from jax.sharding import PartitionSpec as P

ITERS = 3
DAMPING = 0.5
GROUP = 4
LANES = 128
BF16 = jnp.bfloat16
F32 = jnp.float32


def call(kernel, outs, args, smem=1, hbm=(), scratch=(), vmem=24):
    in_specs = [
        pl.BlockSpec(memory_space=pltpu.SMEM if i < smem else pltpu.HBM if i in hbm else pltpu.VMEM)
        for i in range(len(args))
    ]
    shapes = [o if isinstance(o[0], tuple) else (o, F32) for o in outs]
    return pl.pallas_call(
        kernel,
        out_shape=[jax.ShapeDtypeStruct(s, d) for s, d in shapes],
        in_specs=in_specs,
        out_specs=[pl.BlockSpec(memory_space=pltpu.VMEM)] * len(shapes),
        scratch_shapes=list(scratch),
        compiler_params=pltpu.CompilerParams(vmem_limit_bytes=vmem * 1024 * 1024),
    )(*args)


def halves(x):
    high = x.astype(BF16)
    return high, (x - high.astype(F32)).astype(BF16)


def dot(a, b):
    return jnp.dot(a, b, preferred_element_type=F32)


def product(a, b):
    ah, al = halves(a)
    bh, bl = halves(b)
    n = b.shape[1]
    both = dot(ah, jnp.concatenate([bh, bl], axis=1))
    return both[:, :n] + both[:, n:] + dot(al, bh)


def lane_block(rows):
    return lax.broadcasted_iota(jnp.int32, (rows, LANES), 1) // (LANES // GROUP)


def turned(x, blocks):
    shift = (blocks % GROUP) * (LANES // GROUP)
    return x if shift == 0 else pltpu.roll(x, shift, 1)


def transposed(parts):
    block = lane_block(parts[0].shape[0])
    out = []
    for j in range(GROUP):
        total = turned(parts[0], -j)
        for q in range(1, GROUP):
            total = jnp.where(block == q, turned(parts[q], q - j), total)
        out.append(total)
    return out


def cut(x, out):
    rows = x.shape[0] // GROUP
    for j, part in enumerate(transposed([x[q * rows:(q + 1) * rows] for q in range(GROUP)])):
        out[j] = part


def joined(pieces):
    return jnp.concatenate(transposed([pieces[i] for i in range(GROUP)]), axis=0)


def packed(x, chunk):
    first = lane_block(chunk) == 0
    out = None
    for q in range(x.shape[0] // chunk):
        part = turned(jnp.where(first, x[q * chunk:(q + 1) * chunk], 0.0), q)
        out = part if out is None else out + part
    return out


def unpacked(x, count):
    return jnp.concatenate([turned(x, -q) for q in range(count)], axis=0)


def chunk_of(owned):
    return -(-owned // (GROUP * 8)) * 8


def stacked(x):
    return jnp.concatenate(halves(x), axis=0)


def beside(x):
    return jnp.concatenate(halves(x), axis=1)


def combined(p, n):
    m = p.shape[0] // 2
    return p[:m, :n] + p[:m, n:] + p[m:, :n]


def payload(v, width, group, out):
    groups, faces = out.shape[0], v[:2 * width]
    coarse = v[2 * width:]
    owned = coarse.shape[0] // 2
    below = turned(coarse[owned:], 1)
    rows = jnp.concatenate(
        [coarse[:owned] + jnp.where(lane_block(owned) == 0, 0.0, below), packed(below, chunk_of(owned))], axis=0
    )
    at = rows.shape[0]
    down, up = packed(faces[:width], width // GROUP), packed(turned(faces[width:], 1), width // GROUP)
    for h in range(groups):
        out[h, :at] = rows
        out[h, at:] = down
    out[lax.rem(group + 1, groups), at:] = up


def fetch(source, count, rows, target, places, sem):
    def one(j, carry):
        pltpu.make_async_copy(source.at[pl.ds(rows(j), 1)], target.at[pl.ds(places(j), 1)], sem).start()
        return carry

    lax.fori_loop(0, count, one, 0, unroll=8)


def rows_kernel(pos, face, prim, slot, k_ref, f_ref, c_ref, facev, primv, slotv, *rest):
    pieces, spans, edge, right_side, ks, sem = rest
    width, count, order, columns = face.shape[1], prim.shape[1], ks.shape[1], f_ref.shape[1]
    side = 2 * width
    fetch(k_ref, count, lambda j: prim[0, j], ks, lambda j: side + slot[0, j], sem)
    fetch(k_ref, side, lambda j: face[j // width, j % width], ks, lambda j: j, sem)

    def indicator(row):
        place = lax.broadcasted_iota(jnp.int32, (order, row.shape[1]), 0).astype(F32)
        return jnp.where(place == row, 1.0, 0.0).astype(BF16)

    slots = jnp.broadcast_to(slotv[...].astype(F32), (count, count)).T
    prims = jnp.broadcast_to(primv[...].astype(F32), (count, count)).T
    wanted = lax.broadcasted_iota(jnp.int32, (count, count), 1).astype(F32)
    by_slot = jnp.sum(jnp.where(slots == wanted, prims, 0.0), axis=0, keepdims=True)
    right_side[:, :width] = indicator(facev[0:1].astype(F32))
    right_side[:, width:side] = indicator(facev[1:2].astype(F32))
    right_side[:, side:side + count] = indicator(by_slot)
    right_side[:, side + count:side + width] = jnp.zeros((order, width - count), BF16)
    right_side[:, side + width:] = beside(f_ref[...])
    tall = c_ref.shape[1] // LANES
    owned = c_ref.shape[0]
    for i in range(tall):
        edge[width + i * owned:width + (i + 1) * owned] = c_ref[:, i * LANES:(i + 1) * LANES]
    pltpu.make_async_copy(k_ref.at[pl.ds(0, ks.shape[0])], ks, sem).wait()

    at = side + width
    high, low = halves(ks[...])
    both = dot(high, right_side[...])
    part = dot(low, right_side[:, :at + columns])
    cut(both[:, at:at + columns] + both[:, at + columns:] + part[:, at:], pieces)
    block = both[:, :at] + part[:, :at]
    rows = side + count
    for i in range(3):
        kept = side if i == 2 else rows
        spans[i * rows:i * rows + kept] = block[:kept, i * width:(i + 1) * width]
    edge[:width] = jnp.where(pos[0] == GROUP - 1, block[width:side, side:], block[:width, side:])


def sweep_kernel(first, pos, right_side, k_ref, u_ref, ks_ref):
    rows, columns = u_ref.shape
    at = right_side.shape[1] - 2 * columns
    high, low = halves(k_ref[first:first + rows])
    both = dot(high, right_side[...])
    part = dot(low, right_side[:, :at + columns])
    u_ref[...] = both[:, at:at + columns] + both[:, at + columns:] + part[:, at:]
    ks_ref[...] = both[:, :at] + part[:, :at]


GOT = (-1, None, 5, 4)
GOT_NEXT = (5, 4, -1, None)


GOT = (-1, None, 5, 4)
GOT_NEXT = (5, 4, -1, None)


def blocks_kernel(width, pos, c0, c2, s0, s2, came, came_next, theirs, solver, cross, own, edge_up, edge_down):
    side, size, edge_size = 2 * width, s0.shape[0], came.shape[0]
    kept = (size - side) // 2
    owned, tall = c0.shape[0], c0.shape[1] // LANES
    half = solver.shape[0] // 2
    other, at = [], 0
    for rows in (size, size, edge_size, edge_size, edge_size - width, edge_size - width):
        other.append(theirs.at[at:at + rows])
        at += rows
    for k, ref in enumerate((s0, other[0], s2, other[1])):
        own[:, k * side:k * side + width] = stacked(ref[:kept])
        own[:, k * side + width:(k + 1) * side] = stacked(ref[kept:2 * kept])
        cross[:, k * width:(k + 1) * width] = stacked(ref[2 * kept:])

    def placed(block, tile):
        at = (block + 1) * owned
        for i in range(tall):
            high, low = halves(tile(i))
            solver[at:at + owned, i * LANES:(i + 1) * LANES] = high
            solver[half + at:half + at + owned, i * LANES:(i + 1) * LANES] = low

    def wide(ref):
        return lambda i: ref[:, i * LANES:(i + 1) * LANES]

    def high_up(ref, first):
        return lambda i: ref[first + i * owned:first + (i + 1) * owned]

    for m in range(GROUP):

        @pl.when(pos[0] == m)
        def _():
            p = m ^ 1
            placed(m, wide(c0))
            placed(m ^ 2, wide(c2))
            placed(p, high_up(other[4], 0))
            placed(p ^ 2, high_up(other[5], 0))
            held = {}
            for block, ref in zip((GOT[m], GOT_NEXT[m], GOT[p], GOT_NEXT[p]), (came, came_next, other[2], other[3])):
                held.setdefault(block, ref)
            for block in (-1, 4, 5):
                placed(block, high_up(held[block], width))
            edge_up[...] = stacked(held[-1][:width])
            edge_down[...] = stacked(held[4][:width])


def start_kernel(pos, pieces, v_ref, pay_ref):
    v = joined(pieces)
    v_ref[...] = v
    payload(v, v.shape[1], pos[1], pay_ref)


def shared(x, member):
    block = lane_block(x.shape[0])
    high, low = halves(x)
    high, low = high.astype(F32), low.astype(F32)
    out = []
    for k in range(GROUP):
        mine = block == (member ^ k)
        pair = [jnp.where(mine, half, 0.0).astype(BF16) for half in (high, low)]
        out.append(jnp.concatenate(pair, axis=1))
    return jnp.concatenate(out, axis=0)


def turn_kernel(kind, pos, pays, solver, cross, own, edge_up, edge_down, v0, *refs):
    if kind == "first":
        now = v0
    else:
        (now, left_ref, right_ref), refs = refs[:3], refs[3:]
    outs, stack = refs[:-1], refs[-1]
    member, group = pos[0], pos[1]
    groups, width = pays.shape[0], edge_down.shape[1]
    owned = (v0.shape[0] - 2 * width) // 2
    size = owned + chunk_of(owned)
    first = lane_block(owned) == 0

    for h in range(groups):
        extra = unpacked(pays[(h - 1) % groups, owned:size], -(-owned // chunk_of(owned)))[:owned]
        whole = pays[h, :owned] + jnp.where(first, extra, 0.0)
        for i in range(GROUP):
            place = (h * GROUP + i) * owned
            stack[place:place + owned, :] = beside(turned(whole, -i))

    w = combined(dot(solver[...], stack[...]), LANES)
    pair = lane_block(2 * owned)
    q = w[owned:3 * owned]
    for i in range(1, GROUP):
        q = jnp.where(pair == i, turned(w[(i + 1) * owned:(i + 3) * owned], i), q)
    filler = jnp.zeros((width - 2 * owned, LANES), F32)

    def padded(x):
        return jnp.concatenate([x, filler], axis=0)

    faces = now[:2 * width] - combined(dot(cross[...], shared(padded(q), member)), LANES)
    left, right = faces[:width], faces[width:]
    before, after = beside(padded(w[:2 * owned])), beside(padded(w[(GROUP + 1) * owned:]))
    halo_up = pays[lax.rem(group + groups - 1, groups), size:]
    halo_down = pays[lax.rem(group + 1, groups), size:]
    right_before = unpacked(halo_up, GROUP) - combined(dot(edge_up[...], before), LANES)
    left_after = unpacked(halo_down, GROUP) - combined(dot(edge_down[...], after), LANES)
    block = lane_block(width)
    beyond = jnp.where(block == GROUP - 1, turned(left_after, GROUP - 1), turned(left, -1))
    behind = jnp.where(block == 0, right_before, turned(right, 1))
    lam_right = DAMPING * (right - beyond)
    lam_left = DAMPING * (behind - left)
    if kind != "first":
        lam_right = lam_right + right_ref[...]
        lam_left = lam_left + left_ref[...]
    if kind == "last":
        cut(jnp.concatenate([q, lam_right, left_ref[...], right_ref[...]], axis=0), outs[0])
        return
    v_ref, left_out, right_out, pay_ref = outs[:4]
    left_out[...] = lam_left
    right_out[...] = lam_right
    lam = jnp.concatenate([lam_left, -lam_right], axis=0)
    v = v0[...] + combined(dot(own[...], shared(lam, member)), LANES)
    v_ref[...] = v
    payload(v, width, group, pay_ref)


def final_kernel(parts, count, pos, pieces, *refs):
    x = joined(pieces)
    us, kss, (out, lam_ref) = refs[:parts], refs[parts:2 * parts], refs[2 * parts:]
    width = lam_ref.shape[0]
    lam_ref[...] = x[count:count + width]
    at = count + width
    filler = jnp.zeros((width - count, LANES), F32)
    change = beside(jnp.concatenate([x[at:at + width], -x[at + width:], -x[:count], filler], axis=0))
    at = 0
    for u, ks in zip(us, kss):
        out[at:at + u.shape[0]] = u[...] + combined(dot(stacked(ks[...]), change), LANES)
        at += u.shape[0]


def local(condensed, eigen_loads, coarse_inverse, face_rows, primal_rows, primal_slot):
    order, columns = eigen_loads.shape
    owned, coarse = coarse_inverse.shape
    width = face_rows.shape[2]
    side, count = 2 * width, 2 * owned
    kept = side + count
    total = lax.axis_size("sub")
    groups = total // GROUP
    me = lax.axis_index("sub")
    pos = jnp.stack([me % GROUP, me // GROUP]).astype(jnp.int32)
    faces = face_rows[0]

    def mate(x, k):
        return lax.ppermute(x, "sub", [(s, s ^ k) for s in range(total)])

    def crossing(x, pairs):
        pairs = [(g * GROUP + a, (g * GROUP + b) % total) for g in range(groups) for a, b in pairs]
        return lax.ppermute(x, "sub", pairs)

    def traded(x):
        planes = [[g * GROUP + m for m in range(GROUP)] for g in range(groups)]
        return lax.all_to_all(x, "sub", 0, 0, axis_index_groups=planes)

    def along(x):
        lines = [[g * GROUP + m for g in range(groups)] for m in range(GROUP)]
        return lax.all_to_all(x, "sub", 0, 0, axis_index_groups=lines)

    def after(x, other):
        return lax.optimization_barrier((x, other))[0]

    c_next = mate(coarse_inverse, 2)
    tall = owned * coarse // LANES
    pieces, spans, edge, right_side = call(
        rows_kernel,
        [
            (GROUP, kept // GROUP, LANES),
            (2 * kept + side, width),
            (width + tall, width),
            ((order, side + width + 2 * columns), BF16),
        ],
        (pos, faces, primal_rows, primal_slot, condensed, eigen_loads, coarse_inverse, faces, primal_rows, primal_slot),
        smem=4,
        hbm=(4,),
        scratch=[pltpu.VMEM((kept, order), F32), pltpu.SemaphoreType.DMA],
        vmem=52,
    )
    spans_next = mate(spans, 2)
    pieces = traded(after(pieces, c_next))
    pay_shape = (groups, owned + chunk_of(owned) + width // GROUP, LANES)
    v0, pay = call(start_kernel, [(kept, LANES), pay_shape], (pos, pieces))
    edge = after(edge, pay)
    came = crossing(edge, [(GROUP - 1, GROUP), (0, -1), (1, -2)])
    came_next = crossing(edge, [(GROUP - 1, GROUP + 2), (0, -3), (1, -4)])
    got = along(pay)

    parts = 4 if order % 64 == 0 else 1
    block = order // parts
    sweeps, later = [], after(right_side, pay)
    for part in range(parts):
        sweeps.append(call(
            functools.partial(sweep_kernel, part * block),
            [(block, columns), (block, side + width)],
            (pos, later, condensed),
        ))
        later = after(right_side, sweeps[-1])
    us, kss = [x[0] for x in sweeps], [x[1] for x in sweeps]
    spans_next, came, came_next, got = lax.optimization_barrier((spans_next, came, came_next, got, sweeps[:3]))[:4]

    def high_up(x):
        return jnp.concatenate([x[:, i:i + LANES] for i in range(0, coarse, LANES)], axis=0)

    theirs = [spans, spans_next, came, came_next, edge[width:], high_up(c_next)]
    theirs = mate(jnp.concatenate(theirs, axis=0), 1)
    blocks = call(
        functools.partial(blocks_kernel, width),
        [
            ((2 * (GROUP + 3) * owned, coarse), BF16),
            ((2 * side, GROUP * width), BF16),
            ((2 * kept, GROUP * side), BF16),
            ((side, width), BF16),
            ((side, width), BF16),
        ],
        (pos, coarse_inverse, c_next, spans, spans_next, came, came_next, theirs),
    )

    state = ()
    for step in range(ITERS):
        kind = "first" if step == 0 else "last" if step == ITERS - 1 else "middle"
        shapes = [(kept, LANES), (width, LANES), (width, LANES), pay_shape]
        if kind == "last":
            shapes = [(GROUP, (count + 3 * width) // GROUP, LANES)]
        outs = call(
            functools.partial(turn_kernel, kind),
            shapes,
            (pos, got, *blocks, v0, *state),
            scratch=[pltpu.VMEM((coarse, 2 * LANES), BF16)],
        )
        if kind != "last":
            state = outs[:3]
            got = along(outs[3])
    displaced, multipliers = call(
        functools.partial(final_kernel, parts, count),
        [(order, columns), (width, columns)],
        (pos, traded(outs[0]), *us, *kss),
    )
    return displaced, multipliers


def solution(mesh):
    placed = (
        P(("rve", "sub"), None),
        P(("rve", "sub"), None),
        P(("rve", "sub"), None),
        P("sub", None, None),
        P("sub", None),
        P("sub", None),
    )
    return jax.shard_map(
        local,
        mesh=mesh,
        in_specs=placed,
        out_specs=(P(("rve", "sub"), None), P(("rve", "sub"), None)),
        check_vma=False,
    )
```

```python
import functools

import jax
import jax.numpy as jnp
from jax import lax
from jax.experimental import pallas as pl
from jax.experimental.pallas import tpu as pltpu
from jax.sharding import PartitionSpec as P

ITERS = 3
DAMPING = 0.5
GROUP = 4
LANES = 128
BF16 = jnp.bfloat16
F32 = jnp.float32


def call(kernel, outs, args, smem=1, hbm=(), scratch=(), vmem=24):
    in_specs = [
        pl.BlockSpec(memory_space=pltpu.SMEM if i < smem else pltpu.HBM if i in hbm else pltpu.VMEM)
        for i in range(len(args))
    ]
    shapes = [o if isinstance(o[0], tuple) else (o, F32) for o in outs]
    return pl.pallas_call(
        kernel,
        out_shape=[jax.ShapeDtypeStruct(s, d) for s, d in shapes],
        in_specs=in_specs,
        out_specs=[pl.BlockSpec(memory_space=pltpu.VMEM)] * len(shapes),
        scratch_shapes=list(scratch),
        compiler_params=pltpu.CompilerParams(vmem_limit_bytes=vmem * 1024 * 1024),
    )(*args)


def halves(x):
    high = x.astype(BF16)
    return high, (x - high.astype(F32)).astype(BF16)


def dot(a, b):
    return jnp.dot(a, b, preferred_element_type=F32)


def product(a, b):
    ah, al = halves(a)
    bh, bl = halves(b)
    n = b.shape[1]
    both = dot(ah, jnp.concatenate([bh, bl], axis=1))
    return both[:, :n] + both[:, n:] + dot(al, bh)


def lane_block(rows):
    return lax.broadcasted_iota(jnp.int32, (rows, LANES), 1) // (LANES // GROUP)


def turned(x, blocks):
    width = LANES // GROUP
    if isinstance(blocks, int):
        shift = (blocks % GROUP) * width
        return x if shift == 0 else pltpu.roll(x, shift, 1)
    return pltpu.roll(x, lax.rem(blocks + 2 * GROUP, GROUP) * width, 1)


def cut(x, member, out_refs):
    rows = x.shape[0] // GROUP
    block = lane_block(rows)
    parts = [x[q * rows:(q + 1) * rows] for q in range(GROUP)]
    for k, out in enumerate(out_refs):
        to = member ^ k
        packed = jnp.zeros((rows, LANES), F32)
        for q in range(GROUP):
            packed = jnp.where(block == q, turned(parts[q], q - to), packed)
        out[...] = packed


def joined(pieces, member):
    rows = pieces[0].shape[0]
    block = lane_block(rows)
    out = []
    for q in range(GROUP):
        part = jnp.zeros((rows, LANES), F32)
        for k, piece in enumerate(pieces):
            came = member ^ k
            part = jnp.where(block == came, turned(piece, came - q), part)
        out.append(part)
    return jnp.concatenate(out, axis=0)


def packed(x, chunk):
    first = lane_block(chunk) == 0
    out = None
    for q in range(x.shape[0] // chunk):
        part = turned(jnp.where(first, x[q * chunk:(q + 1) * chunk], 0.0), q)
        out = part if out is None else out + part
    return out


def unpacked(x, count):
    return jnp.concatenate([turned(x, -q) for q in range(count)], axis=0)


def chunk_of(owned):
    return -(-owned // (GROUP * 8)) * 8


def stacked(x):
    return jnp.concatenate(halves(x), axis=0)


def beside(x):
    return jnp.concatenate(halves(x), axis=1)


def combined(p, n):
    m = p.shape[0] // 2
    return p[:m, :n] + p[:m, n:] + p[m:, :n]


def payload(v, width, out, out_up, out_down):
    coarse = v[2 * width:]
    owned = coarse.shape[0] // 2
    below = turned(coarse[owned:], 1)
    own = coarse[:owned] + jnp.where(lane_block(owned) == 0, 0.0, below)
    rows = jnp.concatenate([own, packed(below, chunk_of(owned))], axis=0)
    size = rows.shape[0]
    for ref in (out, out_up, out_down):
        ref[:size] = rows
    out_up[size:] = packed(turned(v[width:2 * width], 1), width // GROUP)
    out_down[size:] = packed(v[:width], width // GROUP)


def fetch(source, count, rows, target, places, sem):
    def one(j, carry):
        pltpu.make_async_copy(source.at[pl.ds(rows(j), 1)], target.at[pl.ds(places(j), 1)], sem).start()
        return carry

    lax.fori_loop(0, count, one, 0, unroll=8)


def rows_kernel(pos, face, prim, slot, k_ref, f_ref, facev, primv, slotv, *rest):
    pieces, (spans, edge, places, ks, right_side, sem) = rest[:GROUP], rest[GROUP:]
    width, count, order, columns = face.shape[1], prim.shape[1], ks.shape[1], f_ref.shape[1]
    side = 2 * width
    fetch(k_ref, count, lambda j: prim[0, j], ks, lambda j: side + slot[0, j], sem)
    fetch(k_ref, side, lambda j: face[j // width, j % width], ks, lambda j: j, sem)

    def indicator(row):
        place = lax.broadcasted_iota(jnp.int32, (order, row.shape[1]), 0).astype(F32)
        return jnp.where(place == row, 1.0, 0.0).astype(BF16)

    slots = jnp.broadcast_to(slotv[...].astype(F32), (count, count)).T
    prims = jnp.broadcast_to(primv[...].astype(F32), (count, count)).T
    wanted = lax.broadcasted_iota(jnp.int32, (count, count), 1).astype(F32)
    by_slot = jnp.sum(jnp.where(slots == wanted, prims, 0.0), axis=0, keepdims=True)
    right_side[:, :width] = indicator(facev[0:1].astype(F32))
    right_side[:, width:side] = indicator(facev[1:2].astype(F32))
    right_side[:, side:side + count] = indicator(by_slot)
    right_side[:, side + count:side + width] = jnp.zeros((order, width - count), BF16)
    right_side[:, side + width:] = beside(f_ref[...])
    places[...] = right_side[:, :side + width]
    pltpu.make_async_copy(k_ref.at[pl.ds(0, ks.shape[0])], ks, sem).wait()

    at = side + width
    high, low = halves(ks[...])
    both = dot(high, right_side[...])
    part = dot(low, right_side[:, :at + columns])
    cut(both[:, at:at + columns] + both[:, at + columns:] + part[:, at:], pos[0], pieces)
    block = both[:, :at] + part[:, :at]
    rows = side + count
    for i in range(3):
        kept = side if i == 2 else rows
        spans[i * rows:i * rows + kept] = block[:kept, i * width:(i + 1) * width]
    edge[...] = jnp.where(pos[0] == GROUP - 1, block[width:side, side:], block[:width, side:])


GOT = (-1, None, 5, 4)
GOT_NEXT = (5, 4, -1, None)


GOT = (-1, None, 5, 4)
GOT_NEXT = (5, 4, -1, None)


def solver_kernel(pos, mine, next_mine, got, next_got, theirs, out):
    owned = mine.shape[0]
    half = out.shape[0] // 2
    other = [theirs[i * owned:(i + 1) * owned] for i in range(4)]
    for m in range(GROUP):

        @pl.when(pos[0] == m)
        def _():
            p = m ^ 1
            held = [(m, mine[...]), (m ^ 2, next_mine[...]), (GOT[m], got[...]), (GOT_NEXT[m], next_got[...])]
            held += list(zip((p, p ^ 2, GOT[p], GOT_NEXT[p]), other))
            for block, values in held:
                if block is not None:
                    at = (block + 1) * owned
                    high, low = halves(values)
                    out[at:at + owned] = high
                    out[half + at:half + at + owned] = low


def blocks_kernel(width, pos, s0, s2, came, came_next, theirs, cross, own, edge_up, edge_down):
    side, size = 2 * width, s0.shape[0]
    kept = (size - side) // 2
    other, at = [], 0
    for rows in (size, size, width, width):
        other.append(theirs.at[at:at + rows])
        at += rows
    for k, ref in enumerate((s0, other[0], s2, other[1])):
        own[:, k * side:k * side + width] = stacked(ref[:kept])
        own[:, k * side + width:(k + 1) * side] = stacked(ref[kept:2 * kept])
        cross[:, k * width:(k + 1) * width] = stacked(ref[2 * kept:])
    for m in range(GROUP):

        @pl.when(pos[0] == m)
        def _():
            held = {GOT[m]: came, GOT_NEXT[m]: came_next}
            for block, ref in zip((GOT[m ^ 1], GOT_NEXT[m ^ 1]), other[2:]):
                held.setdefault(block, ref)
            edge_up[...] = stacked(held[-1][...])
            edge_down[...] = stacked(held[4][...])


def start_kernel(pos, p0, p1, p2, p3, v_ref, *pays):
    v = joined([p0[...], p1[...], p2[...], p3[...]], pos[0])
    v_ref[...] = v
    payload(v, v.shape[1], *pays)


def shared(x, member):
    block = lane_block(x.shape[0])
    high, low = halves(x)
    high, low = high.astype(F32), low.astype(F32)
    out = []
    for k in range(GROUP):
        mine = block == (member ^ k)
        pair = [jnp.where(mine, half, 0.0).astype(BF16) for half in (high, low)]
        out.append(jnp.concatenate(pair, axis=1))
    return jnp.concatenate(out, axis=0)


def turn_kernel(kind, groups, pos, *refs):
    pays, (solver, cross, own, edge_up, edge_down, v0), refs = refs[:groups], refs[groups:groups + 6], refs[groups + 6:]
    if kind == "first":
        now = v0
    else:
        (now, left_ref, right_ref), refs = refs[:3], refs[3:]
    outs, stack = refs[:-1], refs[-1]
    member, group = pos[0], pos[1]
    width = edge_down.shape[1]
    owned = (v0.shape[0] - 2 * width) // 2
    size = owned + chunk_of(owned)
    first = lane_block(owned) == 0

    for k in range(groups):
        h = lax.rem(group - k + groups, groups)
        extra = unpacked(pays[(k + 1) % groups][owned:size, :], -(-owned // chunk_of(owned)))[:owned]
        whole = pays[k][:owned, :] + jnp.where(first, extra, 0.0)
        for i in range(GROUP):
            place = pl.multiple_of((h * GROUP + i) * owned, 16)
            stack[pl.ds(place, owned), :] = beside(turned(whole, -i))

    w = combined(dot(solver[...], stack[...]), LANES)
    pair = lane_block(2 * owned)
    q = w[owned:3 * owned]
    for i in range(1, GROUP):
        q = jnp.where(pair == i, turned(w[(i + 1) * owned:(i + 3) * owned], i), q)
    filler = jnp.zeros((width - 2 * owned, LANES), F32)

    def padded(x):
        return jnp.concatenate([x, filler], axis=0)

    faces = now[:2 * width] - combined(dot(cross[...], shared(padded(q), member)), LANES)
    left, right = faces[:width], faces[width:]
    before, after = beside(padded(w[:2 * owned])), beside(padded(w[(GROUP + 1) * owned:]))
    halo_up, halo_down = pays[1][size:, :], pays[groups - 1][size:, :]
    right_before = unpacked(halo_up, GROUP) - combined(dot(edge_up[...], before), LANES)
    left_after = unpacked(halo_down, GROUP) - combined(dot(edge_down[...], after), LANES)
    block = lane_block(width)
    beyond = jnp.where(block == GROUP - 1, turned(left_after, GROUP - 1), turned(left, -1))
    behind = jnp.where(block == 0, right_before, turned(right, 1))
    lam_right = DAMPING * (right - beyond)
    lam_left = DAMPING * (behind - left)
    if kind != "first":
        lam_right = lam_right + right_ref[...]
        lam_left = lam_left + left_ref[...]
    if kind == "last":
        cut(jnp.concatenate([q, lam_right, left_ref[...], right_ref[...]], axis=0), member, outs)
        return
    v_ref, left_out, right_out = outs[:3]
    left_out[...] = lam_left
    right_out[...] = lam_right
    lam = jnp.concatenate([lam_left, -lam_right], axis=0)
    v = v0[...] + combined(dot(own[...], shared(lam, member)), LANES)
    v_ref[...] = v
    payload(v, width, *outs[3:])


def final_kernel(count, pos, p0, p1, p2, p3, f_ref, places, k_ref, out, lam_ref):
    x = joined([p0[...], p1[...], p2[...], p3[...]], pos[0])
    width = lam_ref.shape[0]
    lam_ref[...] = x[count:count + width]
    at = count + width
    filler = jnp.zeros((width - count, LANES), F32)
    change = beside(jnp.concatenate([x[at:at + width], -x[at + width:], -x[:count], filler], axis=0))
    both = dot(places[...], change)
    loads = beside(f_ref[...] + both[:, :LANES] + both[:, LANES:])
    order = k_ref.shape[0]
    rows = 256 if order % 256 == 0 else order
    for at in range(0, order, rows):
        high, low = halves(k_ref[at:at + rows])
        part = dot(high, loads)
        out[at:at + rows] = part[:, :LANES] + part[:, LANES:] + dot(low, loads[:, :LANES])


def local(condensed, eigen_loads, coarse_inverse, face_rows, primal_rows, primal_slot):
    order, columns = eigen_loads.shape
    owned, coarse = coarse_inverse.shape
    width = face_rows.shape[2]
    side, count = 2 * width, 2 * owned
    kept = side + count
    total = lax.axis_size("sub")
    groups = total // GROUP
    me = lax.axis_index("sub")
    pos = jnp.stack([me % GROUP, me // GROUP]).astype(jnp.int32)
    faces = face_rows[0]

    def mate(x, k):
        return lax.ppermute(x, "sub", [(s, s ^ k) for s in range(total)])

    def crossing(x, pairs):
        pairs = [(g * GROUP + a, (g * GROUP + b) % total) for g in range(groups) for a, b in pairs]
        return lax.ppermute(x, "sub", pairs)

    def traded(pieces):
        return [pieces[0]] + [mate(pieces[k], k) for k in range(1, GROUP)]

    def planes(x, by):
        return lax.ppermute(x, "sub", [(s, (s + by * GROUP) % total) for s in range(total)])

    def along(pay, up, down):
        return [pay, planes(up, 1)] + [planes(pay, k) for k in range(2, groups - 1)] + [planes(down, -1)]

    def after(x, other):
        return lax.optimization_barrier((x, other))[0]

    c_next = mate(coarse_inverse, 2)
    got = crossing(coarse_inverse, [(GROUP - 1, GROUP), (0, -1), (1, -2)])
    got_next = crossing(coarse_inverse, [(GROUP - 1, GROUP + 2), (0, -3), (1, -4)])

    *pieces, spans, edge, places = call(
        rows_kernel,
        [(kept // GROUP, LANES)] * GROUP
        + [(2 * kept + side, width), (width, width), ((order, side + width), BF16)],
        (pos, faces, primal_rows, primal_slot, condensed, eigen_loads, faces, primal_rows, primal_slot),
        smem=4,
        hbm=(4,),
        scratch=[
            pltpu.VMEM((kept, order), F32),
            pltpu.VMEM((order, side + width + 2 * columns), BF16),
            pltpu.SemaphoreType.DMA,
        ],
        vmem=52,
    )
    spans_next = mate(spans, 2)
    *pieces, c_next, got, got_next = lax.optimization_barrier((*pieces, c_next, got, got_next))
    pieces = traded(pieces)
    came = crossing(edge, [(GROUP - 1, GROUP), (0, -1)])
    came_next = crossing(after(edge, pieces), [(GROUP - 1, GROUP + 2), (0, -3)])
    theirs_c = mate(after(jnp.concatenate([coarse_inverse, c_next, got, got_next], axis=0), pieces), 1)
    size = owned + chunk_of(owned)
    pay_shapes = [(size, LANES)] + [(size + width // GROUP, LANES)] * 2
    v0, *pays = call(start_kernel, [(kept, LANES), *pay_shapes], (pos, *pieces))
    pays = along(*pays)
    (solver,) = call(
        solver_kernel,
        [((2 * (GROUP + 3) * owned, coarse), BF16)],
        (pos, coarse_inverse, c_next, got, got_next, theirs_c),
    )
    *pays, spans_next, came, came_next = lax.optimization_barrier((*pays, spans_next, came, came_next))
    theirs = mate(jnp.concatenate([spans, spans_next, came, came_next], axis=0), 1)
    blocks = call(
        functools.partial(blocks_kernel, width),
        [
            ((2 * side, GROUP * width), BF16),
            ((2 * kept, GROUP * side), BF16),
            ((side, width), BF16),
            ((side, width), BF16),
        ],
        (pos, spans, spans_next, came, came_next, theirs),
    )

    state = ()
    for step in range(ITERS):
        kind = "first" if step == 0 else "last" if step == ITERS - 1 else "middle"
        shapes = [(kept, LANES), (width, LANES), (width, LANES), *pay_shapes]
        if kind == "last":
            shapes = [((count + 3 * width) // GROUP, LANES)] * GROUP
        outs = call(
            functools.partial(turn_kernel, kind, groups),
            shapes,
            (pos, *pays, solver, *blocks, v0, *state),
            scratch=[pltpu.VMEM((coarse, 2 * LANES), BF16)],
        )
        if kind != "last":
            state = outs[:3]
            pays = along(*outs[3:])
    displaced, multipliers = call(
        functools.partial(final_kernel, count),
        [(order, columns), (width, columns)],
        (pos, *traded(outs), eigen_loads, places, condensed),
    )
    return displaced, multipliers


def solution(mesh):
    placed = (
        P(("rve", "sub"), None),
        P(("rve", "sub"), None),
        P(("rve", "sub"), None),
        P("sub", None, None),
        P("sub", None),
        P("sub", None),
    )
    return jax.shard_map(
        local,
        mesh=mesh,
        in_specs=placed,
        out_specs=(P(("rve", "sub"), None), P(("rve", "sub"), None)),
        check_vma=False,
    )
```

```python
import functools

import jax
import jax.numpy as jnp
from jax import lax
from jax.experimental import pallas as pl
from jax.experimental.pallas import tpu as pltpu
from jax.sharding import PartitionSpec as P

ITERS = 3
DAMPING = 0.5
GROUP = 4
LANES = 128
BF16 = jnp.bfloat16
F32 = jnp.float32


def call(kernel, outs, args, micros, smem=1, hbm=(), scratch=(), vmem=24):
    in_specs = [
        pl.BlockSpec(memory_space=pltpu.SMEM if i < smem else pltpu.HBM if i in hbm else pltpu.VMEM)
        for i in range(len(args))
    ]
    shapes = [o if isinstance(o[0], tuple) else (o, F32) for o in outs]
    return pl.pallas_call(
        kernel,
        out_shape=[jax.ShapeDtypeStruct(s, d) for s, d in shapes],
        in_specs=in_specs,
        out_specs=[pl.BlockSpec(memory_space=pltpu.VMEM)] * len(shapes),
        scratch_shapes=list(scratch),
        compiler_params=pltpu.CompilerParams(vmem_limit_bytes=vmem * 1024 * 1024),
        cost_estimate=pl.CostEstimate(flops=int(micros * 1e9), bytes_accessed=0, transcendentals=0),
    )(*args)


def halves(x):
    high = x.astype(BF16)
    return high, (x - high.astype(F32)).astype(BF16)


def dot(a, b):
    return jnp.dot(a, b, preferred_element_type=F32)


def product(a, b):
    ah, al = halves(a)
    bh, bl = halves(b)
    n = b.shape[1]
    both = dot(ah, jnp.concatenate([bh, bl], axis=1))
    return both[:, :n] + both[:, n:] + dot(al, bh)


def lane_block(rows):
    return lax.broadcasted_iota(jnp.int32, (rows, LANES), 1) // (LANES // GROUP)


def turned(x, blocks):
    width = LANES // GROUP
    if isinstance(blocks, int):
        shift = (blocks % GROUP) * width
        return x if shift == 0 else pltpu.roll(x, shift, 1)
    return pltpu.roll(x, lax.rem(blocks + 2 * GROUP, GROUP) * width, 1)


def cut(x, member, out_refs):
    rows = x.shape[0] // GROUP
    block = lane_block(rows)
    parts = [x[q * rows:(q + 1) * rows] for q in range(GROUP)]
    for k, out in enumerate(out_refs):
        to = member ^ k
        packed = jnp.zeros((rows, LANES), F32)
        for q in range(GROUP):
            packed = jnp.where(block == q, turned(parts[q], q - to), packed)
        out[...] = packed


def joined(pieces, member):
    rows = pieces[0].shape[0]
    block = lane_block(rows)
    out = []
    for q in range(GROUP):
        part = jnp.zeros((rows, LANES), F32)
        for k, piece in enumerate(pieces):
            came = member ^ k
            part = jnp.where(block == came, turned(piece, came - q), part)
        out.append(part)
    return jnp.concatenate(out, axis=0)


def packed(x, chunk):
    first = lane_block(chunk) == 0
    out = None
    for q in range(x.shape[0] // chunk):
        part = turned(jnp.where(first, x[q * chunk:(q + 1) * chunk], 0.0), q)
        out = part if out is None else out + part
    return out


def unpacked(x, count):
    return jnp.concatenate([turned(x, -q) for q in range(count)], axis=0)


def chunk_of(owned):
    return -(-owned // (GROUP * 8)) * 8


def stacked(x):
    return jnp.concatenate(halves(x), axis=0)


def beside(x):
    return jnp.concatenate(halves(x), axis=1)


def combined(p, n):
    m = p.shape[0] // 2
    return p[:m, :n] + p[:m, n:] + p[m:, :n]


def payload(v, width, out, out_up, out_down):
    coarse = v[2 * width:]
    owned = coarse.shape[0] // 2
    below = turned(coarse[owned:], 1)
    own = coarse[:owned] + jnp.where(lane_block(owned) == 0, 0.0, below)
    rows = jnp.concatenate([own, packed(below, chunk_of(owned))], axis=0)
    size = rows.shape[0]
    for ref in (out, out_up, out_down):
        ref[:size] = rows
    out_up[size:] = packed(turned(v[width:2 * width], 1), width // GROUP)
    out_down[size:] = packed(v[:width], width // GROUP)


def fetch(source, count, rows, target, places, sem):
    def one(j, carry):
        pltpu.make_async_copy(source.at[pl.ds(rows(j), 1)], target.at[pl.ds(places(j), 1)], sem).start()
        return carry

    lax.fori_loop(0, count, one, 0, unroll=8)


def rows_kernel(count, table, k_ref, f_ref, tablev, *rest):
    pieces, (spans, edge, places, ks, right_side, sem) = rest[:GROUP], rest[GROUP:]
    width, order, columns = edge.shape[1], ks.shape[1], f_ref.shape[1]
    side = 2 * width
    fetch(k_ref, count, lambda j: table[2, j], ks, lambda j: side + table[3, j], sem)
    fetch(k_ref, side, lambda j: table[j // width, j % width], ks, lambda j: j, sem)

    def indicator(row):
        place = lax.broadcasted_iota(jnp.int32, (order, row.shape[1]), 0).astype(F32)
        return jnp.where(place == row, 1.0, 0.0).astype(BF16)

    slots = jnp.broadcast_to(tablev[3:4, :count].astype(F32), (count, count)).T
    prims = jnp.broadcast_to(tablev[2:3, :count].astype(F32), (count, count)).T
    wanted = lax.broadcasted_iota(jnp.int32, (count, count), 1).astype(F32)
    by_slot = jnp.sum(jnp.where(slots == wanted, prims, 0.0), axis=0, keepdims=True)
    right_side[:, :width] = indicator(tablev[0:1].astype(F32))
    right_side[:, width:side] = indicator(tablev[1:2].astype(F32))
    right_side[:, side:side + count] = indicator(by_slot)
    right_side[:, side + count:side + width] = jnp.zeros((order, width - count), BF16)
    right_side[:, side + width:] = beside(f_ref[...])
    places[...] = right_side[:, :side + width]
    pltpu.make_async_copy(k_ref.at[pl.ds(0, ks.shape[0])], ks, sem).wait()

    at = side + width
    high, low = halves(ks[...])
    both = dot(high, right_side[...])
    part = dot(low, right_side[:, :at + columns])
    cut(both[:, at:at + columns] + both[:, at + columns:] + part[:, at:], table[4, 0], pieces)
    block = both[:, :at] + part[:, :at]
    rows = side + count
    for i in range(3):
        kept = side if i == 2 else rows
        spans[i * rows:i * rows + kept] = block[:kept, i * width:(i + 1) * width]
    edge[...] = jnp.where(table[4, 0] == GROUP - 1, block[width:side, side:], block[:width, side:])


GOT = (-1, None, 5, 4)
GOT_NEXT = (5, 4, -1, None)


GOT = (-1, None, 5, 4)
GOT_NEXT = (5, 4, -1, None)


def solver_kernel(pos, mine, next_mine, got, next_got, theirs, out):
    owned = mine.shape[0]
    half = out.shape[0] // 2
    other = [theirs[i * owned:(i + 1) * owned] for i in range(4)]
    for m in range(GROUP):

        @pl.when(pos[0] == m)
        def _():
            p = m ^ 1
            held = [(m, mine[...]), (m ^ 2, next_mine[...]), (GOT[m], got[...]), (GOT_NEXT[m], next_got[...])]
            held += list(zip((p, p ^ 2, GOT[p], GOT_NEXT[p]), other))
            for block, values in held:
                if block is not None:
                    at = (block + 1) * owned
                    high, low = halves(values)
                    out[at:at + owned] = high
                    out[half + at:half + at + owned] = low


def blocks_kernel(width, pos, s0, s2, came, came_next, theirs, cross, own, edge_up, edge_down):
    side, size = 2 * width, s0.shape[0]
    kept = (size - side) // 2
    other, at = [], 0
    for rows in (size, size, width, width):
        other.append(theirs.at[at:at + rows])
        at += rows
    for k, ref in enumerate((s0, other[0], s2, other[1])):
        own[:, k * side:k * side + width] = stacked(ref[:kept])
        own[:, k * side + width:(k + 1) * side] = stacked(ref[kept:2 * kept])
        cross[:, k * width:(k + 1) * width] = stacked(ref[2 * kept:])
    for m in range(GROUP):

        @pl.when(pos[0] == m)
        def _():
            held = {GOT[m]: came, GOT_NEXT[m]: came_next}
            for block, ref in zip((GOT[m ^ 1], GOT_NEXT[m ^ 1]), other[2:]):
                held.setdefault(block, ref)
            edge_up[...] = stacked(held[-1][...])
            edge_down[...] = stacked(held[4][...])


def start_kernel(pos, p0, p1, p2, p3, v_ref, *pays):
    v = joined([p0[...], p1[...], p2[...], p3[...]], pos[0])
    v_ref[...] = v
    payload(v, v.shape[1], *pays)


def shared(x, member):
    block = lane_block(x.shape[0])
    high, low = halves(x)
    high, low = high.astype(F32), low.astype(F32)
    out = []
    for k in range(GROUP):
        mine = block == (member ^ k)
        pair = [jnp.where(mine, half, 0.0).astype(BF16) for half in (high, low)]
        out.append(jnp.concatenate(pair, axis=1))
    return jnp.concatenate(out, axis=0)


def turn_kernel(kind, groups, pos, *refs):
    pays, (solver, cross, own, edge_up, edge_down, v0), refs = refs[:groups], refs[groups:groups + 6], refs[groups + 6:]
    if kind == "first":
        now = v0
    else:
        (now, left_ref, right_ref), refs = refs[:3], refs[3:]
    outs, stack = refs[:-1], refs[-1]
    member, group = pos[0], pos[1]
    width = edge_down.shape[1]
    owned = (v0.shape[0] - 2 * width) // 2
    size = owned + chunk_of(owned)
    first = lane_block(owned) == 0

    for k in range(groups):
        h = lax.rem(group - k + groups, groups)
        extra = unpacked(pays[(k + 1) % groups][owned:size, :], -(-owned // chunk_of(owned)))[:owned]
        whole = pays[k][:owned, :] + jnp.where(first, extra, 0.0)
        for i in range(GROUP):
            place = pl.multiple_of((h * GROUP + i) * owned, 16)
            stack[pl.ds(place, owned), :] = beside(turned(whole, -i))

    w = combined(dot(solver[...], stack[...]), LANES)
    pair = lane_block(2 * owned)
    q = w[owned:3 * owned]
    for i in range(1, GROUP):
        q = jnp.where(pair == i, turned(w[(i + 1) * owned:(i + 3) * owned], i), q)
    filler = jnp.zeros((width - 2 * owned, LANES), F32)

    def padded(x):
        return jnp.concatenate([x, filler], axis=0)

    faces = now[:2 * width] - combined(dot(cross[...], shared(padded(q), member)), LANES)
    left, right = faces[:width], faces[width:]
    before, after = beside(padded(w[:2 * owned])), beside(padded(w[(GROUP + 1) * owned:]))
    halo_up, halo_down = pays[1][size:, :], pays[groups - 1][size:, :]
    right_before = unpacked(halo_up, GROUP) - combined(dot(edge_up[...], before), LANES)
    left_after = unpacked(halo_down, GROUP) - combined(dot(edge_down[...], after), LANES)
    block = lane_block(width)
    beyond = jnp.where(block == GROUP - 1, turned(left_after, GROUP - 1), turned(left, -1))
    behind = jnp.where(block == 0, right_before, turned(right, 1))
    lam_right = DAMPING * (right - beyond)
    lam_left = DAMPING * (behind - left)
    if kind != "first":
        lam_right = lam_right + right_ref[...]
        lam_left = lam_left + left_ref[...]
    if kind == "last":
        cut(jnp.concatenate([q, lam_right, left_ref[...], right_ref[...]], axis=0), member, outs)
        return
    v_ref, left_out, right_out = outs[:3]
    left_out[...] = lam_left
    right_out[...] = lam_right
    lam = jnp.concatenate([lam_left, -lam_right], axis=0)
    v = v0[...] + combined(dot(own[...], shared(lam, member)), LANES)
    v_ref[...] = v
    payload(v, width, *outs[3:])


def final_kernel(count, pos, p0, p1, p2, p3, f_ref, places, k_ref, out, lam_ref):
    x = joined([p0[...], p1[...], p2[...], p3[...]], pos[0])
    width = lam_ref.shape[0]
    lam_ref[...] = x[count:count + width]
    at = count + width
    filler = jnp.zeros((width - count, LANES), F32)
    change = beside(jnp.concatenate([x[at:at + width], -x[at + width:], -x[:count], filler], axis=0))
    both = dot(places[...], change)
    loads = beside(f_ref[...] + both[:, :LANES] + both[:, LANES:])
    order = k_ref.shape[0]
    rows = 256 if order % 256 == 0 else order
    for at in range(0, order, rows):
        high, low = halves(k_ref[at:at + rows])
        part = dot(high, loads)
        out[at:at + rows] = part[:, :LANES] + part[:, LANES:] + dot(low, loads[:, :LANES])


def local(condensed, eigen_loads, coarse_inverse, face_rows, primal_rows, primal_slot):
    order, columns = eigen_loads.shape
    owned, coarse = coarse_inverse.shape
    width = face_rows.shape[2]
    side, count = 2 * width, 2 * owned
    kept = side + count
    total = lax.axis_size("sub")
    groups = total // GROUP
    me = lax.axis_index("sub")
    pos = jnp.stack([me % GROUP, me // GROUP]).astype(jnp.int32)

    def row(x):
        return jnp.pad(x[None], ((0, 0), (0, width - x.shape[0])))

    table = jnp.concatenate([face_rows[0], row(primal_rows[0]), row(primal_slot[0]), row(pos)], axis=0)

    def mate(x, k):
        return lax.ppermute(x, "sub", [(s, s ^ k) for s in range(total)])

    def crossing(x, pairs):
        pairs = [(g * GROUP + a, (g * GROUP + b) % total) for g in range(groups) for a, b in pairs]
        return lax.ppermute(x, "sub", pairs)

    def traded(pieces):
        return [pieces[0]] + [mate(pieces[k], k) for k in range(1, GROUP)]

    def planes(x, by):
        return lax.ppermute(x, "sub", [(s, (s + by * GROUP) % total) for s in range(total)])

    def along(pay, up, down):
        return [pay, planes(up, 1)] + [planes(pay, k) for k in range(2, groups - 1)] + [planes(down, -1)]

    def after(x, other):
        return lax.optimization_barrier((x, other))[0]

    c_next = mate(coarse_inverse, 2)
    got = crossing(coarse_inverse, [(GROUP - 1, GROUP), (0, -1), (1, -2)])
    got_next = crossing(coarse_inverse, [(GROUP - 1, GROUP + 2), (0, -3), (1, -4)])

    *pieces, spans, edge, places = call(
        functools.partial(rows_kernel, count),
        [(kept // GROUP, LANES)] * GROUP
        + [(2 * kept + side, width), (width, width), ((order, side + width), BF16)],
        (table, condensed, eigen_loads, table),
        7.5,
        hbm=(1,),
        scratch=[
            pltpu.VMEM((kept, order), F32),
            pltpu.VMEM((order, side + width + 2 * columns), BF16),
            pltpu.SemaphoreType.DMA,
        ],
        vmem=52,
    )
    spans_next = mate(after(spans, (c_next, got, got_next)), 2)
    *pieces, c_next, got, got_next = lax.optimization_barrier((*pieces, c_next, got, got_next))
    pieces = traded(pieces)
    came = crossing(after(edge, pieces), [(GROUP - 1, GROUP), (0, -1)])
    theirs_c = mate(after(jnp.concatenate([coarse_inverse, c_next, got, got_next], axis=0), pieces), 1)
    size = owned + chunk_of(owned)
    pay_shapes = [(size, LANES)] + [(size + width // GROUP, LANES)] * 2
    v0, *pays = call(start_kernel, [(kept, LANES), *pay_shapes], (pos, *pieces), 0.9)
    came_next = crossing(after(edge, pays), [(GROUP - 1, GROUP + 2), (0, -3)])
    pays = along(*pays)
    (solver,) = call(
        solver_kernel,
        [((2 * (GROUP + 3) * owned, coarse), BF16)],
        (pos, coarse_inverse, c_next, got, got_next, theirs_c),
        0.7,
    )
    *pays, spans_next, came, came_next = lax.optimization_barrier((*pays, spans_next, came, came_next))
    theirs = mate(jnp.concatenate([spans, spans_next, came, came_next], axis=0), 1)
    blocks = call(
        functools.partial(blocks_kernel, width),
        [
            ((2 * side, GROUP * width), BF16),
            ((2 * kept, GROUP * side), BF16),
            ((side, width), BF16),
            ((side, width), BF16),
        ],
        (pos, spans, spans_next, came, came_next, theirs),
        1,
    )

    state = ()
    for step in range(ITERS):
        kind = "first" if step == 0 else "last" if step == ITERS - 1 else "middle"
        shapes = [(kept, LANES), (width, LANES), (width, LANES), *pay_shapes]
        if kind == "last":
            shapes = [((count + 3 * width) // GROUP, LANES)] * GROUP
        outs = call(
            functools.partial(turn_kernel, kind, groups),
            shapes,
            (pos, *pays, solver, *blocks, v0, *state),
            2.8,
            scratch=[pltpu.VMEM((coarse, 2 * LANES), BF16)],
        )
        if kind != "last":
            state = outs[:3]
            pays = along(*outs[3:])
    displaced, multipliers = call(
        functools.partial(final_kernel, count),
        [(order, columns), (width, columns)],
        (pos, *traded(outs), eigen_loads, places, condensed),
        5.3,
    )
    return displaced, multipliers


def solution(mesh):
    placed = (
        P(("rve", "sub"), None),
        P(("rve", "sub"), None),
        P(("rve", "sub"), None),
        P("sub", None, None),
        P("sub", None),
        P("sub", None),
    )
    return jax.shard_map(
        local,
        mesh=mesh,
        in_specs=placed,
        out_specs=(P(("rve", "sub"), None), P(("rve", "sub"), None)),
        check_vma=False,
    )
```

```python
import functools

import jax
import jax.numpy as jnp
from jax import lax
from jax.experimental import pallas as pl
from jax.experimental.pallas import tpu as pltpu
from jax.sharding import PartitionSpec as P

ITERS = 3
DAMPING = 0.5
GROUP = 4
PAIRED = 4
LANES = 128
BF16 = jnp.bfloat16
F32 = jnp.float32


def call(kernel, outs, args, micros, smem=1, hbm=(), scratch=(), vmem=24):
    in_specs = [
        pl.BlockSpec(memory_space=pltpu.SMEM if i < smem else pltpu.HBM if i in hbm else pltpu.VMEM)
        for i in range(len(args))
    ]
    shapes = [o if isinstance(o[0], tuple) else (o, F32) for o in outs]
    return pl.pallas_call(
        kernel,
        out_shape=[jax.ShapeDtypeStruct(s, d) for s, d in shapes],
        in_specs=in_specs,
        out_specs=[pl.BlockSpec(memory_space=pltpu.VMEM)] * len(shapes),
        scratch_shapes=list(scratch),
        compiler_params=pltpu.CompilerParams(vmem_limit_bytes=vmem * 1024 * 1024),
        cost_estimate=pl.CostEstimate(flops=int(micros * 1e9), bytes_accessed=0, transcendentals=0),
    )(*args)


def halves(x):
    high = x.astype(BF16)
    return high, (x - high.astype(F32)).astype(BF16)


def dot(a, b):
    return jnp.dot(a, b, preferred_element_type=F32)


def product(a, b):
    ah, al = halves(a)
    bh, bl = halves(b)
    n = b.shape[1]
    both = dot(ah, jnp.concatenate([bh, bl], axis=1))
    return both[:, :n] + both[:, n:] + dot(al, bh)


def lane_block(rows):
    return lax.broadcasted_iota(jnp.int32, (rows, LANES), 1) // (LANES // GROUP)


def turned(x, blocks):
    width = LANES // GROUP
    if isinstance(blocks, int):
        shift = (blocks % GROUP) * width
        return x if shift == 0 else pltpu.roll(x, shift, 1)
    return pltpu.roll(x, lax.rem(blocks + 2 * GROUP, GROUP) * width, 1)


def cut(x, member, out_refs):
    rows = x.shape[0] // GROUP
    block = lane_block(rows)
    parts = [x[q * rows:(q + 1) * rows] for q in range(GROUP)]
    for k, out in enumerate(out_refs):
        to = member ^ k
        packed = jnp.zeros((rows, LANES), F32)
        for q in range(GROUP):
            packed = jnp.where(block == q, turned(parts[q], q - to), packed)
        out[...] = packed


def joined(pieces, member):
    rows = pieces[0].shape[0]
    block = lane_block(rows)
    out = []
    for q in range(GROUP):
        part = jnp.zeros((rows, LANES), F32)
        for k, piece in enumerate(pieces):
            came = member ^ k
            part = jnp.where(block == came, turned(piece, came - q), part)
        out.append(part)
    return jnp.concatenate(out, axis=0)


def packed(x, chunk):
    first = lane_block(chunk) == 0
    out = None
    for q in range(x.shape[0] // chunk):
        part = turned(jnp.where(first, x[q * chunk:(q + 1) * chunk], 0.0), q)
        out = part if out is None else out + part
    return out


def unpacked(x, count):
    return jnp.concatenate([turned(x, -q) for q in range(count)], axis=0)


def chunk_of(owned):
    return -(-owned // (GROUP * 8)) * 8


def stacked(x):
    return jnp.concatenate(halves(x), axis=0)


def beside(x):
    return jnp.concatenate(halves(x), axis=1)


def combined(p, n):
    m = p.shape[0] // 2
    return p[:m, :n] + p[:m, n:] + p[m:, :n]


def payload(v, width, paired, odd, out, out_a, out_b):
    coarse = v[2 * width:]
    owned = coarse.shape[0] // 2
    below = turned(coarse[owned:], 1)
    own = coarse[:owned] + jnp.where(lane_block(owned) == 0, 0.0, below)
    rows = jnp.concatenate([own, packed(below, chunk_of(owned))], axis=0)
    size = rows.shape[0]
    for ref in (out, out_a, out_b):
        ref[:size] = rows
    up = packed(turned(v[width:2 * width], 1), width // GROUP)
    down = packed(v[:width], width // GROUP)
    if paired:
        up, down = jnp.where(odd, down, up), jnp.where(odd, up, down)
    out_a[size:] = up
    out_b[size:] = down


def fetch(source, count, rows, target, places, sem):
    def one(j, carry):
        pltpu.make_async_copy(source.at[pl.ds(rows(j), 1)], target.at[pl.ds(places(j), 1)], sem).start()
        return carry

    lax.fori_loop(0, count, one, 0, unroll=8)


def rows_kernel(count, table, k_ref, f_ref, c_ref, tablev, *rest):
    pieces, (spans, edge, places, ks, right_side, sem) = rest[:GROUP], rest[GROUP:]
    width, order, columns = edge.shape[1], ks.shape[1], f_ref.shape[1]
    owned = c_ref.shape[0]
    side = 2 * width
    fetch(k_ref, count, lambda j: table[2, j], ks, lambda j: side + table[3, j], sem)
    fetch(k_ref, side, lambda j: table[j // width, j % width], ks, lambda j: j, sem)

    def indicator(row):
        place = lax.broadcasted_iota(jnp.int32, (order, row.shape[1]), 0).astype(F32)
        return jnp.where(place == row, 1.0, 0.0).astype(BF16)

    slots = jnp.broadcast_to(tablev[3:4, :count].astype(F32), (count, count)).T
    prims = jnp.broadcast_to(tablev[2:3, :count].astype(F32), (count, count)).T
    wanted = lax.broadcasted_iota(jnp.int32, (count, count), 1).astype(F32)
    by_slot = jnp.sum(jnp.where(slots == wanted, prims, 0.0), axis=0, keepdims=True)
    right_side[:, :width] = indicator(tablev[0:1].astype(F32))
    right_side[:, width:side] = indicator(tablev[1:2].astype(F32))
    right_side[:, side:side + count] = indicator(by_slot)
    right_side[:, side + count:side + width] = jnp.zeros((order, width - count), BF16)
    right_side[:, side + width:] = beside(f_ref[...])
    places[...] = right_side[:, :side + width]
    for i in range(c_ref.shape[1] // LANES):
        at = width + i * owned
        edge[at:at + owned] = c_ref[:, i * LANES:(i + 1) * LANES]
    pltpu.make_async_copy(k_ref.at[pl.ds(0, ks.shape[0])], ks, sem).wait()

    at = side + width
    high, low = halves(ks[...])
    both = dot(high, right_side[...])
    part = dot(low, right_side[:, :at + columns])
    cut(both[:, at:at + columns] + both[:, at + columns:] + part[:, at:], table[4, 0], pieces)
    block = both[:, :at] + part[:, :at]
    rows = side + count
    for i in range(3):
        kept = side if i == 2 else rows
        spans[i * rows:i * rows + kept] = block[:kept, i * width:(i + 1) * width]
    edge[:width] = jnp.where(table[4, 0] == GROUP - 1, block[width:side, side:], block[:width, side:])


GOT = (-1, None, 5, 4)
GOT_NEXT = (5, 4, -1, None)


GOT = (-1, None, 5, 4)
GOT_NEXT = (5, 4, -1, None)


def blocks_kernel(width, pos, c0, c2, c_other, s0, s2, came, came_next, theirs, solver, cross, own, edge_up, edge_down):
    side, size, edge_size = 2 * width, s0.shape[0], came.shape[0]
    kept = (size - side) // 2
    owned, tall = c0.shape[0], c0.shape[1] // LANES
    half = solver.shape[0] // 2
    other, at = [], 0
    for rows in (size, size, edge_size, edge_size):
        other.append(theirs.at[at:at + rows])
        at += rows
    for k, ref in enumerate((s0, other[0], s2, other[1])):
        own[:, k * side:k * side + width] = stacked(ref[:kept])
        own[:, k * side + width:(k + 1) * side] = stacked(ref[kept:2 * kept])
        cross[:, k * width:(k + 1) * width] = stacked(ref[2 * kept:])

    def placed(block, values, columns):
        at = (block + 1) * owned
        high, low = halves(values)
        solver[at:at + owned, columns] = high
        solver[half + at:half + at + owned, columns] = low

    for m in range(GROUP):

        @pl.when(pos[0] == m)
        def _():
            p = m ^ 1
            everything = slice(None)
            placed(m, c0[...], everything)
            placed(m ^ 2, c2[...], everything)
            placed(p, c_other[:owned], everything)
            placed(p ^ 2, c_other[owned:], everything)
            held = {GOT[m]: came, GOT_NEXT[m]: came_next}
            for block, ref in zip((GOT[p], GOT_NEXT[p]), other[2:]):
                held.setdefault(block, ref)
            for block in (-1, 4, 5):
                for i in range(tall):
                    at = width + i * owned
                    placed(block, held[block][at:at + owned], slice(i * LANES, (i + 1) * LANES))
            edge_up[...] = stacked(held[-1][:width])
            edge_down[...] = stacked(held[4][:width])


def start_kernel(paired, pos, p0, p1, p2, p3, v_ref, *pays):
    v = joined([p0[...], p1[...], p2[...], p3[...]], pos[0])
    v_ref[...] = v
    payload(v, v.shape[1], paired, pos[1] % 2 == 1, *pays)


def shared(x, member):
    block = lane_block(x.shape[0])
    high, low = halves(x)
    high, low = high.astype(F32), low.astype(F32)
    out = []
    for k in range(GROUP):
        mine = block == (member ^ k)
        pair = [jnp.where(mine, half, 0.0).astype(BF16) for half in (high, low)]
        out.append(jnp.concatenate(pair, axis=1))
    return jnp.concatenate(out, axis=0)


def turn_kernel(kind, groups, pos, *refs):
    pays, (solver, cross, own, edge_up, edge_down, v0), refs = refs[:groups], refs[groups:groups + 6], refs[groups + 6:]
    if kind == "first":
        now = v0
    else:
        (now, left_ref, right_ref), refs = refs[:3], refs[3:]
    outs, (held, stack) = refs[:-2], refs[-2:]
    paired = groups == PAIRED
    member, group = pos[0], pos[1]
    width = edge_down.shape[1]
    owned = (v0.shape[0] - 2 * width) // 2
    size = owned + chunk_of(owned)
    first = lane_block(owned) == 0

    for k in range(groups):
        held[group ^ k if paired else lax.rem(group - k + groups, groups)] = pays[k][:size, :]
    for h in range(groups):
        extra = unpacked(held[(h - 1) % groups, owned:], -(-owned // chunk_of(owned)))[:owned]
        whole = held[h, :owned] + jnp.where(first, extra, 0.0)
        for i in range(GROUP):
            place = (h * GROUP + i) * owned
            stack[place:place + owned, :] = beside(turned(whole, -i))

    w = combined(dot(solver[...], stack[...]), LANES)
    pair = lane_block(2 * owned)
    q = w[owned:3 * owned]
    for i in range(1, GROUP):
        q = jnp.where(pair == i, turned(w[(i + 1) * owned:(i + 3) * owned], i), q)
    filler = jnp.zeros((width - 2 * owned, LANES), F32)

    def padded(x):
        return jnp.concatenate([x, filler], axis=0)

    faces = now[:2 * width] - combined(dot(cross[...], shared(padded(q), member)), LANES)
    left, right = faces[:width], faces[width:]
    before, after = beside(padded(w[:2 * owned])), beside(padded(w[(GROUP + 1) * owned:]))
    halo_up, halo_down = pays[1][size:, :], pays[groups - 1][size:, :]
    if paired:
        odd = group % 2 == 1
        halo_up, halo_down = jnp.where(odd, halo_up, halo_down), jnp.where(odd, halo_down, halo_up)
    right_before = unpacked(halo_up, GROUP) - combined(dot(edge_up[...], before), LANES)
    left_after = unpacked(halo_down, GROUP) - combined(dot(edge_down[...], after), LANES)
    block = lane_block(width)
    beyond = jnp.where(block == GROUP - 1, turned(left_after, GROUP - 1), turned(left, -1))
    behind = jnp.where(block == 0, right_before, turned(right, 1))
    lam_right = DAMPING * (right - beyond)
    lam_left = DAMPING * (behind - left)
    if kind != "first":
        lam_right = lam_right + right_ref[...]
        lam_left = lam_left + left_ref[...]
    if kind == "last":
        cut(jnp.concatenate([q, lam_right, left_ref[...], right_ref[...]], axis=0), member, outs)
        return
    v_ref, left_out, right_out = outs[:3]
    left_out[...] = lam_left
    right_out[...] = lam_right
    lam = jnp.concatenate([lam_left, -lam_right], axis=0)
    v = v0[...] + combined(dot(own[...], shared(lam, member)), LANES)
    v_ref[...] = v
    payload(v, width, paired, group % 2 == 1, *outs[3:])


def final_kernel(count, pos, p0, p1, p2, p3, f_ref, places, k_ref, out, lam_ref):
    x = joined([p0[...], p1[...], p2[...], p3[...]], pos[0])
    width = lam_ref.shape[0]
    lam_ref[...] = x[count:count + width]
    at = count + width
    filler = jnp.zeros((width - count, LANES), F32)
    change = beside(jnp.concatenate([x[at:at + width], -x[at + width:], -x[:count], filler], axis=0))
    both = dot(places[...], change)
    loads = beside(f_ref[...] + both[:, :LANES] + both[:, LANES:])
    order = k_ref.shape[0]
    rows = 256 if order % 256 == 0 else order
    for at in range(0, order, rows):
        high, low = halves(k_ref[at:at + rows])
        part = dot(high, loads)
        out[at:at + rows] = part[:, :LANES] + part[:, LANES:] + dot(low, loads[:, :LANES])


def local(condensed, eigen_loads, coarse_inverse, face_rows, primal_rows, primal_slot):
    order, columns = eigen_loads.shape
    owned, coarse = coarse_inverse.shape
    width = face_rows.shape[2]
    side, count = 2 * width, 2 * owned
    kept = side + count
    total = lax.axis_size("sub")
    groups = total // GROUP
    me = lax.axis_index("sub")
    pos = jnp.stack([me % GROUP, me // GROUP]).astype(jnp.int32)

    def row(x):
        return jnp.pad(x[None], ((0, 0), (0, width - x.shape[0])))

    table = jnp.concatenate([face_rows[0], row(primal_rows[0]), row(primal_slot[0]), row(pos)], axis=0)

    def mate(x, k):
        return lax.ppermute(x, "sub", [(s, s ^ k) for s in range(total)])

    def crossing(x, pairs):
        pairs = [(g * GROUP + a, (g * GROUP + b) % total) for g in range(groups) for a, b in pairs]
        return lax.ppermute(x, "sub", pairs)

    def traded(pieces):
        return [pieces[0]] + [mate(pieces[k], k) for k in range(1, GROUP)]

    def planes(x, by):
        return lax.ppermute(x, "sub", [(s, (s + by * GROUP) % total) for s in range(total)])

    def along(pay, a, b):
        if groups == PAIRED:
            last = mate(b, 3 * GROUP)
            middle = mate(pay, 2 * GROUP)
            return [pay, mate(a, GROUP), middle, last]
        return [pay, planes(a, 1)] + [planes(pay, k) for k in range(2, groups - 1)] + [planes(b, -1)]

    def after(x, other):
        return lax.optimization_barrier((x, other))[0]

    c_next = mate(coarse_inverse, 2)
    tall = owned * coarse // LANES

    *pieces, spans, edge, places = call(
        functools.partial(rows_kernel, count),
        [(kept // GROUP, LANES)] * GROUP
        + [(2 * kept + side, width), (width + tall, width), ((order, side + width), BF16)],
        (table, condensed, eigen_loads, coarse_inverse, table),
        7.5,
        hbm=(1,),
        scratch=[
            pltpu.VMEM((kept, order), F32),
            pltpu.VMEM((order, side + width + 2 * columns), BF16),
            pltpu.SemaphoreType.DMA,
        ],
        vmem=52,
    )
    *pieces, c_next = lax.optimization_barrier((*pieces, c_next))
    pieces = traded(pieces)
    c_other = mate(jnp.concatenate([coarse_inverse, c_next], axis=0), 1)
    spans_next = mate(after(spans, pieces), 2)
    edge = after(edge, pieces)
    came = crossing(edge, [(GROUP - 1, GROUP), (0, -1), (1, -2)])
    came_next = crossing(edge, [(GROUP - 1, GROUP + 2), (0, -3), (1, -4)])
    pieces[0] = after(pieces[0], c_other)
    size = owned + chunk_of(owned)
    pay_shapes = [(size, LANES)] + [(size + width // GROUP, LANES)] * 2
    v0, *pays = call(
        functools.partial(start_kernel, groups == PAIRED),
        [(kept, LANES), *pay_shapes],
        (pos, *pieces),
        0.9,
    )
    pays = along(*pays)
    *pays, spans_next, came, came_next = lax.optimization_barrier((*pays, spans_next, came, came_next))
    theirs = mate(jnp.concatenate([spans, spans_next, came, came_next], axis=0), 1)
    blocks = call(
        functools.partial(blocks_kernel, width),
        [
            ((2 * (GROUP + 3) * owned, coarse), BF16),
            ((2 * side, GROUP * width), BF16),
            ((2 * kept, GROUP * side), BF16),
            ((side, width), BF16),
            ((side, width), BF16),
        ],
        (pos, coarse_inverse, c_next, c_other, spans, spans_next, came, came_next, theirs),
        1.7,
    )

    state = ()
    for step in range(ITERS):
        kind = "first" if step == 0 else "last" if step == ITERS - 1 else "middle"
        shapes = [(kept, LANES), (width, LANES), (width, LANES), *pay_shapes]
        if kind == "last":
            shapes = [((count + 3 * width) // GROUP, LANES)] * GROUP
        outs = call(
            functools.partial(turn_kernel, kind, groups),
            shapes,
            (pos, *pays, *blocks, v0, *state),
            2.8,
            scratch=[pltpu.VMEM((groups, size, LANES), F32), pltpu.VMEM((coarse, 2 * LANES), BF16)],
        )
        if kind != "last":
            state = outs[:3]
            pays = along(*outs[3:])
    displaced, multipliers = call(
        functools.partial(final_kernel, count),
        [(order, columns), (width, columns)],
        (pos, *traded(outs), eigen_loads, places, condensed),
        5.3,
    )
    return displaced, multipliers


def solution(mesh):
    placed = (
        P(("rve", "sub"), None),
        P(("rve", "sub"), None),
        P(("rve", "sub"), None),
        P("sub", None, None),
        P("sub", None),
        P("sub", None),
    )
    return jax.shard_map(
        local,
        mesh=mesh,
        in_specs=placed,
        out_specs=(P(("rve", "sub"), None), P(("rve", "sub"), None)),
        check_vma=False,
    )
```

```python
import functools

import jax
import jax.numpy as jnp
from jax import lax
from jax.experimental import pallas as pl
from jax.experimental.pallas import tpu as pltpu
from jax.sharding import PartitionSpec as P

ITERS = 3
DAMPING = 0.5
GROUP = 4
PAIRED = 4
LANES = 128
BF16 = jnp.bfloat16
F32 = jnp.float32


def call(kernel, outs, args, micros, smem=1, hbm=(), scratch=(), vmem=24):
    in_specs = [
        pl.BlockSpec(memory_space=pltpu.SMEM if i < smem else pltpu.HBM if i in hbm else pltpu.VMEM)
        for i in range(len(args))
    ]
    shapes = [o if isinstance(o[0], tuple) else (o, F32) for o in outs]
    return pl.pallas_call(
        kernel,
        out_shape=[jax.ShapeDtypeStruct(s, d) for s, d in shapes],
        in_specs=in_specs,
        out_specs=[pl.BlockSpec(memory_space=pltpu.VMEM)] * len(shapes),
        scratch_shapes=list(scratch),
        compiler_params=pltpu.CompilerParams(vmem_limit_bytes=vmem * 1024 * 1024),
        cost_estimate=pl.CostEstimate(flops=int(micros * 1e9), bytes_accessed=0, transcendentals=0),
    )(*args)


def halves(x):
    high = x.astype(BF16)
    return high, (x - high.astype(F32)).astype(BF16)


def dot(a, b):
    return jnp.dot(a, b, preferred_element_type=F32)


def product(a, b):
    ah, al = halves(a)
    bh, bl = halves(b)
    n = b.shape[1]
    both = dot(ah, jnp.concatenate([bh, bl], axis=1))
    return both[:, :n] + both[:, n:] + dot(al, bh)


def lane_block(rows):
    return lax.broadcasted_iota(jnp.int32, (rows, LANES), 1) // (LANES // GROUP)


def turned(x, blocks):
    width = LANES // GROUP
    if isinstance(blocks, int):
        shift = (blocks % GROUP) * width
        return x if shift == 0 else pltpu.roll(x, shift, 1)
    return pltpu.roll(x, lax.rem(blocks + 2 * GROUP, GROUP) * width, 1)


def cut(x, member, out_refs):
    rows = x.shape[0] // GROUP
    block = lane_block(rows)
    parts = [x[q * rows:(q + 1) * rows] for q in range(GROUP)]
    for k, out in enumerate(out_refs):
        to = member ^ k
        packed = jnp.zeros((rows, LANES), F32)
        for q in range(GROUP):
            packed = jnp.where(block == q, turned(parts[q], q - to), packed)
        out[...] = packed


def joined(pieces, member):
    rows = pieces[0].shape[0]
    block = lane_block(rows)
    out = []
    for q in range(GROUP):
        part = jnp.zeros((rows, LANES), F32)
        for k, piece in enumerate(pieces):
            came = member ^ k
            part = jnp.where(block == came, turned(piece, came - q), part)
        out.append(part)
    return jnp.concatenate(out, axis=0)


def packed(x, chunk):
    first = lane_block(chunk) == 0
    out = None
    for q in range(x.shape[0] // chunk):
        part = turned(jnp.where(first, x[q * chunk:(q + 1) * chunk], 0.0), q)
        out = part if out is None else out + part
    return out


def unpacked(x, count):
    return jnp.concatenate([turned(x, -q) for q in range(count)], axis=0)


def chunk_of(owned):
    return -(-owned // (GROUP * 8)) * 8


def stacked(x):
    return jnp.concatenate(halves(x), axis=0)


def beside(x):
    return jnp.concatenate(halves(x), axis=1)


def combined(p, n):
    m = p.shape[0] // 2
    return p[:m, :n] + p[:m, n:] + p[m:, :n]


def payload(v, width, paired, odd, out, out_a, out_b):
    coarse = v[2 * width:]
    owned = coarse.shape[0] // 2
    below = turned(coarse[owned:], 1)
    own = coarse[:owned] + jnp.where(lane_block(owned) == 0, 0.0, below)
    rows = jnp.concatenate([own, packed(below, chunk_of(owned))], axis=0)
    size = rows.shape[0]
    for ref in (out, out_a, out_b):
        ref[:size] = rows
    up = packed(turned(v[width:2 * width], 1), width // GROUP)
    down = packed(v[:width], width // GROUP)
    if paired:
        up, down = jnp.where(odd, down, up), jnp.where(odd, up, down)
    out_a[size:] = up
    out_b[size:] = down


def fetch(source, count, rows, target, places, sem):
    def one(j, carry):
        pltpu.make_async_copy(source.at[pl.ds(rows(j), 1)], target.at[pl.ds(places(j), 1)], sem).start()
        return carry

    lax.fori_loop(0, count, one, 0, unroll=8)


def rows_kernel(count, table, k_ref, f_ref, c_ref, tablev, *rest):
    pieces, (spans, edge, right_side, ks, sems) = rest[:GROUP], rest[GROUP:]
    width, order, columns = edge.shape[1], ks.shape[1], f_ref.shape[1]
    owned = c_ref.shape[0]
    side = 2 * width
    fetch(k_ref, count, lambda j: table[2, j], ks, lambda j: side + table[3, j], sems.at[0])
    fetch(k_ref, width, lambda j: table[0, j], ks, lambda j: j, sems.at[1])
    fetch(k_ref, width, lambda j: table[1, j], ks, lambda j: width + j, sems.at[2])

    def indicator(row):
        place = lax.broadcasted_iota(jnp.int32, (order, row.shape[1]), 0).astype(F32)
        return jnp.where(place == row, 1.0, 0.0).astype(BF16)

    slots = jnp.broadcast_to(tablev[3:4, :count].astype(F32), (count, count)).T
    prims = jnp.broadcast_to(tablev[2:3, :count].astype(F32), (count, count)).T
    wanted = lax.broadcasted_iota(jnp.int32, (count, count), 1).astype(F32)
    by_slot = jnp.sum(jnp.where(slots == wanted, prims, 0.0), axis=0, keepdims=True)
    right_side[:, :width] = indicator(tablev[0:1].astype(F32))
    right_side[:, width:side] = indicator(tablev[1:2].astype(F32))
    right_side[:, side:side + count] = indicator(by_slot)
    right_side[:, side + count:side + width] = jnp.zeros((order, width - count), BF16)
    right_side[:, side + width:] = beside(f_ref[...])
    for i in range(c_ref.shape[1] // LANES):
        at = width + i * owned
        edge[at:at + owned] = c_ref[:, i * LANES:(i + 1) * LANES]

    at, rows = side + width, side + count
    v = []
    for i, (first, size) in enumerate(((side, count), (0, width), (width, width))):
        part = ks.at[first:first + size]
        pltpu.make_async_copy(k_ref.at[pl.ds(0, size)], part, sems.at[i]).wait()
        high, low = halves(part[...])
        both = dot(high, right_side[...])
        rest = dot(low, right_side[:, :at + columns])
        v.append(both[:, at:at + columns] + both[:, at + columns:] + rest[:, at:])
        block = both[:, :at] + rest[:, :at]
        spans[first:first + size] = block[:, :width]
        spans[rows + first:rows + first + size] = block[:, width:side]
        if first < side:
            spans[2 * rows + first:2 * rows + first + size] = block[:, side:]

            @pl.when((table[4, 0] == GROUP - 1) == (first > 0))
            def _():
                edge[:width] = block[:, side:]

    cut(jnp.concatenate(v[1:] + v[:1], axis=0), table[4, 0], pieces)


GOT = (-1, None, 5, 4)
GOT_NEXT = (5, 4, -1, None)


GOT = (-1, None, 5, 4)
GOT_NEXT = (5, 4, -1, None)


def blocks_kernel(width, pos, c0, c2, c_other, s0, s2, came, came_next, theirs, solver, cross, own, edge_up, edge_down):
    side, size, edge_size = 2 * width, s0.shape[0], came.shape[0]
    kept = (size - side) // 2
    owned, tall = c0.shape[0], c0.shape[1] // LANES
    half = solver.shape[0] // 2
    other, at = [], 0
    for rows in (size, size, edge_size, edge_size):
        other.append(theirs.at[at:at + rows])
        at += rows
    for k, ref in enumerate((s0, other[0], s2, other[1])):
        own[:, k * side:k * side + width] = stacked(ref[:kept])
        own[:, k * side + width:(k + 1) * side] = stacked(ref[kept:2 * kept])
        cross[:, k * width:(k + 1) * width] = stacked(ref[2 * kept:])

    def placed(block, values, columns):
        at = (block + 1) * owned
        high, low = halves(values)
        solver[at:at + owned, columns] = high
        solver[half + at:half + at + owned, columns] = low

    for m in range(GROUP):

        @pl.when(pos[0] == m)
        def _():
            p = m ^ 1
            everything = slice(None)
            placed(m, c0[...], everything)
            placed(m ^ 2, c2[...], everything)
            placed(p, c_other[:owned], everything)
            placed(p ^ 2, c_other[owned:], everything)
            held = {GOT[m]: came, GOT_NEXT[m]: came_next}
            for block, ref in zip((GOT[p], GOT_NEXT[p]), other[2:]):
                held.setdefault(block, ref)
            for block in (-1, 4, 5):
                for i in range(tall):
                    at = width + i * owned
                    placed(block, held[block][at:at + owned], slice(i * LANES, (i + 1) * LANES))
            edge_up[...] = stacked(held[-1][:width])
            edge_down[...] = stacked(held[4][:width])


def start_kernel(paired, pos, p0, p1, p2, p3, v_ref, *pays):
    v = joined([p0[...], p1[...], p2[...], p3[...]], pos[0])
    v_ref[...] = v
    payload(v, v.shape[1], paired, pos[1] % 2 == 1, *pays)


def shared(x, member):
    block = lane_block(x.shape[0])
    high, low = halves(x)
    high, low = high.astype(F32), low.astype(F32)
    out = []
    for k in range(GROUP):
        mine = block == (member ^ k)
        pair = [jnp.where(mine, half, 0.0).astype(BF16) for half in (high, low)]
        out.append(jnp.concatenate(pair, axis=1))
    return jnp.concatenate(out, axis=0)


def turn_kernel(kind, groups, pos, *refs):
    pays, (solver, cross, own, edge_up, edge_down, v0), refs = refs[:groups], refs[groups:groups + 6], refs[groups + 6:]
    if kind == "first":
        now = v0
    else:
        (now, left_ref, right_ref), refs = refs[:3], refs[3:]
    outs, (held, stack) = refs[:-2], refs[-2:]
    paired = groups == PAIRED
    member, group = pos[0], pos[1]
    width = edge_down.shape[1]
    owned = (v0.shape[0] - 2 * width) // 2
    size = owned + chunk_of(owned)
    first = lane_block(owned) == 0

    for k in range(groups):
        held[group ^ k if paired else lax.rem(group - k + groups, groups)] = pays[k][:size, :]
    for h in range(groups):
        extra = unpacked(held[(h - 1) % groups, owned:], -(-owned // chunk_of(owned)))[:owned]
        whole = held[h, :owned] + jnp.where(first, extra, 0.0)
        for i in range(GROUP):
            place = (h * GROUP + i) * owned
            stack[place:place + owned, :] = beside(turned(whole, -i))

    w = combined(dot(solver[...], stack[...]), LANES)
    pair = lane_block(2 * owned)
    q = w[owned:3 * owned]
    for i in range(1, GROUP):
        q = jnp.where(pair == i, turned(w[(i + 1) * owned:(i + 3) * owned], i), q)
    filler = jnp.zeros((width - 2 * owned, LANES), F32)

    def padded(x):
        return jnp.concatenate([x, filler], axis=0)

    faces = now[:2 * width] - combined(dot(cross[...], shared(padded(q), member)), LANES)
    left, right = faces[:width], faces[width:]
    before, after = beside(padded(w[:2 * owned])), beside(padded(w[(GROUP + 1) * owned:]))
    halo_up, halo_down = pays[1][size:, :], pays[groups - 1][size:, :]
    if paired:
        odd = group % 2 == 1
        halo_up, halo_down = jnp.where(odd, halo_up, halo_down), jnp.where(odd, halo_down, halo_up)
    right_before = unpacked(halo_up, GROUP) - combined(dot(edge_up[...], before), LANES)
    left_after = unpacked(halo_down, GROUP) - combined(dot(edge_down[...], after), LANES)
    block = lane_block(width)
    beyond = jnp.where(block == GROUP - 1, turned(left_after, GROUP - 1), turned(left, -1))
    behind = jnp.where(block == 0, right_before, turned(right, 1))
    lam_right = DAMPING * (right - beyond)
    lam_left = DAMPING * (behind - left)
    if kind != "first":
        lam_right = lam_right + right_ref[...]
        lam_left = lam_left + left_ref[...]
    if kind == "last":
        cut(jnp.concatenate([q, lam_right, left_ref[...], right_ref[...]], axis=0), member, outs)
        return
    v_ref, left_out, right_out = outs[:3]
    left_out[...] = lam_left
    right_out[...] = lam_right
    lam = jnp.concatenate([lam_left, -lam_right], axis=0)
    v = v0[...] + combined(dot(own[...], shared(lam, member)), LANES)
    v_ref[...] = v
    payload(v, width, paired, group % 2 == 1, *outs[3:])


def sweep_kernel(first, pos, right_side, k_ref, u_ref, ks_ref):
    rows, columns = u_ref.shape
    at = right_side.shape[1] - 2 * columns
    high, low = halves(k_ref[first:first + rows])
    both = dot(high, right_side[...])
    part = dot(low, right_side[:, :at + columns])
    u_ref[...] = both[:, at:at + columns] + both[:, at + columns:] + part[:, at:]
    ks_ref[...] = both[:, :at] + part[:, :at]


def final_kernel(parts, count, pos, p0, p1, p2, p3, *refs):
    x = joined([p0[...], p1[...], p2[...], p3[...]], pos[0])
    us, kss, (out, lam_ref) = refs[:parts], refs[parts:2 * parts], refs[2 * parts:]
    width = lam_ref.shape[0]
    lam_ref[...] = x[count:count + width]
    at = count + width
    filler = jnp.zeros((width - count, LANES), F32)
    change = beside(jnp.concatenate([x[at:at + width], -x[at + width:], -x[:count], filler], axis=0))
    at = 0
    for u, ks in zip(us, kss):
        high, low = halves(ks[...])
        part = dot(high, change)
        out[at:at + u.shape[0]] = u[...] + part[:, :LANES] + part[:, LANES:] + dot(low, change[:, :LANES])
        at += u.shape[0]


def local(condensed, eigen_loads, coarse_inverse, face_rows, primal_rows, primal_slot):
    order, columns = eigen_loads.shape
    owned, coarse = coarse_inverse.shape
    width = face_rows.shape[2]
    side, count = 2 * width, 2 * owned
    kept = side + count
    total = lax.axis_size("sub")
    groups = total // GROUP
    me = lax.axis_index("sub")
    pos = jnp.stack([me % GROUP, me // GROUP]).astype(jnp.int32)

    def row(x):
        return jnp.pad(x[None], ((0, 0), (0, width - x.shape[0])))

    table = jnp.concatenate([face_rows[0], row(primal_rows[0]), row(primal_slot[0]), row(pos)], axis=0)

    def mate(x, k):
        return lax.ppermute(x, "sub", [(s, s ^ k) for s in range(total)])

    def crossing(x, pairs):
        pairs = [(g * GROUP + a, (g * GROUP + b) % total) for g in range(groups) for a, b in pairs]
        return lax.ppermute(x, "sub", pairs)

    def traded(pieces):
        return [pieces[0]] + [mate(pieces[k], k) for k in range(1, GROUP)]

    def planes(x, by):
        return lax.ppermute(x, "sub", [(s, (s + by * GROUP) % total) for s in range(total)])

    def along(pay, a, b):
        if groups == PAIRED:
            last = mate(b, 3 * GROUP)
            middle = mate(pay, 2 * GROUP)
            return [pay, mate(a, GROUP), middle, last]
        return [pay, planes(a, 1)] + [planes(pay, k) for k in range(2, groups - 1)] + [planes(b, -1)]

    def after(x, other):
        return lax.optimization_barrier((x, other))[0]

    c_next = mate(coarse_inverse, 2)
    tall = owned * coarse // LANES

    *pieces, spans, edge, right_side = call(
        functools.partial(rows_kernel, count),
        [(kept // GROUP, LANES)] * GROUP
        + [(2 * kept + side, width), (width + tall, width), ((order, side + width + 2 * columns), BF16)],
        (table, condensed, eigen_loads, coarse_inverse, table),
        7.5,
        hbm=(1,),
        scratch=[
            pltpu.VMEM((kept, order), F32),
            pltpu.SemaphoreType.DMA((3,)),
        ],
        vmem=52,
    )
    *pieces, c_next = lax.optimization_barrier((*pieces, c_next))
    pieces = traded(pieces)
    c_other = mate(jnp.concatenate([coarse_inverse, c_next], axis=0), 1)
    spans_next = mate(after(spans, pieces), 2)
    edge = after(edge, pieces)
    came = crossing(edge, [(GROUP - 1, GROUP), (0, -1), (1, -2)])
    came_next = crossing(edge, [(GROUP - 1, GROUP + 2), (0, -3), (1, -4)])
    parts = 4 if order % 64 == 0 else 1
    block = order // parts
    sweeps = []

    def sweep(other):
        if len(sweeps) < parts:
            first = len(sweeps) * block
            shapes = [(block, columns), (block, side + width)]
            kernel = functools.partial(sweep_kernel, first)
            sweeps.append(call(kernel, shapes, (pos, after(right_side, other), condensed), 2.3))
            return sweeps[-1]
        return other

    pieces[0] = after(pieces[0], c_other)
    size = owned + chunk_of(owned)
    pay_shapes = [(size, LANES)] + [(size + width // GROUP, LANES)] * 2
    v0, *pays = call(
        functools.partial(start_kernel, groups == PAIRED),
        [(kept, LANES), *pay_shapes],
        (pos, *pieces),
        0.9,
    )
    swept = sweep(pays)
    pays = along(*pays)
    *pays, spans_next, came, came_next, _ = lax.optimization_barrier((*pays, spans_next, came, came_next, swept))
    theirs = mate(jnp.concatenate([spans, spans_next, came, came_next], axis=0), 1)
    pays[0] = after(pays[0], sweep((spans_next, swept)))
    blocks = call(
        functools.partial(blocks_kernel, width),
        [
            ((2 * (GROUP + 3) * owned, coarse), BF16),
            ((2 * side, GROUP * width), BF16),
            ((2 * kept, GROUP * side), BF16),
            ((side, width), BF16),
            ((side, width), BF16),
        ],
        (pos, coarse_inverse, c_next, c_other, spans, spans_next, came, came_next, theirs),
        1.7,
    )

    state = ()
    for step in range(ITERS):
        kind = "first" if step == 0 else "last" if step == ITERS - 1 else "middle"
        shapes = [(kept, LANES), (width, LANES), (width, LANES), *pay_shapes]
        if kind == "last":
            shapes = [((count + 3 * width) // GROUP, LANES)] * GROUP
        outs = call(
            functools.partial(turn_kernel, kind, groups),
            shapes,
            (pos, *pays, *blocks, v0, *state),
            2.8,
            scratch=[pltpu.VMEM((groups, size, LANES), F32), pltpu.VMEM((coarse, 2 * LANES), BF16)],
        )
        if kind != "last":
            state = outs[:3]
            swept = sweep(outs)
            pays = along(*outs[3:])
            pays[0] = after(pays[0], swept)
    displaced, multipliers = call(
        functools.partial(final_kernel, parts, count),
        [(order, columns), (width, columns)],
        (pos, *traded(outs), *[x[0] for x in sweeps], *[x[1] for x in sweeps]),
        2.6,
    )
    return displaced, multipliers


def solution(mesh):
    placed = (
        P(("rve", "sub"), None),
        P(("rve", "sub"), None),
        P(("rve", "sub"), None),
        P("sub", None, None),
        P("sub", None),
        P("sub", None),
    )
    return jax.shard_map(
        local,
        mesh=mesh,
        in_specs=placed,
        out_specs=(P(("rve", "sub"), None), P(("rve", "sub"), None)),
        check_vma=False,
    )
```

```python
import functools

import jax
import jax.numpy as jnp
from jax import lax
from jax.experimental import pallas as pl
from jax.experimental.pallas import tpu as pltpu
from jax.sharding import PartitionSpec as P

ITERS = 3
DAMPING = 0.5
GROUP = 4
PAIRED = 4
LANES = 128
BF16 = jnp.bfloat16
F32 = jnp.float32


def call(kernel, outs, args, micros, smem=1, hbm=(), scratch=(), vmem=24):
    in_specs = [
        pl.BlockSpec(memory_space=pltpu.SMEM if i < smem else pltpu.HBM if i in hbm else pltpu.VMEM)
        for i in range(len(args))
    ]
    shapes = [o if isinstance(o[0], tuple) else (o, F32) for o in outs]
    return pl.pallas_call(
        kernel,
        out_shape=[jax.ShapeDtypeStruct(s, d) for s, d in shapes],
        in_specs=in_specs,
        out_specs=[pl.BlockSpec(memory_space=pltpu.VMEM)] * len(shapes),
        scratch_shapes=list(scratch),
        compiler_params=pltpu.CompilerParams(vmem_limit_bytes=vmem * 1024 * 1024),
        cost_estimate=pl.CostEstimate(flops=int(micros * 1e9), bytes_accessed=0, transcendentals=0),
    )(*args)


def halves(x):
    high = x.astype(BF16)
    return high, (x - high.astype(F32)).astype(BF16)


def dot(a, b):
    return jnp.dot(a, b, preferred_element_type=F32)


def product(a, b):
    ah, al = halves(a)
    bh, bl = halves(b)
    n = b.shape[1]
    both = dot(ah, jnp.concatenate([bh, bl], axis=1))
    return both[:, :n] + both[:, n:] + dot(al, bh)


def lane_block(rows):
    return lax.broadcasted_iota(jnp.int32, (rows, LANES), 1) // (LANES // GROUP)


def turned(x, blocks):
    width = LANES // GROUP
    if isinstance(blocks, int):
        shift = (blocks % GROUP) * width
        return x if shift == 0 else pltpu.roll(x, shift, 1)
    return pltpu.roll(x, lax.rem(blocks + 2 * GROUP, GROUP) * width, 1)


def cut(x, member, out_refs):
    rows = x.shape[0] // GROUP
    block = lane_block(rows)
    parts = [x[q * rows:(q + 1) * rows] for q in range(GROUP)]
    for k, out in enumerate(out_refs):
        to = member ^ k
        packed = jnp.zeros((rows, LANES), F32)
        for q in range(GROUP):
            packed = jnp.where(block == q, turned(parts[q], q - to), packed)
        out[...] = packed


def joined(pieces, member):
    rows = pieces[0].shape[0]
    block = lane_block(rows)
    out = []
    for q in range(GROUP):
        part = jnp.zeros((rows, LANES), F32)
        for k, piece in enumerate(pieces):
            came = member ^ k
            part = jnp.where(block == came, turned(piece, came - q), part)
        out.append(part)
    return jnp.concatenate(out, axis=0)


def packed(x, chunk):
    first = lane_block(chunk) == 0
    out = None
    for q in range(x.shape[0] // chunk):
        part = turned(jnp.where(first, x[q * chunk:(q + 1) * chunk], 0.0), q)
        out = part if out is None else out + part
    return out


def unpacked(x, count):
    return jnp.concatenate([turned(x, -q) for q in range(count)], axis=0)


def chunk_of(owned):
    return -(-owned // (GROUP * 8)) * 8


def stacked(x):
    return jnp.concatenate(halves(x), axis=0)


def beside(x):
    return jnp.concatenate(halves(x), axis=1)


def combined(p, n):
    m = p.shape[0] // 2
    return p[:m, :n] + p[:m, n:] + p[m:, :n]


def payload(v, width, paired, odd, out, out_a, out_b):
    coarse = v[2 * width:]
    owned = coarse.shape[0] // 2
    below = turned(coarse[owned:], 1)
    own = coarse[:owned] + jnp.where(lane_block(owned) == 0, 0.0, below)
    rows = jnp.concatenate([own, packed(below, chunk_of(owned))], axis=0)
    size = rows.shape[0]
    for ref in (out, out_a, out_b):
        ref[:size] = rows
    up = packed(turned(v[width:2 * width], 1), width // GROUP)
    down = packed(v[:width], width // GROUP)
    if paired:
        up, down = jnp.where(odd, down, up), jnp.where(odd, up, down)
    out_a[size:] = up
    out_b[size:] = down


def fetch(source, count, rows, target, places, sem):
    def one(j, carry):
        pltpu.make_async_copy(source.at[pl.ds(rows(j), 1)], target.at[pl.ds(places(j), 1)], sem).start()
        return carry

    lax.fori_loop(0, count, one, 0, unroll=8)


def rows_kernel(count, table, k_ref, f_ref, *rest):
    pieces, (ks, sems) = rest[:GROUP], rest[GROUP:]
    width, columns = table.shape[1], f_ref.shape[1]
    side = 2 * width
    fetch(k_ref, width, lambda j: table[0, j], ks, lambda j: j, sems.at[0])
    fetch(k_ref, width, lambda j: table[1, j], ks, lambda j: width + j, sems.at[1])
    fetch(k_ref, count, lambda j: table[2, j], ks, lambda j: side + table[3, j], sems.at[2])
    loads = beside(f_ref[...])
    v = []
    for i, (first, size) in enumerate(((0, width), (width, width), (side, count))):
        part = ks.at[first:first + size]
        pltpu.make_async_copy(k_ref.at[pl.ds(0, size)], part, sems.at[i]).wait()
        high, low = halves(part[...])
        both = dot(high, loads)
        v.append(both[:, :columns] + both[:, columns:] + dot(low, loads[:, :columns]))
    cut(jnp.concatenate(v, axis=0), table[4, 0], pieces)


def near_kernel(count, table, ks, f_ref, c_ref, tablev, spans, edge, right_side):
    width, order, owned = table.shape[1], ks.shape[1], c_ref.shape[0]
    side = 2 * width

    def indicator(row):
        place = lax.broadcasted_iota(jnp.int32, (order, row.shape[1]), 0).astype(F32)
        return jnp.where(place == row, 1.0, 0.0).astype(BF16)

    slots = jnp.broadcast_to(tablev[3:4, :count].astype(F32), (count, count)).T
    prims = jnp.broadcast_to(tablev[2:3, :count].astype(F32), (count, count)).T
    wanted = lax.broadcasted_iota(jnp.int32, (count, count), 1).astype(F32)
    by_slot = jnp.sum(jnp.where(slots == wanted, prims, 0.0), axis=0, keepdims=True)
    right_side[:, :width] = indicator(tablev[0:1].astype(F32))
    right_side[:, width:side] = indicator(tablev[1:2].astype(F32))
    right_side[:, side:side + count] = indicator(by_slot)
    right_side[:, side + count:side + width] = jnp.zeros((order, width - count), BF16)
    right_side[:, side + width:] = beside(f_ref[...])
    for i in range(c_ref.shape[1] // LANES):
        at = width + i * owned
        edge[at:at + owned] = c_ref[:, i * LANES:(i + 1) * LANES]
    high, low = halves(ks[...])
    at, rows = side + width, side + count
    block = dot(high, right_side[:, :at]) + dot(low, right_side[:, :at])
    spans[:rows] = block[:, :width]
    spans[rows:2 * rows] = block[:, width:side]
    spans[2 * rows:] = block[:side, side:]
    edge[:width] = jnp.where(table[4, 0] == GROUP - 1, block[width:side, side:], block[:width, side:])


GOT = (-1, None, 5, 4)
GOT_NEXT = (5, 4, -1, None)


GOT = (-1, None, 5, 4)
GOT_NEXT = (5, 4, -1, None)


def blocks_kernel(width, pos, c0, c2, c_other, s0, s2, came, came_next, theirs, solver, cross, own, edge_up, edge_down):
    side, size, edge_size = 2 * width, s0.shape[0], came.shape[0]
    kept = (size - side) // 2
    owned, tall = c0.shape[0], c0.shape[1] // LANES
    half = solver.shape[0] // 2
    other, at = [], 0
    for rows in (size, size, edge_size, edge_size):
        other.append(theirs.at[at:at + rows])
        at += rows
    for k, ref in enumerate((s0, other[0], s2, other[1])):
        own[:, k * side:k * side + width] = stacked(ref[:kept])
        own[:, k * side + width:(k + 1) * side] = stacked(ref[kept:2 * kept])
        cross[:, k * width:(k + 1) * width] = stacked(ref[2 * kept:])

    def placed(block, values, columns):
        at = (block + 1) * owned
        high, low = halves(values)
        solver[at:at + owned, columns] = high
        solver[half + at:half + at + owned, columns] = low

    for m in range(GROUP):

        @pl.when(pos[0] == m)
        def _():
            p = m ^ 1
            everything = slice(None)
            placed(m, c0[...], everything)
            placed(m ^ 2, c2[...], everything)
            placed(p, c_other[:owned], everything)
            placed(p ^ 2, c_other[owned:], everything)
            held = {GOT[m]: came, GOT_NEXT[m]: came_next}
            for block, ref in zip((GOT[p], GOT_NEXT[p]), other[2:]):
                held.setdefault(block, ref)
            for block in (-1, 4, 5):
                for i in range(tall):
                    at = width + i * owned
                    placed(block, held[block][at:at + owned], slice(i * LANES, (i + 1) * LANES))
            edge_up[...] = stacked(held[-1][:width])
            edge_down[...] = stacked(held[4][:width])


def start_kernel(paired, pos, p0, p1, p2, p3, v_ref, *pays):
    v = joined([p0[...], p1[...], p2[...], p3[...]], pos[0])
    v_ref[...] = v
    payload(v, v.shape[1], paired, pos[1] % 2 == 1, *pays)


def shared(x, member):
    block = lane_block(x.shape[0])
    high, low = halves(x)
    high, low = high.astype(F32), low.astype(F32)
    out = []
    for k in range(GROUP):
        mine = block == (member ^ k)
        pair = [jnp.where(mine, half, 0.0).astype(BF16) for half in (high, low)]
        out.append(jnp.concatenate(pair, axis=1))
    return jnp.concatenate(out, axis=0)


def turn_kernel(kind, groups, pos, *refs):
    pays, (solver, cross, own, edge_up, edge_down, v0), refs = refs[:groups], refs[groups:groups + 6], refs[groups + 6:]
    if kind == "first":
        now = v0
    else:
        (now, left_ref, right_ref), refs = refs[:3], refs[3:]
    outs, (held, stack) = refs[:-2], refs[-2:]
    paired = groups == PAIRED
    member, group = pos[0], pos[1]
    width = edge_down.shape[1]
    owned = (v0.shape[0] - 2 * width) // 2
    size = owned + chunk_of(owned)
    first = lane_block(owned) == 0

    for k in range(groups):
        held[group ^ k if paired else lax.rem(group - k + groups, groups)] = pays[k][:size, :]
    for h in range(groups):
        extra = unpacked(held[(h - 1) % groups, owned:], -(-owned // chunk_of(owned)))[:owned]
        whole = held[h, :owned] + jnp.where(first, extra, 0.0)
        for i in range(GROUP):
            place = (h * GROUP + i) * owned
            stack[place:place + owned, :] = beside(turned(whole, -i))

    w = combined(dot(solver[...], stack[...]), LANES)
    pair = lane_block(2 * owned)
    q = w[owned:3 * owned]
    for i in range(1, GROUP):
        q = jnp.where(pair == i, turned(w[(i + 1) * owned:(i + 3) * owned], i), q)
    filler = jnp.zeros((width - 2 * owned, LANES), F32)

    def padded(x):
        return jnp.concatenate([x, filler], axis=0)

    faces = now[:2 * width] - combined(dot(cross[...], shared(padded(q), member)), LANES)
    left, right = faces[:width], faces[width:]
    before, after = beside(padded(w[:2 * owned])), beside(padded(w[(GROUP + 1) * owned:]))
    halo_up, halo_down = pays[1][size:, :], pays[groups - 1][size:, :]
    if paired:
        odd = group % 2 == 1
        halo_up, halo_down = jnp.where(odd, halo_up, halo_down), jnp.where(odd, halo_down, halo_up)
    right_before = unpacked(halo_up, GROUP) - combined(dot(edge_up[...], before), LANES)
    left_after = unpacked(halo_down, GROUP) - combined(dot(edge_down[...], after), LANES)
    block = lane_block(width)
    beyond = jnp.where(block == GROUP - 1, turned(left_after, GROUP - 1), turned(left, -1))
    behind = jnp.where(block == 0, right_before, turned(right, 1))
    lam_right = DAMPING * (right - beyond)
    lam_left = DAMPING * (behind - left)
    if kind != "first":
        lam_right = lam_right + right_ref[...]
        lam_left = lam_left + left_ref[...]
    if kind == "last":
        cut(jnp.concatenate([q, lam_right, left_ref[...], right_ref[...]], axis=0), member, outs)
        return
    v_ref, left_out, right_out = outs[:3]
    left_out[...] = lam_left
    right_out[...] = lam_right
    lam = jnp.concatenate([lam_left, -lam_right], axis=0)
    v = v0[...] + combined(dot(own[...], shared(lam, member)), LANES)
    v_ref[...] = v
    payload(v, width, paired, group % 2 == 1, *outs[3:])


def sweep_kernel(first, pos, right_side, k_ref, u_ref, ks_ref):
    rows, columns = u_ref.shape
    at = right_side.shape[1] - 2 * columns
    high, low = halves(k_ref[first:first + rows])
    both = dot(high, right_side[...])
    part = dot(low, right_side[:, :at + columns])
    u_ref[...] = both[:, at:at + columns] + both[:, at + columns:] + part[:, at:]
    ks_ref[...] = both[:, :at] + part[:, :at]


def final_kernel(parts, count, pos, p0, p1, p2, p3, *refs):
    x = joined([p0[...], p1[...], p2[...], p3[...]], pos[0])
    us, kss, (out, lam_ref) = refs[:parts], refs[parts:2 * parts], refs[2 * parts:]
    width = lam_ref.shape[0]
    lam_ref[...] = x[count:count + width]
    at = count + width
    filler = jnp.zeros((width - count, LANES), F32)
    change = beside(jnp.concatenate([x[at:at + width], -x[at + width:], -x[:count], filler], axis=0))
    at = 0
    for u, ks in zip(us, kss):
        high, low = halves(ks[...])
        part = dot(high, change)
        out[at:at + u.shape[0]] = u[...] + part[:, :LANES] + part[:, LANES:] + dot(low, change[:, :LANES])
        at += u.shape[0]


def local(condensed, eigen_loads, coarse_inverse, face_rows, primal_rows, primal_slot):
    order, columns = eigen_loads.shape
    owned, coarse = coarse_inverse.shape
    width = face_rows.shape[2]
    side, count = 2 * width, 2 * owned
    kept = side + count
    total = lax.axis_size("sub")
    groups = total // GROUP
    me = lax.axis_index("sub")
    pos = jnp.stack([me % GROUP, me // GROUP]).astype(jnp.int32)

    def row(x):
        return jnp.pad(x[None], ((0, 0), (0, width - x.shape[0])))

    table = jnp.concatenate([face_rows[0], row(primal_rows[0]), row(primal_slot[0]), row(pos)], axis=0)

    def mate(x, k):
        return lax.ppermute(x, "sub", [(s, s ^ k) for s in range(total)])

    def crossing(x, pairs):
        pairs = [(g * GROUP + a, (g * GROUP + b) % total) for g in range(groups) for a, b in pairs]
        return lax.ppermute(x, "sub", pairs)

    def traded(pieces):
        return [pieces[0]] + [mate(pieces[k], k) for k in range(1, GROUP)]

    def planes(x, by):
        return lax.ppermute(x, "sub", [(s, (s + by * GROUP) % total) for s in range(total)])

    def along(pay, a, b):
        if groups == PAIRED:
            last = mate(b, 3 * GROUP)
            middle = mate(pay, 2 * GROUP)
            return [pay, mate(a, GROUP), middle, last]
        return [pay, planes(a, 1)] + [planes(pay, k) for k in range(2, groups - 1)] + [planes(b, -1)]

    def after(x, other):
        return lax.optimization_barrier((x, other))[0]

    c_next = mate(coarse_inverse, 2)
    tall = owned * coarse // LANES

    *pieces, ks = call(
        functools.partial(rows_kernel, count),
        [(kept // GROUP, LANES)] * GROUP + [(kept, order)],
        (table, condensed, eigen_loads),
        5.3,
        hbm=(1,),
        scratch=[pltpu.SemaphoreType.DMA((3,))],
        vmem=50,
    )
    spans, edge, right_side = call(
        functools.partial(near_kernel, count),
        [(2 * kept + side, width), (width + tall, width), ((order, side + width + 2 * columns), BF16)],
        (table, ks, eigen_loads, coarse_inverse, table),
        2,
    )
    *pieces, c_next = lax.optimization_barrier((*pieces, c_next))
    pieces = traded(pieces)
    c_other = mate(jnp.concatenate([coarse_inverse, c_next], axis=0), 1)
    spans_next = mate(after(spans, pieces), 2)
    edge = after(edge, pieces)
    came = crossing(edge, [(GROUP - 1, GROUP), (0, -1), (1, -2)])
    came_next = crossing(edge, [(GROUP - 1, GROUP + 2), (0, -3), (1, -4)])
    parts = 4 if order % 64 == 0 else 1
    block = order // parts
    sweeps = []

    def sweep(other):
        if len(sweeps) < parts:
            first = len(sweeps) * block
            shapes = [(block, columns), (block, side + width)]
            kernel = functools.partial(sweep_kernel, first)
            sweeps.append(call(kernel, shapes, (pos, after(right_side, other), condensed), 2.3))
            return sweeps[-1]
        return other

    pieces[0] = after(pieces[0], c_other)
    size = owned + chunk_of(owned)
    pay_shapes = [(size, LANES)] + [(size + width // GROUP, LANES)] * 2
    v0, *pays = call(
        functools.partial(start_kernel, groups == PAIRED),
        [(kept, LANES), *pay_shapes],
        (pos, *pieces),
        0.9,
    )
    swept = sweep(pays)
    pays = along(*pays)
    *pays, spans_next, came, came_next, _ = lax.optimization_barrier((*pays, spans_next, came, came_next, swept))
    theirs = mate(jnp.concatenate([spans, spans_next, came, came_next], axis=0), 1)
    pays[0] = after(pays[0], sweep((spans_next, swept)))
    blocks = call(
        functools.partial(blocks_kernel, width),
        [
            ((2 * (GROUP + 3) * owned, coarse), BF16),
            ((2 * side, GROUP * width), BF16),
            ((2 * kept, GROUP * side), BF16),
            ((side, width), BF16),
            ((side, width), BF16),
        ],
        (pos, coarse_inverse, c_next, c_other, spans, spans_next, came, came_next, theirs),
        1.7,
    )

    state = ()
    for step in range(ITERS):
        kind = "first" if step == 0 else "last" if step == ITERS - 1 else "middle"
        shapes = [(kept, LANES), (width, LANES), (width, LANES), *pay_shapes]
        if kind == "last":
            shapes = [((count + 3 * width) // GROUP, LANES)] * GROUP
        outs = call(
            functools.partial(turn_kernel, kind, groups),
            shapes,
            (pos, *pays, *blocks, v0, *state),
            2.8,
            scratch=[pltpu.VMEM((groups, size, LANES), F32), pltpu.VMEM((coarse, 2 * LANES), BF16)],
        )
        if kind != "last":
            state = outs[:3]
            swept = sweep(outs)
            pays = along(*outs[3:])
            pays[0] = after(pays[0], swept)
    displaced, multipliers = call(
        functools.partial(final_kernel, parts, count),
        [(order, columns), (width, columns)],
        (pos, *traded(outs), *[x[0] for x in sweeps], *[x[1] for x in sweeps]),
        2.6,
    )
    return displaced, multipliers


def solution(mesh):
    placed = (
        P(("rve", "sub"), None),
        P(("rve", "sub"), None),
        P(("rve", "sub"), None),
        P("sub", None, None),
        P("sub", None),
        P("sub", None),
    )
    return jax.shard_map(
        local,
        mesh=mesh,
        in_specs=placed,
        out_specs=(P(("rve", "sub"), None), P(("rve", "sub"), None)),
        check_vma=False,
    )
```

```python
import functools

import jax
import jax.numpy as jnp
from jax import lax
from jax.experimental import pallas as pl
from jax.experimental.pallas import tpu as pltpu
from jax.sharding import PartitionSpec as P

ITERS = 3
DAMPING = 0.5
GROUP = 4
PAIRED = 4
LANES = 128
BF16 = jnp.bfloat16
F32 = jnp.float32


def call(kernel, outs, args, micros, smem=1, hbm=(), scratch=(), vmem=24):
    in_specs = [
        pl.BlockSpec(memory_space=pltpu.SMEM if i < smem else pltpu.HBM if i in hbm else pltpu.VMEM)
        for i in range(len(args))
    ]
    shapes = [o if isinstance(o[0], tuple) else (o, F32) for o in outs]
    return pl.pallas_call(
        kernel,
        out_shape=[jax.ShapeDtypeStruct(s, d) for s, d in shapes],
        in_specs=in_specs,
        out_specs=[pl.BlockSpec(memory_space=pltpu.VMEM)] * len(shapes),
        scratch_shapes=list(scratch),
        compiler_params=pltpu.CompilerParams(vmem_limit_bytes=vmem * 1024 * 1024),
        cost_estimate=pl.CostEstimate(flops=int(micros * 1e9), bytes_accessed=0, transcendentals=0),
    )(*args)


def halves(x):
    high = x.astype(BF16)
    return high, (x - high.astype(F32)).astype(BF16)


def dot(a, b):
    return jnp.dot(a, b, preferred_element_type=F32)


def product(a, b):
    ah, al = halves(a)
    bh, bl = halves(b)
    n = b.shape[1]
    both = dot(ah, jnp.concatenate([bh, bl], axis=1))
    return both[:, :n] + both[:, n:] + dot(al, bh)


def lane_block(rows):
    return lax.broadcasted_iota(jnp.int32, (rows, LANES), 1) // (LANES // GROUP)


def turned(x, blocks):
    width = LANES // GROUP
    if isinstance(blocks, int):
        shift = (blocks % GROUP) * width
        return x if shift == 0 else pltpu.roll(x, shift, 1)
    return pltpu.roll(x, lax.rem(blocks + 2 * GROUP, GROUP) * width, 1)


def cut(x, member, out_refs):
    rows = x.shape[0] // GROUP
    block = lane_block(rows)
    parts = [x[q * rows:(q + 1) * rows] for q in range(GROUP)]
    for k, out in enumerate(out_refs):
        to = member ^ k
        packed = jnp.zeros((rows, LANES), F32)
        for q in range(GROUP):
            packed = jnp.where(block == q, turned(parts[q], q - to), packed)
        out[...] = packed


def joined(pieces, member):
    rows = pieces[0].shape[0]
    block = lane_block(rows)
    out = []
    for q in range(GROUP):
        part = jnp.zeros((rows, LANES), F32)
        for k, piece in enumerate(pieces):
            came = member ^ k
            part = jnp.where(block == came, turned(piece, came - q), part)
        out.append(part)
    return jnp.concatenate(out, axis=0)


def packed(x, chunk):
    first = lane_block(chunk) == 0
    out = None
    for q in range(x.shape[0] // chunk):
        part = turned(jnp.where(first, x[q * chunk:(q + 1) * chunk], 0.0), q)
        out = part if out is None else out + part
    return out


def unpacked(x, count):
    return jnp.concatenate([turned(x, -q) for q in range(count)], axis=0)


def chunk_of(owned):
    return -(-owned // (GROUP * 8)) * 8


def stacked(x):
    return jnp.concatenate(halves(x), axis=0)


def beside(x):
    return jnp.concatenate(halves(x), axis=1)


def combined(p, n):
    m = p.shape[0] // 2
    return p[:m, :n] + p[:m, n:] + p[m:, :n]


def payload(v, width, paired, odd, out, out_a, out_b):
    coarse = v[2 * width:]
    owned = coarse.shape[0] // 2
    below = turned(coarse[owned:], 1)
    own = coarse[:owned] + jnp.where(lane_block(owned) == 0, 0.0, below)
    rows = jnp.concatenate([own, packed(below, chunk_of(owned))], axis=0)
    size = rows.shape[0]
    for ref in (out, out_a, out_b):
        ref[:size] = rows
    up = packed(turned(v[width:2 * width], 1), width // GROUP)
    down = packed(v[:width], width // GROUP)
    if paired:
        up, down = jnp.where(odd, down, up), jnp.where(odd, up, down)
    out_a[size:] = up
    out_b[size:] = down


def fetch(source, count, rows, target, places, sem):
    def one(j, carry):
        pltpu.make_async_copy(source.at[pl.ds(rows(j), 1)], target.at[pl.ds(places(j), 1)], sem).start()
        return carry

    lax.fori_loop(0, count, one, 0, unroll=8)


def rows_kernel(count, table, k_ref, f_ref, *rest):
    pieces, (ks, sems) = rest[:GROUP], rest[GROUP:]
    width, columns = table.shape[1], f_ref.shape[1]
    side = 2 * width
    fetch(k_ref, width, lambda j: table[0, j], ks, lambda j: j, sems.at[0])
    fetch(k_ref, width, lambda j: table[1, j], ks, lambda j: width + j, sems.at[1])
    fetch(k_ref, count, lambda j: table[2, j], ks, lambda j: side + table[3, j], sems.at[2])
    loads = beside(f_ref[...])
    v = []
    for i, (first, size) in enumerate(((0, width), (width, width), (side, count))):
        part = ks.at[first:first + size]
        pltpu.make_async_copy(k_ref.at[pl.ds(0, size)], part, sems.at[i]).wait()
        high, low = halves(part[...])
        both = dot(high, loads)
        v.append(both[:, :columns] + both[:, columns:] + dot(low, loads[:, :columns]))
    cut(jnp.concatenate(v, axis=0), table[4, 0], pieces)


def near_kernel(count, table, ks, f_ref, c_ref, tablev, spans, edge, right_side):
    width, order, owned = table.shape[1], ks.shape[1], c_ref.shape[0]
    side = 2 * width

    def indicator(row):
        place = lax.broadcasted_iota(jnp.int32, (order, row.shape[1]), 0).astype(F32)
        return jnp.where(place == row, 1.0, 0.0).astype(BF16)

    slots = jnp.broadcast_to(tablev[3:4, :count].astype(F32), (count, count)).T
    prims = jnp.broadcast_to(tablev[2:3, :count].astype(F32), (count, count)).T
    wanted = lax.broadcasted_iota(jnp.int32, (count, count), 1).astype(F32)
    by_slot = jnp.sum(jnp.where(slots == wanted, prims, 0.0), axis=0, keepdims=True)
    right_side[:, :width] = indicator(tablev[0:1].astype(F32))
    right_side[:, width:side] = indicator(tablev[1:2].astype(F32))
    right_side[:, side:side + count] = indicator(by_slot)
    right_side[:, side + count:side + width] = jnp.zeros((order, width - count), BF16)
    right_side[:, side + width:] = beside(f_ref[...])
    for i in range(c_ref.shape[1] // LANES):
        at = width + i * owned
        edge[at:at + owned] = c_ref[:, i * LANES:(i + 1) * LANES]
    high, low = halves(ks[...])
    at, rows = side + width, side + count
    block = dot(high, right_side[:, :at]) + dot(low, right_side[:, :at])
    spans[:rows] = block[:, :width]
    spans[rows:2 * rows] = block[:, width:side]
    spans[2 * rows:] = block[:side, side:]
    edge[:width] = jnp.where(table[4, 0] == GROUP - 1, block[width:side, side:], block[:width, side:])


GOT = (-1, None, 5, 4)
GOT_NEXT = (5, 4, -1, None)


GOT = (-1, None, 5, 4)
GOT_NEXT = (5, 4, -1, None)


def blocks_kernel(width, pos, c0, c2, c_other, s0, s2, came, came_next, theirs, solver, cross, own, edge_up, edge_down):
    side, size, edge_size = 2 * width, s0.shape[0], came.shape[0]
    kept = (size - side) // 2
    owned, tall = c0.shape[0], c0.shape[1] // LANES
    half = solver.shape[0] // 2
    other, at = [], 0
    for rows in (size, size, edge_size, edge_size):
        other.append(theirs.at[at:at + rows])
        at += rows
    for k, ref in enumerate((s0, other[0], s2, other[1])):
        own[:, k * side:k * side + width] = stacked(ref[:kept])
        own[:, k * side + width:(k + 1) * side] = stacked(ref[kept:2 * kept])
        cross[:, k * width:(k + 1) * width] = stacked(ref[2 * kept:])

    def placed(block, values, columns):
        at = (block + 1) * owned
        high, low = halves(values)
        solver[at:at + owned, columns] = high
        solver[half + at:half + at + owned, columns] = low

    for m in range(GROUP):

        @pl.when(pos[0] == m)
        def _():
            p = m ^ 1
            everything = slice(None)
            placed(m, c0[...], everything)
            placed(m ^ 2, c2[...], everything)
            placed(p, c_other[:owned], everything)
            placed(p ^ 2, c_other[owned:], everything)
            held = {GOT[m]: came, GOT_NEXT[m]: came_next}
            for block, ref in zip((GOT[p], GOT_NEXT[p]), other[2:]):
                held.setdefault(block, ref)
            for block in (-1, 4, 5):
                for i in range(tall):
                    at = width + i * owned
                    placed(block, held[block][at:at + owned], slice(i * LANES, (i + 1) * LANES))
            edge_up[...] = stacked(held[-1][:width])
            edge_down[...] = stacked(held[4][:width])


def start_kernel(paired, pos, p0, p1, p2, p3, v_ref, *pays):
    v = joined([p0[...], p1[...], p2[...], p3[...]], pos[0])
    v_ref[...] = v
    payload(v, v.shape[1], paired, pos[1] % 2 == 1, *pays)


def shared(x, member):
    block = lane_block(x.shape[0])
    high, low = halves(x)
    high, low = high.astype(F32), low.astype(F32)
    out = []
    for k in range(GROUP):
        mine = block == (member ^ k)
        pair = [jnp.where(mine, half, 0.0).astype(BF16) for half in (high, low)]
        out.append(jnp.concatenate(pair, axis=1))
    return jnp.concatenate(out, axis=0)


def turn_kernel(kind, groups, pos, *refs):
    pays, (solver, cross, own, edge_up, edge_down, v0), refs = refs[:groups], refs[groups:groups + 6], refs[groups + 6:]
    if kind == "first":
        now = v0
    else:
        (now, left_ref, right_ref), refs = refs[:3], refs[3:]
    outs, (held, stack) = refs[:-2], refs[-2:]
    paired = groups == PAIRED
    member, group = pos[0], pos[1]
    width = edge_down.shape[1]
    owned = (v0.shape[0] - 2 * width) // 2
    size = owned + chunk_of(owned)
    first = lane_block(owned) == 0

    for k in range(groups):
        held[group ^ k if paired else lax.rem(group - k + groups, groups)] = pays[k][:size, :]
    for h in range(groups):
        extra = unpacked(held[(h - 1) % groups, owned:], -(-owned // chunk_of(owned)))[:owned]
        whole = held[h, :owned] + jnp.where(first, extra, 0.0)
        for i in range(GROUP):
            place = (h * GROUP + i) * owned
            stack[place:place + owned, :] = beside(turned(whole, -i))

    w = combined(dot(solver[...], stack[...]), LANES)
    pair = lane_block(2 * owned)
    q = w[owned:3 * owned]
    for i in range(1, GROUP):
        q = jnp.where(pair == i, turned(w[(i + 1) * owned:(i + 3) * owned], i), q)
    filler = jnp.zeros((width - 2 * owned, LANES), F32)

    def padded(x):
        return jnp.concatenate([x, filler], axis=0)

    faces = now[:2 * width] - combined(dot(cross[...], shared(padded(q), member)), LANES)
    left, right = faces[:width], faces[width:]
    before, after = beside(padded(w[:2 * owned])), beside(padded(w[(GROUP + 1) * owned:]))
    halo_up, halo_down = pays[1][size:, :], pays[groups - 1][size:, :]
    if paired:
        odd = group % 2 == 1
        halo_up, halo_down = jnp.where(odd, halo_up, halo_down), jnp.where(odd, halo_down, halo_up)
    right_before = unpacked(halo_up, GROUP) - combined(dot(edge_up[...], before), LANES)
    left_after = unpacked(halo_down, GROUP) - combined(dot(edge_down[...], after), LANES)
    block = lane_block(width)
    beyond = jnp.where(block == GROUP - 1, turned(left_after, GROUP - 1), turned(left, -1))
    behind = jnp.where(block == 0, right_before, turned(right, 1))
    lam_right = DAMPING * (right - beyond)
    lam_left = DAMPING * (behind - left)
    if kind != "first":
        lam_right = lam_right + right_ref[...]
        lam_left = lam_left + left_ref[...]
    if kind == "last":
        cut(jnp.concatenate([q, lam_right], axis=0), member, outs)
        return
    v_ref, left_out, right_out = outs[:3]
    left_out[...] = lam_left
    right_out[...] = lam_right
    lam = jnp.concatenate([lam_left, -lam_right], axis=0)
    v = v0[...] + combined(dot(own[...], shared(lam, member)), LANES)
    v_ref[...] = v
    payload(v, width, paired, group % 2 == 1, *outs[3:6])
    if kind == "middle":
        cut(jnp.concatenate([lam_left, -lam_right], axis=0), member, outs[6:])


def sweep_kernel(first, pos, right_side, k_ref, u_ref, ks_ref):
    rows, columns = u_ref.shape
    at = right_side.shape[1] - 2 * columns
    high, low = halves(k_ref[first:first + rows])
    both = dot(high, right_side[...])
    part = dot(low, right_side[:, :at + columns])
    u_ref[...] = both[:, at:at + columns] + both[:, at + columns:] + part[:, at:]
    ks_ref[...] = both[:, :at] + part[:, :at]


def changed(u, ks, change):
    high, low = halves(ks)
    part = dot(high, change)
    return u + part[:, :LANES] + part[:, LANES:] + dot(low, change[:, :LANES])


def spread_kernel(parts, pos, p0, p1, p2, p3, *refs):
    lam = joined([p0[...], p1[...], p2[...], p3[...]], pos[0])
    us, kss, out = refs[:parts], refs[parts:2 * parts], refs[2 * parts]
    side, at = lam.shape[0], 0
    lam = beside(lam)
    for u, ks in zip(us, kss):
        out[at:at + u.shape[0]] = changed(u[...], ks[:, :side], lam)
        at += u.shape[0]


def final_kernel(parts, count, pos, p0, p1, p2, p3, u_ref, *refs):
    x = joined([p0[...], p1[...], p2[...], p3[...]], pos[0])
    kss, (out, lam_ref) = refs[:parts], refs[parts:]
    width = lam_ref.shape[0]
    lam_ref[...] = x[count:]
    change = beside(jnp.concatenate([-x[:count], jnp.zeros((width - count, LANES), F32)], axis=0))
    at = 0
    for ks in kss:
        rows = slice(at, at + ks.shape[0])
        out[rows] = changed(u_ref[rows], ks[:, 2 * width:], change)
        at += ks.shape[0]


def local(condensed, eigen_loads, coarse_inverse, face_rows, primal_rows, primal_slot):
    order, columns = eigen_loads.shape
    owned, coarse = coarse_inverse.shape
    width = face_rows.shape[2]
    side, count = 2 * width, 2 * owned
    kept = side + count
    total = lax.axis_size("sub")
    groups = total // GROUP
    me = lax.axis_index("sub")
    pos = jnp.stack([me % GROUP, me // GROUP]).astype(jnp.int32)

    def row(x):
        return jnp.pad(x[None], ((0, 0), (0, width - x.shape[0])))

    table = jnp.concatenate([face_rows[0], row(primal_rows[0]), row(primal_slot[0]), row(pos)], axis=0)

    def mate(x, k):
        return lax.ppermute(x, "sub", [(s, s ^ k) for s in range(total)])

    def crossing(x, pairs):
        pairs = [(g * GROUP + a, (g * GROUP + b) % total) for g in range(groups) for a, b in pairs]
        return lax.ppermute(x, "sub", pairs)

    def traded(pieces):
        return [pieces[0]] + [mate(pieces[k], k) for k in range(1, GROUP)]

    def planes(x, by):
        return lax.ppermute(x, "sub", [(s, (s + by * GROUP) % total) for s in range(total)])

    def along(pay, a, b):
        if groups == PAIRED:
            last = mate(b, 3 * GROUP)
            middle = mate(pay, 2 * GROUP)
            return [pay, mate(a, GROUP), middle, last]
        return [pay, planes(a, 1)] + [planes(pay, k) for k in range(2, groups - 1)] + [planes(b, -1)]

    def after(x, other):
        return lax.optimization_barrier((x, other))[0]

    c_next = mate(coarse_inverse, 2)
    tall = owned * coarse // LANES

    *pieces, ks = call(
        functools.partial(rows_kernel, count),
        [(kept // GROUP, LANES)] * GROUP + [(kept, order)],
        (table, condensed, eigen_loads),
        5.3,
        hbm=(1,),
        scratch=[pltpu.SemaphoreType.DMA((3,))],
        vmem=50,
    )
    spans, edge, right_side = call(
        functools.partial(near_kernel, count),
        [(2 * kept + side, width), (width + tall, width), ((order, side + width + 2 * columns), BF16)],
        (table, ks, eigen_loads, coarse_inverse, table),
        2,
    )
    *pieces, c_next = lax.optimization_barrier((*pieces, c_next))
    pieces = traded(pieces)
    c_other = mate(jnp.concatenate([coarse_inverse, c_next], axis=0), 1)
    spans_next = mate(after(spans, pieces), 2)
    edge = after(edge, pieces)
    came = crossing(edge, [(GROUP - 1, GROUP), (0, -1), (1, -2)])
    came_next = crossing(edge, [(GROUP - 1, GROUP + 2), (0, -3), (1, -4)])
    parts = 4 if order % 64 == 0 else 1
    block = order // parts
    sweeps = []

    def sweep(other):
        if len(sweeps) < parts:
            first = len(sweeps) * block
            shapes = [(block, columns), (block, side + width)]
            kernel = functools.partial(sweep_kernel, first)
            sweeps.append(call(kernel, shapes, (pos, after(right_side, other), condensed), 2.3))
            return sweeps[-1]
        return other

    pieces[0] = after(pieces[0], c_other)
    size = owned + chunk_of(owned)
    pay_shapes = [(size, LANES)] + [(size + width // GROUP, LANES)] * 2
    v0, *pays = call(
        functools.partial(start_kernel, groups == PAIRED),
        [(kept, LANES), *pay_shapes],
        (pos, *pieces),
        0.9,
    )
    swept = sweep(pays)
    pays = along(*pays)
    *pays, spans_next, came, came_next, _ = lax.optimization_barrier((*pays, spans_next, came, came_next, swept))
    theirs = mate(jnp.concatenate([spans, spans_next, came, came_next], axis=0), 1)
    pays[0] = after(pays[0], sweep((spans_next, swept)))
    blocks = call(
        functools.partial(blocks_kernel, width),
        [
            ((2 * (GROUP + 3) * owned, coarse), BF16),
            ((2 * side, GROUP * width), BF16),
            ((2 * kept, GROUP * side), BF16),
            ((side, width), BF16),
            ((side, width), BF16),
        ],
        (pos, coarse_inverse, c_next, c_other, spans, spans_next, came, came_next, theirs),
        1.7,
    )

    state = ()
    for step in range(ITERS):
        kind = "first" if step == 0 else "last" if step == ITERS - 1 else "middle"
        shapes = [(kept, LANES), (width, LANES), (width, LANES), *pay_shapes]
        if kind == "middle":
            shapes = shapes + [(side // GROUP, LANES)] * GROUP
        if kind == "last":
            shapes = [((count + width) // GROUP, LANES)] * GROUP
        outs = call(
            functools.partial(turn_kernel, kind, groups),
            shapes,
            (pos, *pays, *blocks, v0, *state),
            2.8,
            scratch=[pltpu.VMEM((groups, size, LANES), F32), pltpu.VMEM((coarse, 2 * LANES), BF16)],
        )
        if kind != "last":
            state = outs[:3]
            swept = sweep(outs)
            pays = along(*outs[3:6])
            pays[0] = after(pays[0], swept)
        if kind == "middle":
            lam_pieces = traded(after(outs[6:], swept))
    us, kss = [x[0] for x in sweeps], [x[1] for x in sweeps]
    traded_back = traded(outs)
    (spread,) = call(
        functools.partial(spread_kernel, parts),
        [(order, columns)],
        (pos, *after(lam_pieces, outs), *us, *kss),
        1.3,
    )
    displaced, multipliers = call(
        functools.partial(final_kernel, parts, count),
        [(order, columns), (width, columns)],
        (pos, *traded_back, spread, *kss),
        2,
    )
    return displaced, multipliers


def solution(mesh):
    placed = (
        P(("rve", "sub"), None),
        P(("rve", "sub"), None),
        P(("rve", "sub"), None),
        P("sub", None, None),
        P("sub", None),
        P("sub", None),
    )
    return jax.shard_map(
        local,
        mesh=mesh,
        in_specs=placed,
        out_specs=(P(("rve", "sub"), None), P(("rve", "sub"), None)),
        check_vma=False,
    )
```

```python
import functools

import jax
import jax.numpy as jnp
from jax import lax
from jax.experimental import pallas as pl
from jax.experimental.pallas import tpu as pltpu
from jax.sharding import PartitionSpec as P

ITERS = 3
DAMPING = 0.5
GROUP = 4
PAIRED = 4
LANES = 128
BF16 = jnp.bfloat16
F32 = jnp.float32


def call(kernel, outs, args, micros, smem=1, hbm=(), scratch=(), vmem=24):
    in_specs = [
        pl.BlockSpec(memory_space=pltpu.SMEM if i < smem else pltpu.HBM if i in hbm else pltpu.VMEM)
        for i in range(len(args))
    ]
    shapes = [o if isinstance(o[0], tuple) else (o, F32) for o in outs]
    return pl.pallas_call(
        kernel,
        out_shape=[jax.ShapeDtypeStruct(s, d) for s, d in shapes],
        in_specs=in_specs,
        out_specs=[pl.BlockSpec(memory_space=pltpu.VMEM)] * len(shapes),
        scratch_shapes=list(scratch),
        compiler_params=pltpu.CompilerParams(vmem_limit_bytes=vmem * 1024 * 1024),
        cost_estimate=pl.CostEstimate(flops=int(micros * 1e9), bytes_accessed=0, transcendentals=0),
    )(*args)


def halves(x):
    high = x.astype(BF16)
    return high, (x - high.astype(F32)).astype(BF16)


def dot(a, b):
    return jnp.dot(a, b, preferred_element_type=F32)


def product(a, b):
    ah, al = halves(a)
    bh, bl = halves(b)
    n = b.shape[1]
    both = dot(ah, jnp.concatenate([bh, bl], axis=1))
    return both[:, :n] + both[:, n:] + dot(al, bh)


def lane_block(rows):
    return lax.broadcasted_iota(jnp.int32, (rows, LANES), 1) // (LANES // GROUP)


def turned(x, blocks):
    width = LANES // GROUP
    if isinstance(blocks, int):
        shift = (blocks % GROUP) * width
        return x if shift == 0 else pltpu.roll(x, shift, 1)
    return pltpu.roll(x, lax.rem(blocks + 2 * GROUP, GROUP) * width, 1)


def cut(x, member, out_refs):
    rows = x.shape[0] // GROUP
    block = lane_block(rows)
    parts = [x[q * rows:(q + 1) * rows] for q in range(GROUP)]
    for k, out in enumerate(out_refs):
        to = member ^ k
        packed = jnp.zeros((rows, LANES), F32)
        for q in range(GROUP):
            packed = jnp.where(block == q, turned(parts[q], q - to), packed)
        out[...] = packed


def joined(pieces, member):
    rows = pieces[0].shape[0]
    block = lane_block(rows)
    out = []
    for q in range(GROUP):
        part = jnp.zeros((rows, LANES), F32)
        for k, piece in enumerate(pieces):
            came = member ^ k
            part = jnp.where(block == came, turned(piece, came - q), part)
        out.append(part)
    return jnp.concatenate(out, axis=0)


def packed(x, chunk):
    first = lane_block(chunk) == 0
    out = None
    for q in range(x.shape[0] // chunk):
        part = turned(jnp.where(first, x[q * chunk:(q + 1) * chunk], 0.0), q)
        out = part if out is None else out + part
    return out


def unpacked(x, count):
    return jnp.concatenate([turned(x, -q) for q in range(count)], axis=0)


def chunk_of(owned):
    return -(-owned // (GROUP * 8)) * 8


def stacked(x):
    return jnp.concatenate(halves(x), axis=0)


def beside(x):
    return jnp.concatenate(halves(x), axis=1)


def combined(p, n):
    m = p.shape[0] // 2
    return p[:m, :n] + p[:m, n:] + p[m:, :n]


def payload(v, width, paired, odd, out, out_a, out_b):
    coarse = v[2 * width:]
    owned = coarse.shape[0] // 2
    below = turned(coarse[owned:], 1)
    own = coarse[:owned] + jnp.where(lane_block(owned) == 0, 0.0, below)
    rows = jnp.concatenate([own, packed(below, chunk_of(owned))], axis=0)
    size = rows.shape[0]
    for ref in (out, out_a, out_b):
        ref[:size] = rows
    up = packed(turned(v[width:2 * width], 1), width // GROUP)
    down = packed(v[:width], width // GROUP)
    if paired:
        up, down = jnp.where(odd, down, up), jnp.where(odd, up, down)
    out_a[size:] = up
    out_b[size:] = down


def fetch(source, count, rows, target, places, sem):
    def one(j, carry):
        pltpu.make_async_copy(source.at[pl.ds(rows(j), 1)], target.at[pl.ds(places(j), 1)], sem).start()
        return carry

    lax.fori_loop(0, count, one, 0, unroll=8)


def rows_kernel(count, table, k_ref, f_ref, *rest):
    pieces, (ks, sems) = rest[:GROUP], rest[GROUP:]
    width, columns = table.shape[1], f_ref.shape[1]
    side = 2 * width
    fetch(k_ref, width, lambda j: table[0, j], ks, lambda j: j, sems.at[0])
    fetch(k_ref, width, lambda j: table[1, j], ks, lambda j: width + j, sems.at[1])
    fetch(k_ref, count, lambda j: table[2, j], ks, lambda j: side + table[3, j], sems.at[2])
    loads = beside(f_ref[...])
    v = []
    for i, (first, size) in enumerate(((0, width), (width, width), (side, count))):
        part = ks.at[first:first + size]
        pltpu.make_async_copy(k_ref.at[pl.ds(0, size)], part, sems.at[i]).wait()
        high, low = halves(part[...])
        both = dot(high, loads)
        v.append(both[:, :columns] + both[:, columns:] + dot(low, loads[:, :columns]))
    cut(jnp.concatenate(v, axis=0), table[4, 0], pieces)


def near_kernel(count, table, ks, f_ref, c_ref, tablev, spans, edge, right_side):
    width, order, owned = table.shape[1], ks.shape[1], c_ref.shape[0]
    side = 2 * width

    def indicator(row):
        place = lax.broadcasted_iota(jnp.int32, (order, row.shape[1]), 0).astype(F32)
        return jnp.where(place == row, 1.0, 0.0).astype(BF16)

    slots = jnp.broadcast_to(tablev[3:4, :count].astype(F32), (count, count)).T
    prims = jnp.broadcast_to(tablev[2:3, :count].astype(F32), (count, count)).T
    wanted = lax.broadcasted_iota(jnp.int32, (count, count), 1).astype(F32)
    by_slot = jnp.sum(jnp.where(slots == wanted, prims, 0.0), axis=0, keepdims=True)
    right_side[:, :width] = indicator(tablev[0:1].astype(F32))
    right_side[:, width:side] = indicator(tablev[1:2].astype(F32))
    right_side[:, side:side + count] = indicator(by_slot)
    right_side[:, side + count:side + width] = jnp.zeros((order, width - count), BF16)
    right_side[:, side + width:] = beside(f_ref[...])
    for i in range(c_ref.shape[1] // LANES):
        at = width + i * owned
        edge[at:at + owned] = c_ref[:, i * LANES:(i + 1) * LANES]
    high, low = halves(ks[...])
    at, rows = side + width, side + count
    block = dot(high, right_side[:, :at]) + dot(low, right_side[:, :at])
    spans[:rows] = block[:, :width]
    spans[rows:2 * rows] = block[:, width:side]
    spans[2 * rows:] = block[:side, side:]
    edge[:width] = jnp.where(table[4, 0] == GROUP - 1, block[width:side, side:], block[:width, side:])


GOT = (-1, None, 5, 4)
GOT_NEXT = (5, 4, -1, None)


GOT = (-1, None, 5, 4)
GOT_NEXT = (5, 4, -1, None)


def blocks_kernel(width, pos, c0, c2, c_other, s0, s1, s2, came, came_next, theirs, solver, cross, own, edge_up, edge_down):
    side, size, edge_size = 2 * width, s0.shape[0], came.shape[0]
    kept = (size - side) // 2
    owned, tall = c0.shape[0], c0.shape[1] // LANES
    half = solver.shape[0] // 2
    other, at = [], 0
    for rows in (size, edge_size, edge_size):
        other.append(theirs.at[at:at + rows])
        at += rows
    for k, ref in enumerate((s0, s1, s2, other[0])):
        own[:, k * side:k * side + width] = stacked(ref[:kept])
        own[:, k * side + width:(k + 1) * side] = stacked(ref[kept:2 * kept])
        cross[:, k * width:(k + 1) * width] = stacked(ref[2 * kept:])

    def placed(block, values, columns):
        at = (block + 1) * owned
        high, low = halves(values)
        solver[at:at + owned, columns] = high
        solver[half + at:half + at + owned, columns] = low

    for m in range(GROUP):

        @pl.when(pos[0] == m)
        def _():
            p = m ^ 1
            everything = slice(None)
            placed(m, c0[...], everything)
            placed(m ^ 2, c2[...], everything)
            placed(p, c_other[:owned], everything)
            placed(p ^ 2, c_other[owned:], everything)
            held = {GOT[m]: came, GOT_NEXT[m]: came_next}
            for block, ref in zip((GOT[p], GOT_NEXT[p]), other[1:]):
                held.setdefault(block, ref)
            for block in (-1, 4, 5):
                for i in range(tall):
                    at = width + i * owned
                    placed(block, held[block][at:at + owned], slice(i * LANES, (i + 1) * LANES))
            edge_up[...] = stacked(held[-1][:width])
            edge_down[...] = stacked(held[4][:width])


def start_kernel(paired, pos, p0, p1, p2, p3, v_ref, *pays):
    v = joined([p0[...], p1[...], p2[...], p3[...]], pos[0])
    v_ref[...] = v
    payload(v, v.shape[1], paired, pos[1] % 2 == 1, *pays)


def shared(x, member):
    block = lane_block(x.shape[0])
    high, low = halves(x)
    high, low = high.astype(F32), low.astype(F32)
    out = []
    for k in range(GROUP):
        mine = block == (member ^ k)
        pair = [jnp.where(mine, half, 0.0).astype(BF16) for half in (high, low)]
        out.append(jnp.concatenate(pair, axis=1))
    return jnp.concatenate(out, axis=0)


def turn_kernel(kind, groups, pos, *refs):
    pays, (solver, cross, own, edge_up, edge_down, v0), refs = refs[:groups], refs[groups:groups + 6], refs[groups + 6:]
    if kind == "first":
        now = v0
    else:
        (now, left_ref, right_ref), refs = refs[:3], refs[3:]
    outs, (held, stack) = refs[:-2], refs[-2:]
    paired = groups == PAIRED
    member, group = pos[0], pos[1]
    width = edge_down.shape[1]
    owned = (v0.shape[0] - 2 * width) // 2
    size = owned + chunk_of(owned)
    first = lane_block(owned) == 0

    for k in range(groups):
        held[group ^ k if paired else lax.rem(group - k + groups, groups)] = pays[k][:size, :]
    for h in range(groups):
        extra = unpacked(held[(h - 1) % groups, owned:], -(-owned // chunk_of(owned)))[:owned]
        whole = held[h, :owned] + jnp.where(first, extra, 0.0)
        for i in range(GROUP):
            place = (h * GROUP + i) * owned
            stack[place:place + owned, :] = beside(turned(whole, -i))

    w = combined(dot(solver[...], stack[...]), LANES)
    pair = lane_block(2 * owned)
    q = w[owned:3 * owned]
    for i in range(1, GROUP):
        q = jnp.where(pair == i, turned(w[(i + 1) * owned:(i + 3) * owned], i), q)
    filler = jnp.zeros((width - 2 * owned, LANES), F32)

    def padded(x):
        return jnp.concatenate([x, filler], axis=0)

    faces = now[:2 * width] - combined(dot(cross[...], shared(padded(q), member)), LANES)
    left, right = faces[:width], faces[width:]
    before, after = beside(padded(w[:2 * owned])), beside(padded(w[(GROUP + 1) * owned:]))
    halo_up, halo_down = pays[1][size:, :], pays[groups - 1][size:, :]
    if paired:
        odd = group % 2 == 1
        halo_up, halo_down = jnp.where(odd, halo_up, halo_down), jnp.where(odd, halo_down, halo_up)
    right_before = unpacked(halo_up, GROUP) - combined(dot(edge_up[...], before), LANES)
    left_after = unpacked(halo_down, GROUP) - combined(dot(edge_down[...], after), LANES)
    block = lane_block(width)
    beyond = jnp.where(block == GROUP - 1, turned(left_after, GROUP - 1), turned(left, -1))
    behind = jnp.where(block == 0, right_before, turned(right, 1))
    lam_right = DAMPING * (right - beyond)
    lam_left = DAMPING * (behind - left)
    if kind != "first":
        lam_right = lam_right + right_ref[...]
        lam_left = lam_left + left_ref[...]
    if kind == "last":
        cut(jnp.concatenate([q, lam_right], axis=0), member, outs)
        return
    v_ref, left_out, right_out = outs[:3]
    left_out[...] = lam_left
    right_out[...] = lam_right
    lam = jnp.concatenate([lam_left, -lam_right], axis=0)
    v = v0[...] + combined(dot(own[...], shared(lam, member)), LANES)
    v_ref[...] = v
    payload(v, width, paired, group % 2 == 1, *outs[3:6])
    if kind == "middle":
        cut(jnp.concatenate([lam_left, -lam_right], axis=0), member, outs[6:])


def sweep_kernel(first, pos, right_side, k_ref, u_ref, ks_ref):
    rows, columns = u_ref.shape
    at = right_side.shape[1] - 2 * columns
    high, low = halves(k_ref[first:first + rows])
    both = dot(high, right_side[...])
    part = dot(low, right_side[:, :at + columns])
    u_ref[...] = both[:, at:at + columns] + both[:, at + columns:] + part[:, at:]
    ks_ref[...] = both[:, :at] + part[:, :at]


def changed(u, ks, change):
    high, low = halves(ks)
    part = dot(high, change)
    return u + part[:, :LANES] + part[:, LANES:] + dot(low, change[:, :LANES])


def spread_kernel(parts, pos, p0, p1, p2, p3, *refs):
    lam = joined([p0[...], p1[...], p2[...], p3[...]], pos[0])
    us, kss, out = refs[:parts], refs[parts:2 * parts], refs[2 * parts]
    side, at = lam.shape[0], 0
    lam = beside(lam)
    for u, ks in zip(us, kss):
        out[at:at + u.shape[0]] = changed(u[...], ks[:, :side], lam)
        at += u.shape[0]


def final_kernel(parts, count, pos, p0, p1, p2, p3, u_ref, *refs):
    x = joined([p0[...], p1[...], p2[...], p3[...]], pos[0])
    kss, (out, lam_ref) = refs[:parts], refs[parts:]
    width = lam_ref.shape[0]
    lam_ref[...] = x[count:]
    change = beside(jnp.concatenate([-x[:count], jnp.zeros((width - count, LANES), F32)], axis=0))
    at = 0
    for ks in kss:
        rows = slice(at, at + ks.shape[0])
        out[rows] = changed(u_ref[rows], ks[:, 2 * width:], change)
        at += ks.shape[0]


def local(condensed, eigen_loads, coarse_inverse, face_rows, primal_rows, primal_slot):
    order, columns = eigen_loads.shape
    owned, coarse = coarse_inverse.shape
    width = face_rows.shape[2]
    side, count = 2 * width, 2 * owned
    kept = side + count
    total = lax.axis_size("sub")
    groups = total // GROUP
    me = lax.axis_index("sub")
    pos = jnp.stack([me % GROUP, me // GROUP]).astype(jnp.int32)

    def row(x):
        return jnp.pad(x[None], ((0, 0), (0, width - x.shape[0])))

    table = jnp.concatenate([face_rows[0], row(primal_rows[0]), row(primal_slot[0]), row(pos)], axis=0)

    def mate(x, k):
        return lax.ppermute(x, "sub", [(s, s ^ k) for s in range(total)])

    def crossing(x, pairs):
        pairs = [(g * GROUP + a, (g * GROUP + b) % total) for g in range(groups) for a, b in pairs]
        return lax.ppermute(x, "sub", pairs)

    def traded(pieces):
        return [pieces[0]] + [mate(pieces[k], k) for k in range(1, GROUP)]

    def planes(x, by):
        return lax.ppermute(x, "sub", [(s, (s + by * GROUP) % total) for s in range(total)])

    def along(pay, a, b):
        if groups == PAIRED:
            last = mate(b, 3 * GROUP)
            middle = mate(pay, 2 * GROUP)
            return [pay, mate(a, GROUP), middle, last]
        return [pay, planes(a, 1)] + [planes(pay, k) for k in range(2, groups - 1)] + [planes(b, -1)]

    def after(x, other):
        return lax.optimization_barrier((x, other))[0]

    c_next = mate(coarse_inverse, 2)
    tall = owned * coarse // LANES

    *pieces, ks = call(
        functools.partial(rows_kernel, count),
        [(kept // GROUP, LANES)] * GROUP + [(kept, order)],
        (table, condensed, eigen_loads),
        5.3,
        hbm=(1,),
        scratch=[pltpu.SemaphoreType.DMA((3,))],
        vmem=50,
    )
    spans, edge, right_side = call(
        functools.partial(near_kernel, count),
        [(2 * kept + side, width), (width + tall, width), ((order, side + width + 2 * columns), BF16)],
        (table, ks, eigen_loads, coarse_inverse, table),
        2,
    )
    *pieces, c_next = lax.optimization_barrier((*pieces, c_next))
    pieces = traded(pieces)
    c_other = mate(jnp.concatenate([coarse_inverse, c_next], axis=0), 1)
    tied = after(spans, pieces)
    spans_next = mate(tied, 2)
    spans_other = mate(tied, 1)
    edge = after(edge, pieces)
    came = crossing(edge, [(GROUP - 1, GROUP), (0, -1), (1, -2)])
    came_next = crossing(edge, [(GROUP - 1, GROUP + 2), (0, -3), (1, -4)])
    parts = 4 if order % 64 == 0 else 1
    block = order // parts
    sweeps = []

    def sweep(other):
        if len(sweeps) < parts:
            first = len(sweeps) * block
            shapes = [(block, columns), (block, side + width)]
            kernel = functools.partial(sweep_kernel, first)
            sweeps.append(call(kernel, shapes, (pos, after(right_side, other), condensed), 2.3))
            return sweeps[-1]
        return other

    pieces[0] = after(pieces[0], (c_other, spans_other))
    size = owned + chunk_of(owned)
    pay_shapes = [(size, LANES)] + [(size + width // GROUP, LANES)] * 2
    v0, *pays = call(
        functools.partial(start_kernel, groups == PAIRED),
        [(kept, LANES), *pay_shapes],
        (pos, *pieces),
        0.9,
    )
    swept = sweep(pays)
    pays = along(*pays)
    *pays, spans_next, came, came_next, _ = lax.optimization_barrier((*pays, spans_next, came, came_next, swept))
    theirs = mate(jnp.concatenate([spans_next, came, came_next], axis=0), 1)
    pays[0] = after(pays[0], sweep((spans_next, swept)))
    blocks = call(
        functools.partial(blocks_kernel, width),
        [
            ((2 * (GROUP + 3) * owned, coarse), BF16),
            ((2 * side, GROUP * width), BF16),
            ((2 * kept, GROUP * side), BF16),
            ((side, width), BF16),
            ((side, width), BF16),
        ],
        (pos, coarse_inverse, c_next, c_other, spans, spans_other, spans_next, came, came_next, theirs),
        1.7,
    )

    state = ()
    for step in range(ITERS):
        kind = "first" if step == 0 else "last" if step == ITERS - 1 else "middle"
        shapes = [(kept, LANES), (width, LANES), (width, LANES), *pay_shapes]
        if kind == "middle":
            shapes = shapes + [(side // GROUP, LANES)] * GROUP
        if kind == "last":
            shapes = [((count + width) // GROUP, LANES)] * GROUP
        outs = call(
            functools.partial(turn_kernel, kind, groups),
            shapes,
            (pos, *pays, *blocks, v0, *state),
            2.8,
            scratch=[pltpu.VMEM((groups, size, LANES), F32), pltpu.VMEM((coarse, 2 * LANES), BF16)],
        )
        if kind != "last":
            state = outs[:3]
            swept = sweep(outs)
            pays = along(*outs[3:6])
            pays[0] = after(pays[0], swept)
        if kind == "middle":
            lam_pieces = traded(after(outs[6:], swept))
    us, kss = [x[0] for x in sweeps], [x[1] for x in sweeps]
    traded_back = traded(outs)
    (spread,) = call(
        functools.partial(spread_kernel, parts),
        [(order, columns)],
        (pos, *after(lam_pieces, outs), *us, *kss),
        1.3,
    )
    displaced, multipliers = call(
        functools.partial(final_kernel, parts, count),
        [(order, columns), (width, columns)],
        (pos, *traded_back, spread, *kss),
        2,
    )
    return displaced, multipliers


def solution(mesh):
    placed = (
        P(("rve", "sub"), None),
        P(("rve", "sub"), None),
        P(("rve", "sub"), None),
        P("sub", None, None),
        P("sub", None),
        P("sub", None),
    )
    return jax.shard_map(
        local,
        mesh=mesh,
        in_specs=placed,
        out_specs=(P(("rve", "sub"), None), P(("rve", "sub"), None)),
        check_vma=False,
    )
```

```python
import functools

import jax
import jax.numpy as jnp
from jax import lax
from jax.experimental import pallas as pl
from jax.experimental.pallas import tpu as pltpu
from jax.sharding import PartitionSpec as P

ITERS = 3
DAMPING = 0.5
GROUP = 4
PAIRED = 4
LANES = 128
BF16 = jnp.bfloat16
F32 = jnp.float32


def call(kernel, outs, args, micros, smem=1, hbm=(), scratch=(), vmem=24):
    in_specs = [
        pl.BlockSpec(memory_space=pltpu.SMEM if i < smem else pltpu.HBM if i in hbm else pltpu.VMEM)
        for i in range(len(args))
    ]
    shapes = [o if isinstance(o[0], tuple) else (o, F32) for o in outs]
    return pl.pallas_call(
        kernel,
        out_shape=[jax.ShapeDtypeStruct(s, d) for s, d in shapes],
        in_specs=in_specs,
        out_specs=[pl.BlockSpec(memory_space=pltpu.VMEM)] * len(shapes),
        scratch_shapes=list(scratch),
        compiler_params=pltpu.CompilerParams(vmem_limit_bytes=vmem * 1024 * 1024),
        cost_estimate=pl.CostEstimate(flops=int(micros * 1e9), bytes_accessed=0, transcendentals=0),
    )(*args)


def halves(x):
    high = x.astype(BF16)
    return high, (x - high.astype(F32)).astype(BF16)


def dot(a, b):
    return jnp.dot(a, b, preferred_element_type=F32)


def product(a, b):
    ah, al = halves(a)
    bh, bl = halves(b)
    n = b.shape[1]
    both = dot(ah, jnp.concatenate([bh, bl], axis=1))
    return both[:, :n] + both[:, n:] + dot(al, bh)


def lane_block(rows):
    return lax.broadcasted_iota(jnp.int32, (rows, LANES), 1) // (LANES // GROUP)


def turned(x, blocks):
    width = LANES // GROUP
    if isinstance(blocks, int):
        shift = (blocks % GROUP) * width
        return x if shift == 0 else pltpu.roll(x, shift, 1)
    return pltpu.roll(x, lax.rem(blocks + 2 * GROUP, GROUP) * width, 1)


def cut(x, member, out_refs):
    rows = x.shape[0] // GROUP
    block = lane_block(rows)
    parts = [x[q * rows:(q + 1) * rows] for q in range(GROUP)]
    for k, out in enumerate(out_refs):
        to = member ^ k
        packed = jnp.zeros((rows, LANES), F32)
        for q in range(GROUP):
            packed = jnp.where(block == q, turned(parts[q], q - to), packed)
        out[...] = packed


def joined(pieces, member):
    rows = pieces[0].shape[0]
    block = lane_block(rows)
    out = []
    for q in range(GROUP):
        part = jnp.zeros((rows, LANES), F32)
        for k, piece in enumerate(pieces):
            came = member ^ k
            part = jnp.where(block == came, turned(piece, came - q), part)
        out.append(part)
    return jnp.concatenate(out, axis=0)


def packed(x, chunk):
    first = lane_block(chunk) == 0
    out = None
    for q in range(x.shape[0] // chunk):
        part = turned(jnp.where(first, x[q * chunk:(q + 1) * chunk], 0.0), q)
        out = part if out is None else out + part
    return out


def unpacked(x, count):
    return jnp.concatenate([turned(x, -q) for q in range(count)], axis=0)


def chunk_of(owned):
    return -(-owned // (GROUP * 8)) * 8


def stacked(x):
    return jnp.concatenate(halves(x), axis=0)


def beside(x):
    return jnp.concatenate(halves(x), axis=1)


def combined(p, n):
    m = p.shape[0] // 2
    return p[:m, :n] + p[:m, n:] + p[m:, :n]


def payload(v, width, paired, odd, out, out_a, out_b):
    coarse = v[2 * width:]
    owned = coarse.shape[0] // 2
    below = turned(coarse[owned:], 1)
    own = coarse[:owned] + jnp.where(lane_block(owned) == 0, 0.0, below)
    rows = jnp.concatenate([own, packed(below, chunk_of(owned))], axis=0)
    size = rows.shape[0]
    for ref in (out, out_a, out_b):
        ref[:size] = rows
    up = packed(turned(v[width:2 * width], 1), width // GROUP)
    down = packed(v[:width], width // GROUP)
    if paired:
        up, down = jnp.where(odd, down, up), jnp.where(odd, up, down)
    out_a[size:] = up
    out_b[size:] = down


def fetch(source, count, rows, target, places, sem):
    def one(j, carry):
        pltpu.make_async_copy(source.at[pl.ds(rows(j), 1)], target.at[pl.ds(places(j), 1)], sem).start()
        return carry

    lax.fori_loop(0, count, one, 0, unroll=8)


def rows_kernel(count, table, k_ref, f_ref, *rest):
    pieces, (ks, sems) = rest[:GROUP], rest[GROUP:]
    width, columns = table.shape[1], f_ref.shape[1]
    side = 2 * width
    fetch(k_ref, width, lambda j: table[0, j], ks, lambda j: j, sems.at[0])
    fetch(k_ref, width, lambda j: table[1, j], ks, lambda j: width + j, sems.at[1])
    fetch(k_ref, count, lambda j: table[2, j], ks, lambda j: side + table[3, j], sems.at[2])
    loads = beside(f_ref[...])
    v = []
    for i, (first, size) in enumerate(((0, width), (width, width), (side, count))):
        part = ks.at[first:first + size]
        pltpu.make_async_copy(k_ref.at[pl.ds(0, size)], part, sems.at[i]).wait()
        high, low = halves(part[...])
        both = dot(high, loads)
        v.append(both[:, :columns] + both[:, columns:] + dot(low, loads[:, :columns]))
    cut(jnp.concatenate(v, axis=0), table[4, 0], pieces)


def near_kernel(count, table, ks, f_ref, c_ref, tablev, spans, edge, right_side):
    width, order, owned = table.shape[1], ks.shape[1], c_ref.shape[0]
    side = 2 * width

    def indicator(row):
        place = lax.broadcasted_iota(jnp.int32, (order, row.shape[1]), 0).astype(F32)
        return jnp.where(place == row, 1.0, 0.0).astype(BF16)

    slots = jnp.broadcast_to(tablev[3:4, :count].astype(F32), (count, count)).T
    prims = jnp.broadcast_to(tablev[2:3, :count].astype(F32), (count, count)).T
    wanted = lax.broadcasted_iota(jnp.int32, (count, count), 1).astype(F32)
    by_slot = jnp.sum(jnp.where(slots == wanted, prims, 0.0), axis=0, keepdims=True)
    right_side[:, :width] = indicator(tablev[0:1].astype(F32))
    right_side[:, width:side] = indicator(tablev[1:2].astype(F32))
    right_side[:, side:side + count] = indicator(by_slot)
    right_side[:, side + count:side + width] = jnp.zeros((order, width - count), BF16)
    right_side[:, side + width:] = beside(f_ref[...])
    for i in range(c_ref.shape[1] // LANES):
        at = width + i * owned
        edge[at:at + owned] = c_ref[:, i * LANES:(i + 1) * LANES]
    high, low = halves(ks[...])
    at, rows = side + width, side + count
    block = dot(high, right_side[:, :at]) + dot(low, right_side[:, :at])
    spans[:rows] = block[:, :width]
    spans[rows:2 * rows] = block[:, width:side]
    spans[2 * rows:] = block[:side, side:]
    edge[:width] = jnp.where(table[4, 0] == GROUP - 1, block[width:side, side:], block[:width, side:])


GOT = (-1, None, 5, 4)
GOT_NEXT = (5, 4, -1, None)


GOT = (-1, None, 5, 4)
GOT_NEXT = (5, 4, -1, None)


def blocks_kernel(width, pos, c0, c2, c_other, s0, s1, s2, came, came_next, theirs, solver, cross, own, edge_up, edge_down):
    side, size, edge_size = 2 * width, s0.shape[0], came.shape[0]
    kept = (size - side) // 2
    owned, tall = c0.shape[0], c0.shape[1] // LANES
    half = solver.shape[0] // 2
    other, at = [], 0
    for rows in (size, edge_size, edge_size):
        other.append(theirs.at[at:at + rows])
        at += rows
    for k, ref in enumerate((s0, s1, s2, other[0])):
        own[:, k * side:k * side + width] = stacked(ref[:kept])
        own[:, k * side + width:(k + 1) * side] = stacked(ref[kept:2 * kept])
        cross[:, k * width:(k + 1) * width] = stacked(ref[2 * kept:])

    def placed(block, values, columns):
        at = (block + 1) * owned
        high, low = halves(values)
        solver[at:at + owned, columns] = high
        solver[half + at:half + at + owned, columns] = low

    for m in range(GROUP):

        @pl.when(pos[0] == m)
        def _():
            p = m ^ 1
            everything = slice(None)
            placed(m, c0[...], everything)
            placed(m ^ 2, c2[...], everything)
            placed(p, c_other[:owned], everything)
            placed(p ^ 2, c_other[owned:], everything)
            held = {GOT[m]: came, GOT_NEXT[m]: came_next}
            for block, ref in zip((GOT[p], GOT_NEXT[p]), other[1:]):
                held.setdefault(block, ref)
            for block in (-1, 4, 5):
                for i in range(tall):
                    at = width + i * owned
                    placed(block, held[block][at:at + owned], slice(i * LANES, (i + 1) * LANES))
            edge_up[...] = stacked(held[-1][:width])
            edge_down[...] = stacked(held[4][:width])


def start_kernel(paired, pos, p0, p1, p2, p3, v_ref, *pays):
    v = joined([p0[...], p1[...], p2[...], p3[...]], pos[0])
    v_ref[...] = v
    payload(v, v.shape[1], paired, pos[1] % 2 == 1, *pays)


def shared(x, member):
    block = lane_block(x.shape[0])
    high, low = halves(x)
    high, low = high.astype(F32), low.astype(F32)
    out = []
    for k in range(GROUP):
        mine = block == (member ^ k)
        pair = [jnp.where(mine, half, 0.0).astype(BF16) for half in (high, low)]
        out.append(jnp.concatenate(pair, axis=1))
    return jnp.concatenate(out, axis=0)


def turn_kernel(kind, groups, pos, *refs):
    pays, (solver, cross, own, edge_up, edge_down, v0), refs = refs[:groups], refs[groups:groups + 6], refs[groups + 6:]
    if kind == "first":
        now = v0
    else:
        (now, left_ref, right_ref), refs = refs[:3], refs[3:]
    outs, (held, stack) = refs[:-2], refs[-2:]
    paired = groups == PAIRED
    if paired:
        pays = pays[:1] + pays[:0:-1]
    member, group = pos[0], pos[1]
    width = edge_down.shape[1]
    owned = (v0.shape[0] - 2 * width) // 2
    size = owned + chunk_of(owned)
    first = lane_block(owned) == 0

    for k in range(groups):
        held[group ^ k if paired else lax.rem(group - k + groups, groups)] = pays[k][:size, :]
    for h in range(groups):
        extra = unpacked(held[(h - 1) % groups, owned:], -(-owned // chunk_of(owned)))[:owned]
        whole = held[h, :owned] + jnp.where(first, extra, 0.0)
        for i in range(GROUP):
            place = (h * GROUP + i) * owned
            stack[place:place + owned, :] = beside(turned(whole, -i))

    w = combined(dot(solver[...], stack[...]), LANES)
    pair = lane_block(2 * owned)
    q = w[owned:3 * owned]
    for i in range(1, GROUP):
        q = jnp.where(pair == i, turned(w[(i + 1) * owned:(i + 3) * owned], i), q)
    filler = jnp.zeros((width - 2 * owned, LANES), F32)

    def padded(x):
        return jnp.concatenate([x, filler], axis=0)

    faces = now[:2 * width] - combined(dot(cross[...], shared(padded(q), member)), LANES)
    left, right = faces[:width], faces[width:]
    before, after = beside(padded(w[:2 * owned])), beside(padded(w[(GROUP + 1) * owned:]))
    halo_up, halo_down = pays[1][size:, :], pays[groups - 1][size:, :]
    if paired:
        odd = group % 2 == 1
        halo_up, halo_down = jnp.where(odd, halo_up, halo_down), jnp.where(odd, halo_down, halo_up)
    right_before = unpacked(halo_up, GROUP) - combined(dot(edge_up[...], before), LANES)
    left_after = unpacked(halo_down, GROUP) - combined(dot(edge_down[...], after), LANES)
    block = lane_block(width)
    beyond = jnp.where(block == GROUP - 1, turned(left_after, GROUP - 1), turned(left, -1))
    behind = jnp.where(block == 0, right_before, turned(right, 1))
    lam_right = DAMPING * (right - beyond)
    lam_left = DAMPING * (behind - left)
    if kind != "first":
        lam_right = lam_right + right_ref[...]
        lam_left = lam_left + left_ref[...]
    if kind == "last":
        cut(jnp.concatenate([q, lam_right], axis=0), member, outs)
        return
    v_ref, left_out, right_out = outs[:3]
    left_out[...] = lam_left
    right_out[...] = lam_right
    lam = jnp.concatenate([lam_left, -lam_right], axis=0)
    v = v0[...] + combined(dot(own[...], shared(lam, member)), LANES)
    v_ref[...] = v
    payload(v, width, paired, group % 2 == 1, *outs[3:6])
    if kind == "middle":
        cut(jnp.concatenate([lam_left, -lam_right], axis=0), member, outs[6:])


def sweep_kernel(first, pos, right_side, k_ref, u_ref, ks_ref):
    rows, columns = u_ref.shape
    at = right_side.shape[1] - 2 * columns
    high, low = halves(k_ref[first:first + rows])
    both = dot(high, right_side[...])
    part = dot(low, right_side[:, :at + columns])
    u_ref[...] = both[:, at:at + columns] + both[:, at + columns:] + part[:, at:]
    ks_ref[...] = both[:, :at] + part[:, :at]


def changed(u, ks, change):
    high, low = halves(ks)
    part = dot(high, change)
    return u + part[:, :LANES] + part[:, LANES:] + dot(low, change[:, :LANES])


def spread_kernel(parts, pos, p0, p1, p2, p3, *refs):
    lam = joined([p0[...], p1[...], p2[...], p3[...]], pos[0])
    us, kss, out = refs[:parts], refs[parts:2 * parts], refs[2 * parts]
    side, at = lam.shape[0], 0
    lam = beside(lam)
    for u, ks in zip(us, kss):
        out[at:at + u.shape[0]] = changed(u[...], ks[:, :side], lam)
        at += u.shape[0]


def final_kernel(parts, count, pos, p0, p1, p2, p3, u_ref, *refs):
    x = joined([p0[...], p1[...], p2[...], p3[...]], pos[0])
    kss, (out, lam_ref) = refs[:parts], refs[parts:]
    width = lam_ref.shape[0]
    lam_ref[...] = x[count:]
    change = beside(jnp.concatenate([-x[:count], jnp.zeros((width - count, LANES), F32)], axis=0))
    at = 0
    for ks in kss:
        rows = slice(at, at + ks.shape[0])
        out[rows] = changed(u_ref[rows], ks[:, 2 * width:], change)
        at += ks.shape[0]


def local(condensed, eigen_loads, coarse_inverse, face_rows, primal_rows, primal_slot):
    order, columns = eigen_loads.shape
    owned, coarse = coarse_inverse.shape
    width = face_rows.shape[2]
    side, count = 2 * width, 2 * owned
    kept = side + count
    total = lax.axis_size("sub")
    groups = total // GROUP
    me = lax.axis_index("sub")
    pos = jnp.stack([me % GROUP, me // GROUP]).astype(jnp.int32)

    def row(x):
        return jnp.pad(x[None], ((0, 0), (0, width - x.shape[0])))

    table = jnp.concatenate([face_rows[0], row(primal_rows[0]), row(primal_slot[0]), row(pos)], axis=0)

    def mate(x, k):
        return lax.ppermute(x, "sub", [(s, s ^ k) for s in range(total)])

    def crossing(x, pairs):
        pairs = [(g * GROUP + a, (g * GROUP + b) % total) for g in range(groups) for a, b in pairs]
        return lax.ppermute(x, "sub", pairs)

    def traded(pieces):
        return [pieces[0]] + [mate(pieces[k], k) for k in range(1, GROUP)]

    def planes(x, by):
        return lax.ppermute(x, "sub", [(s, (s + by * GROUP) % total) for s in range(total)])

    def along(pay, a, b):
        if groups == PAIRED:
            last = mate(b, 3 * GROUP)
            middle = mate(pay, 2 * GROUP)
            return [pay, last, middle, mate(a, GROUP)]
        return [pay, planes(a, 1)] + [planes(pay, k) for k in range(2, groups - 1)] + [planes(b, -1)]

    def after(x, other):
        return lax.optimization_barrier((x, other))[0]

    c_next = mate(coarse_inverse, 2)
    tall = owned * coarse // LANES

    *pieces, ks = call(
        functools.partial(rows_kernel, count),
        [(kept // GROUP, LANES)] * GROUP + [(kept, order)],
        (table, condensed, eigen_loads),
        5.3,
        hbm=(1,),
        scratch=[pltpu.SemaphoreType.DMA((3,))],
        vmem=50,
    )
    spans, edge, right_side = call(
        functools.partial(near_kernel, count),
        [(2 * kept + side, width), (width + tall, width), ((order, side + width + 2 * columns), BF16)],
        (table, ks, eigen_loads, coarse_inverse, table),
        2,
    )
    *pieces, c_next = lax.optimization_barrier((*pieces, c_next))
    pieces = traded(pieces)
    c_other = mate(jnp.concatenate([coarse_inverse, c_next], axis=0), 1)
    tied = after(spans, pieces)
    spans_next = mate(tied, 2)
    spans_other = mate(tied, 1)
    edge = after(edge, pieces)
    came = crossing(edge, [(GROUP - 1, GROUP), (0, -1), (1, -2)])
    came_next = crossing(edge, [(GROUP - 1, GROUP + 2), (0, -3), (1, -4)])
    parts = 4 if order % 64 == 0 else 1
    block = order // parts
    sweeps = []

    def sweep(other):
        if len(sweeps) < parts:
            first = len(sweeps) * block
            shapes = [(block, columns), (block, side + width)]
            kernel = functools.partial(sweep_kernel, first)
            sweeps.append(call(kernel, shapes, (pos, after(right_side, other), condensed), 2.3))
            return sweeps[-1]
        return other

    pieces[0] = after(pieces[0], (c_other, spans_other))
    size = owned + chunk_of(owned)
    pay_shapes = [(size, LANES)] + [(size + width // GROUP, LANES)] * 2
    v0, *pays = call(
        functools.partial(start_kernel, groups == PAIRED),
        [(kept, LANES), *pay_shapes],
        (pos, *pieces),
        0.9,
    )
    swept = sweep(pays)
    pays = along(*pays)
    *pays, spans_next, came, came_next, _ = lax.optimization_barrier((*pays, spans_next, came, came_next, swept))
    theirs = mate(jnp.concatenate([spans_next, came, came_next], axis=0), 1)
    pays[0] = after(pays[0], sweep((spans_next, swept)))
    blocks = call(
        functools.partial(blocks_kernel, width),
        [
            ((2 * (GROUP + 3) * owned, coarse), BF16),
            ((2 * side, GROUP * width), BF16),
            ((2 * kept, GROUP * side), BF16),
            ((side, width), BF16),
            ((side, width), BF16),
        ],
        (pos, coarse_inverse, c_next, c_other, spans, spans_other, spans_next, came, came_next, theirs),
        1.7,
    )

    state = ()
    for step in range(ITERS):
        kind = "first" if step == 0 else "last" if step == ITERS - 1 else "middle"
        shapes = [(kept, LANES), (width, LANES), (width, LANES), *pay_shapes]
        if kind == "middle":
            shapes = shapes + [(side // GROUP, LANES)] * GROUP
        if kind == "last":
            shapes = [((count + width) // GROUP, LANES)] * GROUP
        outs = call(
            functools.partial(turn_kernel, kind, groups),
            shapes,
            (pos, *pays, *blocks, v0, *state),
            2.8,
            scratch=[pltpu.VMEM((groups, size, LANES), F32), pltpu.VMEM((coarse, 2 * LANES), BF16)],
        )
        if kind != "last":
            state = outs[:3]
            swept = sweep(outs)
            pays = along(*outs[3:6])
            pays[0] = after(pays[0], swept)
        if kind == "middle":
            lam_pieces = traded(after(outs[6:], swept))
    us, kss = [x[0] for x in sweeps], [x[1] for x in sweeps]
    traded_back = traded(outs)
    (spread,) = call(
        functools.partial(spread_kernel, parts),
        [(order, columns)],
        (pos, *after(lam_pieces, outs), *us, *kss),
        1.3,
    )
    displaced, multipliers = call(
        functools.partial(final_kernel, parts, count),
        [(order, columns), (width, columns)],
        (pos, *traded_back, spread, *kss),
        2,
    )
    return displaced, multipliers


def solution(mesh):
    placed = (
        P(("rve", "sub"), None),
        P(("rve", "sub"), None),
        P(("rve", "sub"), None),
        P("sub", None, None),
        P("sub", None),
        P("sub", None),
    )
    return jax.shard_map(
        local,
        mesh=mesh,
        in_specs=placed,
        out_specs=(P(("rve", "sub"), None), P(("rve", "sub"), None)),
        check_vma=False,
    )
```
